128 devices in a mesh: section: 2 (over y_hi), dp: 8 (over y_lo, x), tensor: 8 (over z, core).
Axes of the slice: x: 4, y: 4 (y_hi: 2, y_lo: 2; y = y_hi * 2 + y_lo), z: 4, core: 2. Of those that a mesh axis runs over, the one named last changes fastest.
Arguments:
- inputs: bfloat16 [256, 9216], P('tensor', 'dp'), may hold values from -11 to 11
- cotangent: bfloat16 [256, 9216], P('tensor', 'dp'), may hold values from -6 to 6
- w_first: bfloat16 [2, 9216, 18432], P('section', 'dp', 'tensor'), may hold values from -1 to 1
- w_second: bfloat16 [2, 18432, 9216], P('section', 'tensor', 'dp'), may hold values from -0.046875 to 0.046875
Outputs:
- input_grads: bfloat16 [2, 256, 9216], P('section', 'tensor', 'dp')
- first_grads: bfloat16 [2, 9216, 18432], P('section', 'dp', 'tensor')
- second_grads: bfloat16 [2, 18432, 9216], P('section', 'tensor', 'dp')
The draws below stay inside these ranges and needn't reach their ends.
All inputs are finite; a program needn't handle non-finite values.
Results may differ from the reference program's by a relative error of at most 0.011.
Values may be sent and summed in bfloat16 or wider, within the bound.
No kernel may reach another device: no remote copies, remote signals or barrier semaphores. Data moves between devices by JAX's collectives and lax.ppermute only.
A program may use at most 128 MiB of HBM per device.

```python
import math
import jax
import jax.numpy as jnp
from jax import lax

D = 9216
FF = 18432
TOKENS = 256
N_DP = 8
N_TENSOR = 8


def draw_inputs(key, part):
    key = jax.random.fold_in(key, 11)
    key_base = jax.random.fold_in(key, 0)
    ramp = 0.5 + jnp.arange(D, dtype=jnp.float32) / D
    base = jnp.clip(jax.random.normal(key_base, (TOKENS, D), jnp.float32), -4.0, 4.0)
    return (base * ramp + 0.3 * ramp).astype(jnp.bfloat16)


def rising_rows(low_end, high_end):
    ratio = math.log(high_end / low_end)
    spread = math.sqrt((high_end * high_end - low_end * low_end) / (2.0 * ratio))
    steps = jnp.arange(D, dtype=jnp.float32) / (D - 1)
    return jnp.exp(math.log(low_end) + ratio * steps) / spread


def draw_w_first(key, part):
    key = jax.random.fold_in(key, 23)
    noise = jnp.clip(jax.random.normal(key, (2, D, FF), jnp.float32), -4.0, 4.0)
    scales = rising_rows(0.3, 3.0)
    common = 0.1
    values = (noise + common) * scales[None, :, None] / math.sqrt(D)
    return values.astype(jnp.bfloat16)


def block_scale(rng, extent, pieces, least, top_value):
    def one(axis_at, shards_of):
        heights = jax.random.uniform(jax.random.fold_in(jax.random.fold_in(rng, 6), axis_at), (shards_of,), jnp.float32, least / len(pieces), top_value / len(pieces))
        return jnp.repeat(jnp.exp(heights), extent[axis_at] // shards_of).reshape((-1,) + (1,) * (len(extent) - axis_at - 1))

    loudness = one(*pieces[0])
    for cut in pieces[1:]:
        loudness = loudness * one(*cut)
    return loudness


def gaussian(own_key, extent, scale, most, cuts=(), held_as=jnp.bfloat16):
    drawn = scale * jax.random.normal(own_key, extent, jnp.float32)
    if cuts:
        drawn = drawn * block_scale(own_key, extent, cuts, -0.22, 0.18)
    return jnp.clip(drawn, -most, most).astype(held_as)


def setup_inputs(seed: int = 0) -> dict:
    splits = jax.random.split(jax.random.key(seed), 5)
    return {
        "inputs": draw_inputs(jax.random.fold_in(splits[4], 71), 0),
        "cotangent": gaussian(splits[1], (TOKENS, D), 1.0, 6.0, ((0, 8), (1, 8))),
        "w_first": draw_w_first(jax.random.fold_in(splits[4], 71), 0),
        "w_second": gaussian(splits[3], (2, FF, D), FF ** -0.5, 0.046875, ((0, 2), (1, 8), (2, 8))),
    }


EPSILON = 1e-05

def later_rows_view(stored):
    rows, cols = stored.shape
    blocks = stored.reshape(2, N_TENSOR // 2, rows // N_TENSOR, N_DP, 2, cols // (2 * N_DP))
    return blocks.transpose(1, 2, 4, 3, 0, 5).reshape(rows, cols)

def later_rows_store(logical):
    rows, cols = logical.shape
    blocks = logical.reshape(N_TENSOR // 2, rows // N_TENSOR, 2, N_DP, 2, cols // (2 * N_DP))
    return blocks.transpose(4, 0, 1, 3, 2, 5).reshape(rows, cols)

def later_cols_view(stored):
    rows, cols = stored.shape
    blocks = stored.reshape(N_DP, rows // (2 * N_DP), 2, 2, N_TENSOR // 2, cols // N_TENSOR)
    return blocks.transpose(0, 3, 1, 4, 2, 5).reshape(rows, cols)

def later_cols_store(logical):
    rows, cols = logical.shape
    blocks = logical.reshape(N_DP, 2, rows // (2 * N_DP), N_TENSOR // 2, 2, cols // N_TENSOR)
    return blocks.transpose(0, 2, 4, 1, 3, 5).reshape(rows, cols)

def layer_forward(stream, w_in, w_out):
    values = stream.astype(jnp.float32)
    mean_row = lax.optimization_barrier(jnp.sum(values, axis=1)) / D
    inv_std = lax.rsqrt(lax.optimization_barrier(jnp.sum(values * values, axis=1)) / D - mean_row * mean_row + EPSILON)
    centred = (values - mean_row[:, None]) * inv_std[:, None]
    normed = centred.astype(jnp.bfloat16)
    pre_act = jnp.dot(normed, w_in, preferred_element_type=jnp.float32)
    acted = jax.nn.gelu(pre_act).astype(jnp.bfloat16)
    result = (values + jnp.dot(acted, w_out, preferred_element_type=jnp.float32)).astype(jnp.bfloat16)
    return (result, (centred, inv_std, normed, pre_act, acted))

def layer_backward(grad_out, saved, w_in, w_out):
    centred, inv_std, normed, pre_act, acted = saved
    out_grad = jnp.dot(acted.T, grad_out, preferred_element_type=jnp.float32).astype(jnp.bfloat16)
    grad_acted = jnp.dot(grad_out, w_out.T, preferred_element_type=jnp.float32)
    _, gelu_back = jax.vjp(jax.nn.gelu, pre_act)
    grad_pre = gelu_back(grad_acted)[0].astype(jnp.bfloat16)
    in_grad = jnp.dot(normed.T, grad_pre, preferred_element_type=jnp.float32).astype(jnp.bfloat16)
    grad_normed = jnp.dot(grad_pre, w_in.T, preferred_element_type=jnp.float32)
    mean_grad = lax.optimization_barrier(jnp.sum(grad_normed, axis=1))
    mean_mixed = lax.optimization_barrier(jnp.sum(grad_normed * centred, axis=1))
    stream_grad = grad_out.astype(jnp.float32) + inv_std[:, None] * (grad_normed - mean_grad[:, None] / D - centred * (mean_mixed[:, None] / D))
    return (stream_grad.astype(jnp.bfloat16), in_grad, out_grad)

def reference(inputs, cotangent, w_first, w_second):
    later_in_w = later_cols_view(w_first[1])
    later_out_w = later_rows_view(w_second[1])
    first_out, saved_first = layer_forward(inputs, w_first[0], w_second[0])
    _, saved_later = layer_forward(first_out, later_in_w, later_out_w)
    later_grad, later_in, later_out = layer_backward(later_rows_view(cotangent), saved_later, later_in_w, later_out_w)
    first_grad, first_in, first_outw = layer_backward(later_grad, saved_first, w_first[0], w_second[0])
    return (jnp.stack([first_grad, later_rows_store(later_grad)]), jnp.stack([first_in, later_cols_store(later_in)]), jnp.stack([first_outw, later_rows_store(later_out)]))
```

```python
import jax
import jax.numpy as jnp
from jax import lax
from jax.sharding import PartitionSpec as P

D = 9216
EPSILON = 1e-05
AXES = ("section", "dp", "tensor")
BF = jnp.bfloat16
F32 = jnp.float32
BOTH, FIRST, LATER = (0, 1), (0,), (1,)


def send(value, move, sections=BOTH):
    pairs = []
    for s in sections:
        for d in range(8):
            for t in range(8):
                s2, d2, t2 = move(s, d, t)
                pairs.append(((s * 8 + d) * 8 + t, (s2 * 8 + d2) * 8 + t2))
    return lax.ppermute(value, AXES, pairs)


def along_x(k):
    return lambda s, d, t: (s, d // 4 * 4 + (d + k) % 4, t)


def along_z(k):
    return lambda s, d, t: (s, d, (t + 2 * k) % 8)


def other_y(s, d, t):
    return (s, d ^ 4, t)


def other_core(s, d, t):
    return (s, d, t ^ 1)


def other_half(s, d, t):
    return (s, d, t ^ 4)


def other_half_row(s, d, t):
    return (s, d // 4 * 4 + (d + 2) % 4, t ^ 4)


def other_section(s, d, t):
    return (1 - s, d, t)


def dot(left, right, dims=((1,), (0,))):
    return lax.dot_general(left, right, (dims, ((), ())), preferred_element_type=F32)


def gather_tensor(x, sections=BOTH):
    pair = jnp.concatenate([x] + [send(x, along_z(k), sections) for k in (1, 2, 3)], axis=0)
    return jnp.concatenate([pair, send(pair, other_core, sections)], axis=0)


def scatter_tensor(partial, sections=BOTH):
    rows = partial.shape[0] // 8
    half = partial.shape[0] // 2
    arrived = send(partial[half:].astype(BF), other_core, sections)
    total = partial[:half].astype(F32) + arrived.astype(F32)
    mine = total[:rows]
    for k in (1, 2, 3):
        block = total[k * rows : (k + 1) * rows].astype(BF)
        mine = mine + send(block, along_z(-k), sections).astype(F32)
    return mine


def swap_dp(blocks):
    return lax.all_to_all(blocks, "dp", 0, 0, tiled=True)


def sum_dp(value, sections):
    total = value
    for k in (1, 2, 3):
        total = total + send(value, along_x(k), sections)
    return total + send(total, other_y, sections)


def two_sums(one, two, sections):
    both = sum_dp(jnp.stack([jnp.sum(one, axis=1), jnp.sum(two, axis=1)]), sections)
    return both[0], both[1]


def norm_from(values, sections):
    row_sums, square_sums = two_sums(values, values * values, sections)
    mean_row = row_sums / D
    inv_std = lax.rsqrt(square_sums / D - mean_row * mean_row + EPSILON)
    return ((values - mean_row[:, None]) * inv_std[:, None], inv_std)


def norm_back(grad_out, grad_normed, centred, inv_std, sections):
    mean_grad, mean_mixed = two_sums(grad_normed, grad_normed * centred, sections)
    stream_grad = grad_out.astype(F32) + inv_std[:, None] * (
        grad_normed - mean_grad[:, None] / D - centred * (mean_mixed[:, None] / D)
    )
    return stream_grad.astype(BF)


def one_hot(condition):
    return condition.astype(BF)


def body(inputs, cotangent, w_first, w_second):
    w_in, w_out = w_first[0], w_second[0]
    rows, width = inputs.shape
    hidden = w_in.shape[1]
    part = width // 2
    tokens = 8 * rows
    first = lax.axis_index("section") == 0
    at = lax.axis_index("tensor")
    z_at, core_at = at // 2, at % 2
    half = at // 4

    slot_row = jnp.arange(tokens)
    slot_owner = ((z_at - slot_row // rows % 4) % 4) * 2 + (core_at ^ (slot_row // (4 * rows)))
    slot_token = slot_owner * rows + slot_row % rows

    def planes(own_plane):
        pick = one_hot(
            jnp.arange(width)[None, :]
            == 2 * jnp.arange(part)[:, None] + jnp.where(own_plane, half, 1 - half)
        )
        return dot(pick, w_in).astype(BF)

    empty_plane = jnp.zeros((part, hidden), BF)
    away = lax.cond(first, lambda: empty_plane, lambda: planes(False))
    came = send(away, other_half, LATER)

    values = inputs.astype(F32)
    centred_first, inv_first = norm_from(values, FIRST)
    normed_own = centred_first.astype(BF)
    lead = gather_tensor(jnp.where(first, normed_own, cotangent))

    def cot_rows():
        blocks = lead.reshape(2, 4, rows, 2, part)
        k_near = jnp.where(z_at % 2 == 0, 3, 1)
        near = lax.dynamic_index_in_dim(blocks, k_near, 1, keepdims=True)
        far = lax.dynamic_index_in_dim(blocks, 4 - k_near, 1, keepdims=True)
        mine = jnp.concatenate([blocks[:, :1], near], axis=1)
        rest = jnp.concatenate([blocks[:, 2:3], far], axis=1)
        def flat(group):
            return group.transpose(0, 1, 3, 2, 4).reshape(tokens, part)

        index = jnp.arange(tokens)
        e, j = index // (4 * rows), index // (2 * rows) % 2
        q, r = index // rows % 2, index % rows
        c_block = (z_at % 2 ^ j) * 2 + (core_at ^ e)
        token = c_block * 2 * rows + 2 * r + q
        order = one_hot(slot_token[:, None] == token[None, :])
        own = dot(order, flat(mine)).astype(BF)
        other = dot(order, flat(rest)).astype(BF)
        return own, other

    def lead_second():
        own, other = cot_rows()
        blank = jnp.zeros_like(own)
        padded = jnp.concatenate(
            [jnp.concatenate([own, blank], axis=1), jnp.concatenate([blank, own], axis=1)], axis=0
        )
        spread = dot(padded, w_out, ((1,), (1,))).astype(BF)
        spread = spread.reshape(2, tokens, 2, hidden // 2)
        low = jnp.concatenate([spread[0, :, 0], spread[1, :, 0]], axis=1)
        high = jnp.concatenate([spread[0, :, 1], spread[1, :, 1]], axis=1)
        cot_own = jnp.where(
            half == 0,
            jnp.concatenate([own[:rows], other[:rows]], axis=1),
            jnp.concatenate([other[:rows], own[:rows]], axis=1),
        )
        return jnp.where(half == 0, low, high), jnp.where(half == 0, high, low), padded, cot_own

    def lead_first():
        made = dot(lead, w_in).astype(BF)
        return made, made, jnp.zeros((2 * tokens, width), BF), normed_own

    part_a, part_b, cot_padded, cot_own = lax.cond(first, lead_first, lead_second)
    sum_a = jnp.sum(swap_dp(part_a.reshape(8, rows, hidden)).astype(F32), axis=0)
    acted_own_first = jax.nn.gelu(sum_a).astype(BF)
    blocks_b = swap_dp(jnp.where(first, acted_own_first[None], part_b.reshape(8, rows, hidden)))
    acted_first = blocks_b.reshape(tokens, hidden)
    sum_b = jnp.sum(blocks_b.astype(F32), axis=0)
    branch_part = lax.cond(
        first,
        lambda: dot(acted_first, w_out).astype(BF),
        lambda: jnp.zeros((tokens, width), BF),
    )
    branch = scatter_tensor(branch_part, FIRST)
    stream_own = send((values + branch).astype(BF), other_section, FIRST)

    grad_acted = sum_a + send(sum_b.astype(BF), other_half_row, LATER).astype(F32)
    groups = hidden // 256
    lane = jnp.arange(256)
    weave = one_hot(lane[None, :] == 2 * (lane[:, None] % 128) + lane[:, None] // 128)

    def weave_lanes(value):
        stacked = value.reshape(rows, 2, groups, 128).transpose(2, 0, 1, 3)
        stacked = stacked.reshape(groups * rows, 256)
        top = stacked.astype(BF)
        rest = (stacked - top.astype(F32)).astype(BF)
        done = dot(top, weave) + dot(rest, weave)
        return done.reshape(groups, rows, 256).transpose(1, 0, 2).reshape(rows, hidden)

    def unweave_lanes(value):
        stacked = value.reshape(rows, groups, 256).transpose(1, 0, 2).reshape(groups * rows, 256)
        done = dot(stacked, weave, ((1,), (1,))).astype(BF)
        done = done.reshape(groups, rows, 2, 128).transpose(1, 2, 0, 3)
        return done.reshape(rows, hidden)

    grad_acted = weave_lanes(grad_acted)

    def joined():
        kept = planes(True)
        return jnp.where(
            half == 0,
            jnp.concatenate([kept, came], axis=0),
            jnp.concatenate([came, kept], axis=0),
        )

    w_full = lax.cond(first, lambda: w_in, joined)

    stream = stream_own.astype(F32)
    centred_later, inv_later = norm_from(stream, LATER)
    normed_later = gather_tensor(centred_later.astype(BF), LATER)
    pre_part = dot(normed_later, w_full).astype(BF)
    pre_later = jnp.sum(swap_dp(pre_part.reshape(8, rows, hidden)).astype(F32), axis=0)
    acted_later, gelu_back = jax.vjp(jax.nn.gelu, pre_later)
    grad_pre_own = gelu_back(grad_acted)[0].astype(BF)
    grad_pre_later = swap_dp(
        jnp.broadcast_to(grad_pre_own[None], (8, rows, hidden))
    ).reshape(tokens, hidden)
    back_part = dot(grad_pre_later, w_full, ((1,), (1,))).astype(BF)
    grad_normed = scatter_tensor(back_part, LATER)
    later_grad = norm_back(cot_own, grad_normed, centred_later, inv_later, LATER)
    acted_mine = unweave_lanes(acted_later.astype(BF))
    acted_theirs = send(acted_mine, other_half_row, LATER)
    grad_pre_theirs = send(grad_pre_later, other_half, LATER)

    returned = send(later_grad, other_section, LATER)
    own_grad = jnp.where(first, returned, later_grad)
    grad_all = gather_tensor(own_grad)
    grad_part = lax.cond(
        first,
        lambda: dot(grad_all, w_out, ((1,), (1,))).astype(BF),
        lambda: jnp.broadcast_to(acted_mine[None], (8, rows, hidden)).reshape(tokens, hidden),
    )
    blocks_c = swap_dp(grad_part.reshape(8, rows, hidden))
    acted_mine_all = blocks_c.reshape(tokens, hidden)
    grad_acted_first = jnp.sum(blocks_c.astype(F32), axis=0)
    _, gelu_back_first = jax.vjp(jax.nn.gelu, sum_a)
    grad_pre_first_own = gelu_back_first(grad_acted_first)[0].astype(BF)
    blocks_d = swap_dp(
        jnp.broadcast_to(
            jnp.where(first, grad_pre_first_own, acted_theirs)[None], (8, rows, hidden)
        )
    ).reshape(tokens, hidden)

    def out_second():
        mine = acted_mine_all.reshape(tokens, 2, hidden // 2)
        theirs = blocks_d.reshape(tokens, 2, hidden // 2)
        low, high = jnp.where(half == 0, mine, theirs), jnp.where(half == 0, theirs, mine)
        left = jnp.concatenate(
            [jnp.concatenate([low[:, q], high[:, q]], axis=1) for q in (0, 1)], axis=0
        )
        return dot(left, cot_padded, ((0,), (0,))).astype(BF)

    out_grad = lax.cond(
        first, lambda: dot(acted_first, grad_all, ((0,), (0,))).astype(BF), out_second
    )

    def in_second():
        feature = jnp.arange(width)
        pieces = []
        turned = normed_later.reshape(2, 2, 2 * rows, width)
        turned = jnp.concatenate([turned[:, 1:], turned[:, :1]], axis=1).reshape(tokens, width)
        for plane, normed in ((half, normed_later), (1 - half, turned)):
            pick = one_hot(
                (feature[:, None] // part == half)
                & (feature[None, :] == 2 * (feature[:, None] % part) + plane)
            )
            pieces.append(dot(normed, pick).astype(BF))
        left = jnp.concatenate(pieces, axis=0)
        right = jnp.concatenate([grad_pre_later, grad_pre_theirs], axis=0)
        return dot(left, right, ((0,), (0,))).astype(BF)

    in_grad = lax.cond(
        first, lambda: dot(lead, blocks_d, ((0,), (0,))).astype(BF), in_second
    )
    back_first = lax.cond(
        first,
        lambda: dot(blocks_d, w_in, ((1,), (1,))).astype(BF),
        lambda: jnp.zeros((tokens, width), BF),
    )
    first_normed = scatter_tensor(back_first, FIRST)
    first_grad = norm_back(own_grad, first_normed, centred_first, inv_first, FIRST)

    place = jnp.arange(2 * rows)
    stored_token = (at % 4) * 2 * rows + 2 * (place % rows) + place // rows
    chosen = dot(one_hot(stored_token[:, None] == slot_token[None, :]), grad_all).astype(BF)
    chosen = jnp.where(half == 0, chosen[:, :part], chosen[:, part:])
    stored = jnp.concatenate([chosen[:rows], chosen[rows:]], axis=1)
    return (jnp.where(first, first_grad, stored)[None], in_grad[None], out_grad[None])


def solution(mesh):
    return jax.shard_map(
        body,
        mesh=mesh,
        in_specs=(
            P("tensor", "dp"),
            P("tensor", "dp"),
            P("section", "dp", "tensor"),
            P("section", "tensor", "dp"),
        ),
        out_specs=(
            P("section", "tensor", "dp"),
            P("section", "dp", "tensor"),
            P("section", "tensor", "dp"),
        ),
        check_vma=False,
    )
```

```python
import jax
import jax.numpy as jnp
from jax import lax
from jax.experimental import pallas as pl
from jax.experimental.pallas import tpu as pltpu
from jax.sharding import PartitionSpec as P

D = 9216
EPSILON = 1e-05
AXES = ("section", "dp", "tensor")
BF = jnp.bfloat16
F32 = jnp.float32
LATER = (1,)
BOTH = (0, 1)
VMEM_BYTES = 40 * 2**20


def send(value, move, sections=BOTH):
    pairs = []
    for s in (0, 1):
        for d in range(8):
            for t in range(8):
                s2, d2, t2 = move(s, d, t) if s in sections else (s, d, t)
                pairs.append(((s * 8 + d) * 8 + t, (s2 * 8 + d2) * 8 + t2))
    return lax.ppermute(value, AXES, pairs)


def along_x(k):
    return lambda s, d, t: (s, d // 4 * 4 + (d + k) % 4, t)


def along_z(k):
    return lambda s, d, t: (s, d, (t + 2 * k) % 8)


def across_z(k):
    return lambda s, d, t: (1 - s, d, (t + 2 * k) % 8)


def other_y(s, d, t):
    return (s, d ^ 4, t)


def other_core(s, d, t):
    return (s, d, t ^ 1)


def other_half(s, d, t):
    return (s, d, t ^ 4)


def other_half_row(s, d, t):
    return (s, d // 4 * 4 + (d + 2) % 4, t ^ 4)


def other_section(s, d, t):
    return (1 - s, d, t)


def dot(left, right, dims=((1,), (0,))):
    return lax.dot_general(left, right, (dims, ((), ())), preferred_element_type=F32)


VMEM = pl.BlockSpec(memory_space=pltpu.VMEM)
ANY = pl.BlockSpec(memory_space=pl.ANY)


def kernel_call(kernel, out_shape, in_specs, out_specs, work, **more):
    flops, moved = work
    return pl.pallas_call(
        kernel,
        out_shape=out_shape,
        in_specs=in_specs,
        out_specs=out_specs,
        compiler_params=pltpu.CompilerParams(vmem_limit_bytes=VMEM_BYTES),
        cost_estimate=pl.CostEstimate(flops=flops, bytes_accessed=moved, transcendentals=0),
        **more,
    )


def blank(*shape):
    return kernel_call(lambda out: None, jax.ShapeDtypeStruct(shape, BF), [], ANY, (0, 0))()


def weight_dot(x, parts, turned=False):
    rows = sum(part.shape[0] for part in parts)
    cols = parts[0].shape[1]
    depth, width = (cols, rows) if turned else (rows, cols)
    ends = [width // 9, width // 3, 2 * width // 3, width]
    starts = [0] + ends[:-1]
    pieces = []
    for at, end in zip(starts, ends):
        row = 0
        for index, part in enumerate(parts):
            low, high = (max(at, row), min(end, row + part.shape[0])) if turned else (row, row + part.shape[0])
            if low < high:
                pieces.append((at, index, low, high, row))
            row += part.shape[0]

    def kernel(x_ref, *refs):
        w_refs, (out, held, sems) = refs[: len(parts)], refs[len(parts) :]
        copies = []
        for number, (at, index, low, high, row) in enumerate(pieces):
            end = ends[starts.index(at)]
            lanes = slice(0, cols) if turned else slice(at, end)
            copy = pltpu.make_async_copy(
                w_refs[index].at[low - row : high - row, lanes],
                held.at[low:high, lanes],
                sems.at[number],
            )
            copy.start()
            copies.append((at, copy))
        left = x_ref[:, :depth]
        for at, end in zip(starts, ends):
            for begun, copy in copies:
                if begun == at:
                    copy.wait()
            if turned:
                made = dot(left, held[at:end, :], ((1,), (1,)))
            else:
                made = dot(left, held[:, at:end])
            out[:, at:end] = made.astype(BF)

    tokens = x.shape[0]
    return kernel_call(
        kernel,
        jax.ShapeDtypeStruct((tokens, width), BF),
        [VMEM] + [ANY] * len(parts),
        VMEM,
        (2 * tokens * rows * cols, 2 * (rows * cols + tokens * (rows + cols))),
        scratch_shapes=[
            pltpu.VMEM((rows, cols), BF),
            pltpu.SemaphoreType.DMA((len(pieces),)),
        ],
    )(x, *parts)


def split_planes(w, pick, pieces):
    height, width = w.shape
    part = height // 2
    block = pick.shape[0]
    sub = block // 2

    def kernel(w_ref, pick_ref, kept, *away):
        for at in range(height // block):
            rows = dot(pick_ref[...], w_ref[at * block : (at + 1) * block, :]).astype(BF)
            kept[at * sub : (at + 1) * sub, :] = rows[:sub]
            per = part // pieces // sub
            away[at // per][at % per * sub : (at % per + 1) * sub, :] = rows[sub:]

    shapes = [jax.ShapeDtypeStruct((part, width), BF)]
    shapes += [jax.ShapeDtypeStruct((part // pieces, width), BF)] * pieces
    return kernel_call(
        kernel,
        shapes,
        [VMEM, VMEM],
        [VMEM] * (1 + pieces),
        (2 * height * width * block, 4 * height * width),
    )(w, pick)


def cot_spread(padded, w_out, half):
    _, tokens, width = padded.shape
    height = w_out.shape[0] // 2

    def kernel(half_ref, x_ref, w_ref, out):
        for q in (0, 1):
            made = dot(x_ref[q], w_ref[...], ((1,), (1,)))
            out[0, :, q * height : (q + 1) * height] = made.astype(BF)

    return pl.pallas_call(
        kernel,
        out_shape=jax.ShapeDtypeStruct((2, tokens, 2 * height), BF),
        grid_spec=pltpu.PrefetchScalarGridSpec(
            num_scalar_prefetch=1,
            grid=(2,),
            in_specs=[
                pl.BlockSpec((2, tokens, width), lambda i, half_ref: (0, 0, 0)),
                pl.BlockSpec((height, width), lambda i, half_ref: (half_ref[0] ^ i, 0)),
            ],
            out_specs=pl.BlockSpec((1, tokens, 2 * height), lambda i, half_ref: (i, 0, 0)),
        ),
        compiler_params=pltpu.CompilerParams(vmem_limit_bytes=VMEM_BYTES),
    )(half.reshape(1), padded, w_out)


def out_product(mine, theirs, padded, half):
    tokens, double = mine.shape
    height = double // 2
    width = padded.shape[2]

    def kernel(half_ref, mine_ref, theirs_ref, x_ref, out):
        def fill(ref):
            total = dot(ref[:, :height], x_ref[0], ((0,), (0,)))
            total += dot(ref[:, height:], x_ref[1], ((0,), (0,)))
            out[...] = total.astype(BF)

        @pl.when(pl.program_id(0) == 0)
        def _():
            fill(mine_ref)

        @pl.when(pl.program_id(0) == 1)
        def _():
            fill(theirs_ref)

    whole = pl.BlockSpec((tokens, double), lambda i, half_ref: (0, 0))
    return pl.pallas_call(
        kernel,
        out_shape=jax.ShapeDtypeStruct((double, width), BF),
        grid_spec=pltpu.PrefetchScalarGridSpec(
            num_scalar_prefetch=1,
            grid=(2,),
            in_specs=[
                whole,
                whole,
                pl.BlockSpec((2, tokens, width), lambda i, half_ref: (0, 0, 0)),
            ],
            out_specs=pl.BlockSpec((height, width), lambda i, half_ref: (half_ref[0] ^ i, 0)),
        ),
        compiler_params=pltpu.CompilerParams(vmem_limit_bytes=VMEM_BYTES),
    )(half.reshape(1), mine, theirs, padded)


def outer_product(lefts, rights, width, steps):
    tokens, height = lefts[0].shape
    count = len(lefts)
    tile = height // steps

    def kernel(*refs):
        out = refs[-1]
        total = 0.0
        for left, right in zip(refs[:count], refs[count:-1]):
            total = total + dot(left[...], right[:, :width], ((0,), (0,)))
        out[...] = total.astype(BF)

    return pl.pallas_call(
        kernel,
        out_shape=jax.ShapeDtypeStruct((height, width), BF),
        grid=(steps,),
        in_specs=[pl.BlockSpec((tokens, tile), lambda i: (0, i))] * count
        + [pl.BlockSpec(right.shape, lambda i: (0, 0)) for right in rights],
        out_specs=pl.BlockSpec((tile, width), lambda i: (i, 0)),
        compiler_params=pltpu.CompilerParams(vmem_limit_bytes=VMEM_BYTES),
    )(*lefts, *rights)


def halves(values):
    top = lax.reduce_precision(values, 8, 7)
    return top.astype(BF), (values - top).astype(BF)


def pack(*columns):
    top, rest = halves(jnp.stack(columns, axis=1))
    both = jnp.concatenate([top, rest], axis=1)
    return jnp.pad(both, ((0, 0), (0, 128 - both.shape[1])))


def unpack(block, count):
    block = block.astype(F32)
    both = block[:, :count] + block[:, count : 2 * count]
    return [both[:, i] for i in range(count)]


def gather_tensor(x):
    pair = jnp.concatenate([x] + [send(x, along_z(k)) for k in (1, 2, 3)], axis=0)
    return jnp.concatenate([pair, send(pair, other_core)], axis=0)


def sum_cores(partial):
    half = partial.shape[0] // 2
    arrived = send(partial[half:], other_core)
    return partial[:half].astype(F32) + arrived.astype(F32)


def scatter_tensor(partial, sums):
    rows = partial.shape[0] // 8
    width = partial.shape[1]
    half = partial.shape[0] // 2
    arrived = send(jnp.concatenate([partial[half:], pack(*(c[half:] for c in sums))], axis=1), other_core)
    total = partial[:half].astype(F32) + arrived[:, :width].astype(F32)
    sums = [c[:half] + other for c, other in zip(sums, unpack(arrived[:, width:], 2))]
    ready = jnp.concatenate([total.astype(BF), pack(*sums)], axis=1)
    mine, sums = total[:rows], [c[:rows] for c in sums]
    for k in (1, 2, 3):
        came = send(ready[k * rows : (k + 1) * rows], along_z(-k))
        mine = mine + came[:, :width].astype(F32)
        sums = [c + other for c, other in zip(sums, unpack(came[:, width:], 2))]
    return mine, sums


def swap_dp(blocks):
    return lax.all_to_all(blocks, "dp", 0, 0, tiled=True)


def share_dp(own):
    whole = swap_dp(jnp.broadcast_to(own[None], (8, *own.shape)))
    return whole.reshape(8 * own.shape[0], own.shape[1])


def sum_dp(value):
    total = value
    for k in (1, 2, 3):
        total = total + send(value, along_x(k))
    return total + send(total, other_y)


def norm_back(grad_out, grad_normed, centred, inv_std, sums):
    mean_grad, mean_mixed = sums
    stream_grad = grad_out.astype(F32) + inv_std[:, None] * (
        grad_normed - mean_grad[:, None] / D - centred * (mean_mixed[:, None] / D)
    )
    return stream_grad.astype(BF)


def one_hot(condition):
    return condition.astype(BF)


def after(value, *others):
    return lax.optimization_barrier((value, *others))[0]


def body(inputs, cotangent, w_first, w_second):
    w_in, w_out = w_first[0], w_second[0]
    rows, width = inputs.shape
    hidden = w_in.shape[1]
    part = width // 2
    tokens = 8 * rows
    first = lax.axis_index("section") == 0
    at = lax.axis_index("tensor")
    z_at, core_at = at // 2, at % 2
    half = at // 4

    slot_row = jnp.arange(tokens)
    slot_owner = ((z_at - slot_row // rows % 4) % 4) * 2 + (core_at ^ (slot_row // (4 * rows)))
    slot_token = slot_owner * rows + slot_row % rows

    block = 128
    index = jnp.arange(block)
    picked = 2 * (index % (block // 2)) + jnp.where(index < block // 2, half, 1 - half)
    pick = one_hot(index[None, :] == picked[:, None])
    pieces = 3

    def no_planes():
        return [blank(part, hidden)] + [blank(part // pieces, hidden) for _ in range(pieces)]

    kept, *away = lax.cond(first, no_planes, lambda: list(split_planes(w_in, pick, pieces)))
    came = [send(piece, other_half, LATER) for piece in away]
    w_parts = [kept, *came]

    values = inputs.astype(F32)
    both = sum_dp(jnp.stack([jnp.sum(values, axis=1), jnp.sum(values * values, axis=1)]))
    mean_row = both[0] / D
    inv_first = lax.rsqrt(both[1] / D - mean_row * mean_row + EPSILON)
    centred_first = (values - mean_row[:, None]) * inv_first[:, None]
    lead = gather_tensor(jnp.where(first, centred_first.astype(BF), cotangent))

    def lead_second():
        blocks = lead.reshape(2, 4, rows, 2, part)
        k_near = jnp.where(z_at % 2 == 0, 3, 1)
        near = lax.dynamic_index_in_dim(blocks, k_near, 1, keepdims=True)
        far = lax.dynamic_index_in_dim(blocks, 4 - k_near, 1, keepdims=True)
        mine = jnp.concatenate([blocks[:, :1], near], axis=1)
        rest = jnp.concatenate([blocks[:, 2:3], far], axis=1)

        def flat(group):
            return group.transpose(0, 1, 3, 2, 4).reshape(tokens, part)

        row = jnp.arange(tokens)
        e, j = row // (4 * rows), row // (2 * rows) % 2
        q, r = row // rows % 2, row % rows
        c_block = (z_at % 2 ^ j) * 2 + (core_at ^ e)
        token = c_block * 2 * rows + 2 * r + q
        order = one_hot(slot_token[:, None] == token[None, :])
        own = dot(order, flat(mine)).astype(BF)
        other = dot(order[:rows], flat(rest)).astype(BF)
        blanks = jnp.zeros_like(own)
        padded = jnp.stack(
            [jnp.concatenate([own, blanks], axis=1), jnp.concatenate([blanks, own], axis=1)]
        )
        spread = cot_spread(padded, w_out, half)
        cot_own = jnp.where(
            half == 0,
            jnp.concatenate([own[:rows], other], axis=1),
            jnp.concatenate([other, own[:rows]], axis=1),
        )
        return spread[0], spread[1], padded, cot_own

    def lead_first():
        made = weight_dot(lead, [w_in])
        return made, blank(tokens, hidden), blank(2, tokens, width), blank(rows, width)

    part_a, part_b, cot_padded, cot_own = lax.cond(first, lead_first, lead_second)
    sum_a = jnp.sum(swap_dp(after(part_a, came[0]).reshape(8, rows, hidden)).astype(F32), axis=0)
    acted_own_first = jax.nn.gelu(sum_a).astype(BF)
    ready_b = jnp.where(first, acted_own_first[None], part_b.reshape(8, rows, hidden))
    blocks_b = swap_dp(after(ready_b, came[1]))
    acted_first = blocks_b.reshape(tokens, hidden)
    sum_b = jnp.sum(blocks_b.astype(F32), axis=0)
    branch_part = lax.cond(
        first, lambda: weight_dot(acted_first, [w_out]), lambda: blank(tokens, width)
    )
    branch_part = after(branch_part, came[2])
    branch = sum_cores(branch_part).astype(BF)
    stream = values
    for k in range(4):
        arrived = send(branch[k * rows : (k + 1) * rows], across_z(-k))
        stream = stream + arrived.astype(F32)
    stream_own = stream.astype(BF)

    grad_acted = sum_a + send(sum_b.astype(BF), other_half_row, LATER).astype(F32)
    groups = hidden // 256
    lane = jnp.arange(256)
    weave = one_hot(lane[None, :] == 2 * (lane[:, None] % 128) + lane[:, None] // 128)

    def weave_lanes(value):
        stacked = value.reshape(rows, 2, groups, 128).transpose(2, 0, 1, 3)
        top, rest = halves(stacked.reshape(groups * rows, 256))
        done = dot(top, weave) + dot(rest, weave)
        return done.reshape(groups, rows, 256).transpose(1, 0, 2).reshape(rows, hidden)

    def unweave_lanes(value):
        stacked = value.reshape(rows, groups, 256).transpose(1, 0, 2).reshape(groups * rows, 256)
        done = dot(stacked, weave, ((1,), (1,))).astype(BF)
        done = done.reshape(groups, rows, 2, 128).transpose(1, 2, 0, 3)
        return done.reshape(rows, hidden)

    def swap_halves(value):
        turned = jnp.concatenate([value[:, part:], value[:, :part]], axis=1)
        return jnp.where(half == 0, value, turned)

    grad_acted = weave_lanes(grad_acted)

    def column_sums(*parts):
        ones = jnp.ones((8, parts[0].shape[0]), BF)
        return sum(dot(ones[:, : w.shape[0]], w)[0] for w in parts)

    columns = lax.cond(
        first, lambda: column_sums(w_in), lambda: column_sums(*w_parts)
    )

    stream_all = gather_tensor(stream_own)
    spread = stream_all.astype(F32)
    block_mean = jnp.sum(spread, axis=1) / width
    off_mean = spread - block_mean[:, None]
    block_square = jnp.sum(off_mean * off_mean, axis=1)
    shift = lax.reduce_precision(block_mean, 8, 7)
    shifted = swap_halves((spread - shift[:, None]).astype(BF))
    pre_part = lax.cond(
        first, lambda: blank(tokens, hidden), lambda: weight_dot(shifted, w_parts)
    )
    column_rows = hidden // 128
    top, rest = halves(columns)
    column_block = jnp.concatenate(
        [top.reshape(column_rows, 128), rest.reshape(column_rows, 128)], axis=1
    )
    token_block = jnp.concatenate(
        [
            piece.reshape(8, 1, rows)
            for piece in (*halves(block_mean), *halves(block_square))
        ],
        axis=2,
    )
    token_block = jnp.pad(
        token_block, ((0, 0), (0, rows - column_rows - 1), (0, 256 - 4 * rows))
    )
    beside = jnp.concatenate(
        [jnp.broadcast_to(column_block[None], (8, column_rows, 256)), token_block], axis=1
    )
    blocks = swap_dp(jnp.concatenate([pre_part.reshape(8, rows, hidden), beside], axis=2))
    beside = blocks[:, : column_rows + 1, hidden:].astype(F32)
    columns_dp = (beside[:, :column_rows, :128] + beside[:, :column_rows, 128:]).reshape(8, hidden)
    token_row = beside[:, column_rows, : 4 * rows].reshape(8, 4, rows)
    shifts = token_row[:, 0]
    means, squares = shifts + token_row[:, 1], token_row[:, 2] + token_row[:, 3]
    mean_later = jnp.sum(means, axis=0) / 8
    off = means - mean_later[None]
    inv_later = lax.rsqrt(
        (jnp.sum(squares, axis=0) + width * jnp.sum(off * off, axis=0)) / D + EPSILON
    )
    pre_later = jnp.sum(blocks[:, :, :hidden].astype(F32), axis=0)
    for d in range(8):
        pre_later = pre_later + (shifts[d] - mean_later)[:, None] * columns_dp[d][None, :]
    pre_later = pre_later * inv_later[:, None]
    column_total = jnp.sum(columns_dp, axis=0)

    acted_later, gelu_back = jax.vjp(jax.nn.gelu, pre_later)
    grad_pre_own = gelu_back(grad_acted)[0].astype(BF)

    def back_sums(grad_pre, pre):
        grad_pre = grad_pre.astype(F32)
        return jnp.sum(grad_pre * column_total[None], axis=1), jnp.sum(grad_pre * pre, axis=1)

    later_pack = pack(mean_later, inv_later, *back_sums(grad_pre_own, pre_later))
    grad_pre_later = share_dp(jnp.concatenate([grad_pre_own, later_pack], axis=1))
    mean_all, inv_all, *later_sums = unpack(grad_pre_later[:, hidden:], 4)
    centred_all = (spread - mean_all[:, None]) * inv_all[:, None]
    normed_later = centred_all.astype(BF)
    back_part = swap_halves(
        lax.cond(
            first,
            lambda: blank(tokens, width),
            lambda: weight_dot(grad_pre_later, w_parts, turned=True),
        )
    )
    grad_normed, later_sums = scatter_tensor(back_part, later_sums)
    later_grad = norm_back(cot_own, grad_normed, centred_all[:rows], inv_all[:rows], later_sums)
    acted_mine = unweave_lanes(acted_later.astype(BF))
    acted_theirs = send(acted_mine, other_half_row, LATER)
    grad_pre_theirs = send(grad_pre_later[:, :hidden], other_half, LATER)

    returned = send(later_grad, other_section)
    own_grad = jnp.where(first, returned, later_grad)
    grad_all = gather_tensor(own_grad)
    grad_part = lax.cond(
        first,
        lambda: weight_dot(grad_all, [w_out], turned=True),
        lambda: jnp.broadcast_to(acted_mine[None], (8, rows, hidden)).reshape(tokens, hidden),
    )
    blocks_c = swap_dp(grad_part.reshape(8, rows, hidden))
    acted_mine_all = blocks_c.reshape(tokens, hidden)
    grad_acted_first = jnp.sum(blocks_c.astype(F32), axis=0)
    _, gelu_back_first = jax.vjp(jax.nn.gelu, sum_a)
    grad_pre_first = gelu_back_first(grad_acted_first)[0].astype(BF)
    first_pack = pack(*back_sums(grad_pre_first, sum_a))
    blocks_d = share_dp(
        jnp.concatenate([jnp.where(first, grad_pre_first, acted_theirs), first_pack], axis=1)
    )
    back_first = lax.cond(
        first,
        lambda: weight_dot(blocks_d, [w_in], turned=True),
        lambda: blank(tokens, width),
    )
    first_normed, first_sums = scatter_tensor(back_first, unpack(blocks_d[:, hidden:], 2))
    first_grad = norm_back(own_grad, first_normed, centred_first, inv_first, first_sums)

    out_grad = lax.cond(
        first,
        lambda: outer_product([acted_first], [grad_all], width, 3),
        lambda: out_product(acted_mine_all, blocks_d[:, :hidden], cot_padded, half),
    )

    def in_second():
        feature = jnp.arange(width)
        turned = normed_later.reshape(2, 2, 2 * rows, width)
        turned = jnp.concatenate([turned[:, 1:], turned[:, :1]], axis=1).reshape(tokens, width)
        lefts = []
        for plane, normed in ((half, normed_later), (1 - half, turned)):
            pick = one_hot(
                (feature[:, None] // part == half)
                & (feature[None, :] == 2 * (feature[:, None] % part) + plane)
            )
            lefts.append(dot(normed, pick).astype(BF))
        return outer_product(lefts, [grad_pre_later, grad_pre_theirs], hidden, 3)

    in_grad = lax.cond(first, lambda: outer_product([lead], [blocks_d], hidden, 3), in_second)

    place = jnp.arange(2 * rows)
    stored_token = (at % 4) * 2 * rows + 2 * (place % rows) + place // rows
    chosen = dot(one_hot(stored_token[:, None] == slot_token[None, :]), grad_all).astype(BF)
    chosen = jnp.where(half == 0, chosen[:, :part], chosen[:, part:])
    stored = jnp.concatenate([chosen[:rows], chosen[rows:]], axis=1)
    return (jnp.where(first, first_grad, stored)[None], in_grad[None], out_grad[None])


def solution(mesh):
    return jax.shard_map(
        body,
        mesh=mesh,
        in_specs=(
            P("tensor", "dp"),
            P("tensor", "dp"),
            P("section", "dp", "tensor"),
            P("section", "tensor", "dp"),
        ),
        out_specs=(
            P("section", "tensor", "dp"),
            P("section", "dp", "tensor"),
            P("section", "tensor", "dp"),
        ),
        check_vma=False,
    )
```

```python
import jax
import jax.numpy as jnp
from jax import lax
from jax.experimental import pallas as pl
from jax.experimental.layout import Layout, with_layout_constraint
from jax.experimental.pallas import tpu as pltpu
from jax.sharding import PartitionSpec as P

D = 9216
EPSILON = 1e-05
AXES = ("section", "dp", "tensor")
BF = jnp.bfloat16
F32 = jnp.float32
LATER = (1,)
BOTH = (0, 1)
MIB = 2**20


def by_rows(value):
    return with_layout_constraint(value, Layout(major_to_minor=tuple(range(value.ndim))))


def send(value, move, sections=BOTH):
    pairs = []
    for s in sections:
        for d in range(8):
            for t in range(8):
                s2, d2, t2 = move(s, d, t)
                pairs.append(((s * 8 + d) * 8 + t, (s2 * 8 + d2) * 8 + t2))
    return by_rows(lax.ppermute(by_rows(value), AXES, pairs))


def along_x(k):
    return lambda s, d, t: (s, d // 4 * 4 + (d + k) % 4, t)


def along_z(k):
    return lambda s, d, t: (s, d, (t + 2 * k) % 8)


def across_z(k):
    return lambda s, d, t: (1 - s, d, (t + 2 * k) % 8)


def other_y(s, d, t):
    return (s, d ^ 4, t)


def other_core(s, d, t):
    return (s, d, t ^ 1)


def other_half(s, d, t):
    return (s, d, t ^ 4)


def other_half_row(s, d, t):
    return (s, d // 4 * 4 + (d + 2) % 4, t ^ 4)


def other_section(s, d, t):
    return (1 - s, d, t)


def dot(left, right, dims=((1,), (0,))):
    return lax.dot_general(left, right, (dims, ((), ())), preferred_element_type=F32)


VMEM = pl.BlockSpec(memory_space=pltpu.VMEM)
ANY = pl.BlockSpec(memory_space=pl.ANY)
SMEM = pl.BlockSpec(memory_space=pltpu.SMEM)


def kernel_call(kernel, out_shape, in_specs, out_specs, work, limit=4, **more):
    flops, moved = work
    return pl.pallas_call(
        kernel,
        out_shape=out_shape,
        in_specs=in_specs,
        out_specs=out_specs,
        compiler_params=pltpu.CompilerParams(vmem_limit_bytes=limit * MIB),
        cost_estimate=pl.CostEstimate(flops=flops, bytes_accessed=moved, transcendentals=0),
        **more,
    )


def blank(*shape):
    return kernel_call(lambda out: None, jax.ShapeDtypeStruct(shape, BF), [], ANY, (0, 0))()


def stream_plan(parts, turned):
    rows = sum(part.shape[0] for part in parts)
    cols = parts[0].shape[1]
    width = rows if turned else cols
    ends = [width // 9, width // 3, 2 * width // 3, width]
    chunks = list(zip([0] + ends[:-1], ends))
    pieces = []
    for number, (at, end) in enumerate(chunks):
        row = 0
        for index, part in enumerate(parts):
            low, high = row, row + part.shape[0]
            row = high
            if turned:
                low, high = max(at, low), min(end, high)
            if low < high:
                pieces.append((number, index, low, high))
    return rows, cols, chunks, pieces, turned


def stream_copies(plan, parts, held, sems, turn=0):
    rows, cols, chunks, pieces, turned = plan
    first_rows = [0]
    for part in parts:
        first_rows.append(first_rows[-1] + part.shape[0])
    copies = []
    for sem, (number, index, low, high) in enumerate(pieces):
        at, end = (0, cols) if turned else chunks[number]
        begin = first_rows[index]
        to = low if isinstance(turn, int) else pl.multiple_of(lax.rem(low + turn, rows), 16)
        copy = pltpu.make_async_copy(
            parts[index].at[pl.ds(low - begin, high - low), pl.ds(at, end - at)],
            held.at[pl.ds(to, high - low), pl.ds(at, end - at)],
            sems.at[sem],
        )
        copies.append((number, copy))
    return copies


def weight_dot(x, w):
    plan = stream_plan([w], False)
    rows, cols, chunks, pieces, _ = plan
    tokens = x.shape[0]

    def kernel(x_ref, w_ref, out, held, sems):
        copies = stream_copies(plan, [w_ref], held, sems)
        for _, copy in copies:
            copy.start()
        left = x_ref[...]
        for number, (at, end) in enumerate(chunks):
            copies[number][1].wait()
            out[:, at:end] = dot(left, held[:, at:end]).astype(BF)

    return kernel_call(
        kernel,
        jax.ShapeDtypeStruct((tokens, cols), BF),
        [VMEM, ANY],
        VMEM,
        (2 * tokens * rows * cols, 2 * (rows * cols + tokens * (rows + cols))),
        limit=9,
        scratch_shapes=[pltpu.VMEM((rows, cols), BF), pltpu.SemaphoreType.DMA((len(pieces),))],
    )(x, w)


def grad_spread(place, x, w, own):
    plan = stream_plan([w], True)
    rows, cols, chunks, pieces, _ = plan
    tokens = x.shape[0]
    part = tokens // 8

    def kernel(place_ref, x_ref, w_ref, own_ref, out, held, sems):
        @pl.when(place_ref[0] == 0)
        def _():
            copies = stream_copies(plan, [w_ref], held, sems)
            for _, copy in copies:
                copy.start()
            left = x_ref[...]
            for number, (at, end) in enumerate(chunks):
                copies[number][1].wait()
                made = dot(left, held[at:end, :], ((1,), (1,))).astype(BF)
                out[:, :, at:end] = made.reshape(8, part, end - at)

        @pl.when(place_ref[0] == 1)
        def _():
            for j in range(8):
                out[j] = own_ref[...]

    return kernel_call(
        kernel,
        jax.ShapeDtypeStruct((8, part, rows), BF),
        [SMEM, VMEM, ANY, VMEM],
        VMEM,
        (2 * tokens * rows * cols, 2 * (rows * cols + tokens * (rows + cols))),
        limit=9,
        scratch_shapes=[pltpu.VMEM((rows, cols), BF), pltpu.SemaphoreType.DMA((len(pieces),))],
    )(place, x, w, own)


ROOT = 0.7978845608028654
CUBE = 0.044715


def gelu_parts(v):
    bent = jnp.tanh(ROOT * (v + CUBE * v * v * v))
    slope = 0.5 * (1.0 + bent) + 0.5 * v * (1.0 - bent * bent) * ROOT * (1.0 + 3.0 * CUBE * v * v)
    return 0.5 * v * (1.0 + bent), slope


def two_terms(value):
    top = value.astype(BF).astype(F32)
    return top, value - top


def lane_pack(columns):
    rows = columns[0].shape[0]
    lane = lax.broadcasted_iota(jnp.int32, (rows, 128), 1)
    block = jnp.zeros((rows, 128), F32)
    for number, column in enumerate(columns):
        block = jnp.where(lane == number, column, block)
    return block


def sums_pack(mean, inv, one, two):
    pairs = [two_terms(c) for c in (mean, inv, one, two)]
    return lane_pack([p[0] for p in pairs] + [p[1] for p in pairs]).astype(BF)


def spread_first(place, swapped, part_b):
    _, rows, hidden = swapped.shape

    def kernel(place_ref, swapped_ref, part_ref, total_ref, ready_ref, sem):
        @pl.when(place_ref[0] == 1)
        def _():
            copy = pltpu.make_async_copy(part_ref, ready_ref, sem)
            copy.start()
            copy.wait()

        for g in range(hidden // 128):
            lanes = slice(g * 128, (g + 1) * 128)
            total = swapped_ref[0, :, lanes].astype(F32)
            for j in range(1, 8):
                total = total + swapped_ref[j, :, lanes].astype(F32)
            total_ref[:, lanes] = total

        @pl.when(place_ref[0] == 0)
        def _():
            for g in range(hidden // 128):
                lanes = slice(g * 128, (g + 1) * 128)
                acted = gelu_parts(total_ref[:, lanes])[0].astype(BF)
                for j in range(8):
                    ready_ref[j, :, lanes] = acted

    return kernel_call(
        kernel,
        [
            jax.ShapeDtypeStruct((rows, hidden), F32),
            jax.ShapeDtypeStruct(swapped.shape, BF),
        ],
        [SMEM, VMEM, ANY],
        [VMEM, VMEM],
        (30 * rows * hidden, 40 * rows * hidden),
        scratch_shapes=[pltpu.SemaphoreType.DMA(())],
    )(place, swapped, part_b)


def branch_first(place, blocks, w_out):
    _, rows, hidden = blocks.shape
    tokens = 8 * rows
    plan = stream_plan([w_out], False)
    _, width, chunks, pieces, _ = plan

    def kernel(place_ref, x_ref, w_ref, low, high, total_ref, held, sems):
        @pl.when(place_ref[0] == 0)
        def _():
            copies = stream_copies(plan, [w_ref], held, sems)
            for _, copy in copies:
                copy.start()
            left = x_ref[...].reshape(tokens, hidden)
            for number, (at, end) in enumerate(chunks):
                copies[number][1].wait()
                made = dot(left, held[:, at:end]).astype(BF)
                low[:, at:end] = made[: tokens // 2]
                high[:, at:end] = made[tokens // 2 :]

        @pl.when(place_ref[0] == 1)
        def _():
            for g in range(hidden // 128):
                lanes = slice(g * 128, (g + 1) * 128)
                total = x_ref[0, :, lanes].astype(F32)
                for j in range(1, 8):
                    total = total + x_ref[j, :, lanes].astype(F32)
                total_ref[:, lanes] = total.astype(BF)

    return kernel_call(
        kernel,
        [
            jax.ShapeDtypeStruct((tokens // 2, width), BF),
            jax.ShapeDtypeStruct((tokens // 2, width), BF),
            jax.ShapeDtypeStruct((rows, hidden), BF),
        ],
        [SMEM, VMEM, ANY],
        [VMEM] * 3,
        (2 * tokens * hidden * width, 2 * hidden * width),
        limit=9,
        scratch_shapes=[
            pltpu.VMEM((hidden, width), BF),
            pltpu.SemaphoreType.DMA((len(pieces),)),
        ],
    )(place, blocks, w_out)


def pre_later_part(place, pair, other, w_in, w_parts):
    quarter, width = pair.shape
    tokens = 2 * quarter
    rows = tokens // 8
    hidden = w_in.shape[1]
    plans = [stream_plan([w_in], False), stream_plan(w_parts, False)]
    chunks = plans[0][2]
    count = max(len(plan[3]) for plan in plans)

    def kernel(place_ref, pair_ref, other_ref, w_ref, *refs):
        part_refs, (out, held, left, sems) = refs[: len(w_parts)], refs[len(w_parts) :]
        copies = [
            stream_copies(plans[0], [w_ref], held, sems),
            stream_copies(plans[1], part_refs, held, sems, place_ref[1] * (width // 2)),
        ]
        for section in (0, 1):

            @pl.when(place_ref[0] == section)
            def _():
                for _, copy in copies[section]:
                    copy.start()

        for e, ref in enumerate((pair_ref, other_ref)):
            spread = ref[...].astype(F32)
            mean = jnp.sum(spread, axis=1, keepdims=True) / width
            off = spread - mean
            square = jnp.sum(off * off, axis=1, keepdims=True)
            shift = mean.astype(BF).astype(F32)
            left[e * quarter : (e + 1) * quarter, :] = (spread - shift).astype(BF)
            block = lane_pack([*two_terms(mean), *two_terms(square)]).astype(BF)
            out[e * 4 : (e + 1) * 4, :, hidden + 256 :] = block.reshape(4, rows, 128)
        left[tokens:, :] = jnp.ones((16, width), BF)
        tops, rests = [], []
        for number, (at, end) in enumerate(chunks):
            for section in (0, 1):

                @pl.when(place_ref[0] == section)
                def _():
                    for begun, copy in copies[section]:
                        if begun == number:
                            copy.wait()

            made = dot(left[...], held[:, at:end])
            out[:, :, at:end] = made[:tokens].astype(BF).reshape(8, rows, end - at)
            top, rest = two_terms(made[tokens : tokens + 1])
            for g in range((end - at) // 128):
                tops.append(top[:, g * 128 : (g + 1) * 128])
                rests.append(rest[:, g * 128 : (g + 1) * 128])
        empty = [jnp.zeros((rows - len(tops), 128), F32)]
        for number, rows_list in enumerate((tops, rests)):
            block = jnp.concatenate(rows_list + empty, axis=0).astype(BF)
            lanes = slice(hidden + 128 * number, hidden + 128 * (number + 1))
            for j in range(8):
                out[j, :, lanes] = block

    return kernel_call(
        kernel,
        jax.ShapeDtypeStruct((8, rows, hidden + 384), BF),
        [SMEM, VMEM, VMEM, ANY] + [ANY] * len(w_parts),
        VMEM,
        (2 * tokens * hidden * width, 2 * hidden * width),
        limit=12,
        scratch_shapes=[
            pltpu.VMEM((width, hidden), BF),
            pltpu.VMEM((tokens + 16, width), BF),
            pltpu.SemaphoreType.DMA((count,)),
        ],
    )(place, pair, other, w_in, *w_parts)


def weave(turned):
    row = lax.broadcasted_iota(jnp.int32, (256, 256), 0)
    lane = lax.broadcasted_iota(jnp.int32, (256, 256), 1)
    if turned:
        row, lane = lane, row
    return jnp.where(lane == 2 * (row % 128) + row // 128, 1.0, 0.0).astype(BF)


def grad_pre_later(blocks, grad_mine, grad_theirs, width):
    _, rows, wide = blocks.shape
    hidden = wide - 384
    plane = hidden // 2

    def kernel(blocks_ref, mine_ref, theirs_ref, ready, acted_ref, total_ref, grad_ref, held_ref):
        order, back = weave(False), weave(True)
        for b in range(hidden // 256):
            pair = []
            for q in (0, 1):
                lanes = slice(q * plane + b * 128, q * plane + (b + 1) * 128)
                pair.append(mine_ref[:, lanes] + theirs_ref[:, lanes].astype(F32))
            top, rest = two_terms(jnp.concatenate(pair, axis=1))
            done = dot(top.astype(BF), order) + dot(rest.astype(BF), order)
            grad_ref[:, b * 256 : (b + 1) * 256] = done
        beside = blocks_ref[:, :, hidden:].astype(F32)
        stats = beside[:, :, 256:]
        shifts = [stats[d, :, 0:1] for d in range(8)]
        means = [stats[d, :, 0:1] + stats[d, :, 1:2] for d in range(8)]
        mean = sum(means) / 8
        square = sum(
            stats[d, :, 2:3] + stats[d, :, 3:4] + width * (means[d] - mean) ** 2 for d in range(8)
        )
        inv = lax.rsqrt(square / D + EPSILON)
        moves = [shift - mean for shift in shifts]
        one = jnp.zeros((rows, 1), F32)
        two = jnp.zeros((rows, 1), F32)
        for g in range(hidden // 128):
            lanes = slice(g * 128, (g + 1) * 128)
            pre = jnp.zeros((rows, 128), F32)
            columns = jnp.zeros((1, 128), F32)
            for d in range(8):
                column = beside[d, g : g + 1, :128] + beside[d, g : g + 1, 128:256]
                columns = columns + column
                pre = pre + blocks_ref[d, :, lanes].astype(F32) + moves[d] * column
            pre = pre * inv
            total_ref[:, lanes] = jnp.broadcast_to(columns, (8, 128))
            acted, slope = gelu_parts(pre)
            held_ref[:, lanes] = acted.astype(BF)
            grad = (grad_ref[:, lanes] * slope).astype(BF)
            for j in range(8):
                ready[j, :, lanes] = grad
            grad = grad.astype(F32)
            one = one + jnp.sum(grad * columns, axis=1, keepdims=True)
            two = two + jnp.sum(grad * pre, axis=1, keepdims=True)
        block = sums_pack(mean, inv, one, two)
        for j in range(8):
            ready[j, :, hidden:] = block
        for b in range(hidden // 256):
            done = dot(held_ref[:, b * 256 : (b + 1) * 256], back).astype(BF)
            acted_ref[:, b * 128 : (b + 1) * 128] = done[:, :128]
            acted_ref[:, plane + b * 128 : plane + (b + 1) * 128] = done[:, 128:]

    return kernel_call(
        kernel,
        [
            jax.ShapeDtypeStruct((8, rows, hidden + 128), BF),
            jax.ShapeDtypeStruct((rows, hidden), BF),
            jax.ShapeDtypeStruct((8, hidden), F32),
        ],
        [VMEM] * 3,
        [VMEM] * 3,
        (80 * rows * hidden, 40 * rows * hidden),
        scratch_shapes=[pltpu.VMEM((rows, hidden), F32), pltpu.VMEM((rows, hidden), BF)],
    )(blocks, grad_mine, grad_theirs)


def grad_pre_first(place, blocks, pre, columns, theirs):
    _, rows, hidden = blocks.shape

    def kernel(place_ref, blocks_ref, pre_ref, columns_ref, theirs_ref, ready):
        @pl.when(place_ref[0] == 0)
        def _():
            one = jnp.zeros((rows, 1), F32)
            two = jnp.zeros((rows, 1), F32)
            for g in range(hidden // 128):
                lanes = slice(g * 128, (g + 1) * 128)
                total = blocks_ref[0, :, lanes].astype(F32)
                for j in range(1, 8):
                    total = total + blocks_ref[j, :, lanes].astype(F32)
                pre = pre_ref[:, lanes]
                grad = (total * gelu_parts(pre)[1]).astype(BF)
                for j in range(8):
                    ready[j, :, lanes] = grad
                grad = grad.astype(F32)
                one = one + jnp.sum(grad * columns_ref[0:1, lanes], axis=1, keepdims=True)
                two = two + jnp.sum(grad * pre, axis=1, keepdims=True)
            block = sums_pack(one, one, one, two)
            for j in range(8):
                ready[j, :, hidden:] = block

        @pl.when(place_ref[0] == 1)
        def _():
            for j in range(8):
                ready[j, :, :hidden] = theirs_ref[...]
                ready[j, :, hidden:] = jnp.zeros((rows, 128), BF)

    return kernel_call(
        kernel,
        jax.ShapeDtypeStruct((8, rows, hidden + 128), BF),
        [SMEM] + [VMEM] * 4,
        VMEM,
        (60 * rows * hidden, 40 * rows * hidden),
    )(place, blocks, pre, columns, theirs)


def back_part(place, section, grad_pre, w_parts):
    tokens, wide = grad_pre.shape
    hidden = wide - 128
    plan = stream_plan(w_parts, True)
    width, _, chunks, pieces, _ = plan

    def kernel(place_ref, x_ref, *refs):
        w_refs, (low, high, held, made, sems) = refs[: len(w_parts)], refs[len(w_parts) :]

        @pl.when(place_ref[0] == section)
        def _():
            copies = stream_copies(plan, w_refs, held, sems)
            for _, copy in copies:
                copy.start()
            left = x_ref[:, :hidden]
            for number, (at, end) in enumerate(chunks):
                for begun, copy in copies:
                    if begun == number:
                        copy.wait()
                made[:, at:end] = dot(left, held[at:end, :], ((1,), (1,)))
            done = made[...]
            if section == 1:
                done = jnp.where(place_ref[1] == 0, done, pltpu.roll(done, width // 2, 1))
            done = done.astype(BF)
            for number, out in enumerate((low, high)):
                part = slice(number * tokens // 2, (number + 1) * tokens // 2)
                out[:, :width] = done[part]
                out[:, width:] = x_ref[part, hidden:]

    return kernel_call(
        kernel,
        [jax.ShapeDtypeStruct((tokens // 2, width + 128), BF)] * 2,
        [SMEM, VMEM] + [ANY] * len(w_parts),
        [VMEM] * 2,
        (2 * tokens * hidden * width, 2 * hidden * width),
        limit=12,
        scratch_shapes=[
            pltpu.VMEM((width, hidden), BF),
            pltpu.VMEM((tokens, width), F32),
            pltpu.SemaphoreType.DMA((len(pieces),)),
        ],
    )(place, grad_pre, *w_parts)


def joined_sums(block):
    return block + pltpu.roll(block, 124, 1)


def core_sum(low, arrived):
    quarter, wide = low.shape
    width = wide - 128
    rows = quarter // 4

    def kernel(low_ref, arrived_ref, mine, *ready):
        for k in range(4):
            part = slice(k * rows, (k + 1) * rows)
            total = low_ref[part, :width].astype(F32) + arrived_ref[part, :width].astype(F32)
            sums = joined_sums(low_ref[part, width:].astype(F32))
            sums = sums + joined_sums(arrived_ref[part, width:].astype(F32))
            if k == 0:
                mine[:, :width] = total
                mine[:, width:] = sums
            else:
                ready[k - 1][:, :width] = total.astype(BF)
                top, rest = two_terms(sums)
                lane = lax.broadcasted_iota(jnp.int32, (rows, 128), 1)
                ready[k - 1][:, width:] = jnp.where(lane < 4, top, pltpu.roll(rest, 4, 1)).astype(BF)

    return kernel_call(
        kernel,
        [jax.ShapeDtypeStruct((rows, wide), F32)] + [jax.ShapeDtypeStruct((rows, wide), BF)] * 3,
        [VMEM] * 2,
        [VMEM] * 4,
        (2 * quarter * wide, 8 * quarter * wide),
    )(low, arrived)


def norm_back(mine, arrived, grad_out, stream, stats, tail=None):
    rows, wide = mine.shape
    width = wide - 128
    extra = () if tail is None else tail

    def kernel(mine_ref, one, two, three, grad_ref, stream_ref, stats_ref, *refs):
        out = refs[-1]

        def fill():
            total = mine_ref[:, :width]
            sums = mine_ref[:, width:]
            for ref in (one, two, three):
                total = total + ref[:, :width].astype(F32)
                sums = sums + joined_sums(ref[:, width:].astype(F32))
            stats = joined_sums(stats_ref[...].astype(F32))
            mean, inv = stats[:, 0:1], stats[:, 1:2]
            centred = (stream_ref[...].astype(F32) - mean) * inv
            grad = total - sums[:, 2:3] / D - centred * (sums[:, 3:4] / D)
            out[...] = (grad_ref[...].astype(F32) + inv * grad).astype(BF)

        if tail is None:
            fill()
            return
        place_ref, order_ref, whole_ref = refs[:3]
        pl.when(place_ref[0] == 0)(fill)

        @pl.when(place_ref[0] == 1)
        def _():
            chosen = dot(order_ref[...], whole_ref[...])
            turned = pltpu.roll(chosen, width // 2, 1)
            lane = lax.broadcasted_iota(jnp.int32, (rows, width), 1)
            own = place_ref[1] == 0
            left = jnp.where(own, chosen[:rows], turned[:rows])
            right = jnp.where(own, turned[rows:], chosen[rows:])
            out[...] = jnp.where(lane < width // 2, left, right).astype(BF)

    specs = [VMEM] * 7 + ([SMEM, VMEM, VMEM] if extra else [])
    return kernel_call(
        kernel,
        jax.ShapeDtypeStruct((rows, width), BF),
        specs,
        VMEM,
        (20 * rows * wide, 20 * rows * wide),
    )(mine, *arrived, grad_out, stream, stats, *extra)


def scatter_tensor(low, high):
    mine, *ready = core_sum(low, send(high, other_core))
    return mine, [send(block, along_z(-k)) for k, block in zip((1, 2, 3), ready)]


def split_planes(w, pick, sizes):
    height, width = w.shape
    part = height // 2
    block = pick.shape[0]
    sub = block // 2

    def kernel(w_ref, pick_ref, kept, *refs):
        away, (held, planes, sems, out_sem) = refs[: len(sizes)], refs[len(sizes) :]
        steps = height // block
        copies = [
            pltpu.make_async_copy(
                w_ref.at[pl.ds(at * block, block)], held.at[pl.ds(at * block, block)], sems.at[at]
            )
            for at in range(steps)
        ]
        for copy in copies:
            copy.start()
        for at, copy in enumerate(copies):
            copy.wait()
            rows = dot(pick_ref[...], held[at * block : (at + 1) * block, :]).astype(BF)
            planes[0, at * sub : (at + 1) * sub, :] = rows[:sub]
            planes[1, at * sub : (at + 1) * sub, :] = rows[sub:]
        outs = [pltpu.make_async_copy(planes.at[0], kept, out_sem.at[0])]
        row = 0
        for number, (size, ref) in enumerate(zip(sizes, away)):
            outs.append(
                pltpu.make_async_copy(planes.at[1, pl.ds(row, size)], ref, out_sem.at[number + 1])
            )
            row += size
        for copy in outs:
            copy.start()
        for copy in outs:
            copy.wait()

    shapes = [jax.ShapeDtypeStruct((size, width), BF) for size in (part, *sizes)]
    return kernel_call(
        kernel,
        shapes,
        [ANY, VMEM],
        [ANY] * (1 + len(sizes)),
        (2 * height * width * block, 4 * height * width),
        limit=13,
        scratch_shapes=[
            pltpu.VMEM((height, width), BF),
            pltpu.VMEM((2, part, width), BF),
            pltpu.SemaphoreType.DMA((height // block,)),
            pltpu.SemaphoreType.DMA((1 + len(sizes),)),
        ],
    )(w, pick)


def cot_spread(padded, w_out, half):
    _, tokens, width = padded.shape
    height = w_out.shape[0] // 2

    def kernel(half_ref, x_ref, w_ref, out):
        for q in (0, 1):
            made = dot(x_ref[q], w_ref[...], ((1,), (1,)))
            out[0, :, q * height : (q + 1) * height] = made.astype(BF)

    return pl.pallas_call(
        kernel,
        out_shape=jax.ShapeDtypeStruct((2, tokens, 2 * height), BF),
        grid_spec=pltpu.PrefetchScalarGridSpec(
            num_scalar_prefetch=1,
            grid=(2,),
            in_specs=[
                pl.BlockSpec((2, tokens, width), lambda i, half_ref: (0, 0, 0)),
                pl.BlockSpec((height, width), lambda i, half_ref: (half_ref[0] ^ i, 0)),
            ],
            out_specs=pl.BlockSpec((1, tokens, 2 * height), lambda i, half_ref: (i, 0, 0)),
        ),
        compiler_params=pltpu.CompilerParams(vmem_limit_bytes=14 * MIB),
    )(half.reshape(1), padded, w_out)


def fill_rows(out, buf, sems, tiles):
    copies = []
    for number, (row, make) in enumerate(tiles):
        slot = number % 2
        if number >= 2:
            copies[number - 2].wait()
        buf[slot] = make().astype(BF)
        copy = pltpu.make_async_copy(
            buf.at[slot], out.at[pl.ds(row, buf.shape[1])], sems.at[slot]
        )
        copy.start()
        copies.append(copy)
    for copy in copies[-2:]:
        copy.wait()


def products_early(place, acted, grad_all, pair, other, grad_pre, theirs):
    tokens, hidden = acted.shape
    width = grad_all.shape[1]
    part = width // 2
    quarter = tokens // 2

    def kernel(
        place_ref, acted_ref, grad_ref, pair_ref, other_ref, pre_ref, theirs_ref,
        out_ref, in_ref, lefts, out_buf, in_buf, out_sems, in_sems,
    ):
        @pl.when(place_ref[0] == 0)
        def _():
            tile = out_buf.shape[1]

            def make(at):
                return lambda: dot(acted_ref[:, at : at + tile], grad_ref[...], ((0,), (0,)))

            fill_rows(
                out_ref, out_buf, out_sems, [(at, make(at)) for at in range(0, hidden, tile)]
            )

        @pl.when(place_ref[0] == 1)
        def _():
            half = place_ref[1]
            row = lax.broadcasted_iota(jnp.int32, (128, 256), 0)
            lane = lax.broadcasted_iota(jnp.int32, (128, 256), 1)
            picks = [
                jnp.where(lane == 2 * row + plane, 1.0, 0.0).astype(BF)
                for plane in (half, 1 - half)
            ]
            for e, ref in enumerate((pair_ref, other_ref)):
                rows = slice(e * quarter, (e + 1) * quarter)
                stats = joined_sums(pre_ref[rows, hidden:].astype(F32))
                normed = (ref[...].astype(F32) - stats[:, 0:1]) * stats[:, 1:2]
                normed = jnp.where(half == 0, normed, pltpu.roll(normed, part, 1)).astype(BF)
                for b in range(-(-part // 128)):
                    end = min(256 * (b + 1), width)
                    for number, pick in enumerate(picks):
                        made = dot(normed[:, 128 * b : 128 * (b + 1)], pick).astype(BF)
                        made = made[:, : end - 256 * b]
                        if number == 0:
                            lefts[0, rows, 256 * b : end] = made
                        else:
                            mid, at = quarter // 2, e * quarter
                            lefts[1, at + mid : at + quarter, 256 * b : end] = made[:mid]
                            lefts[1, at : at + mid, 256 * b : end] = made[mid:]
            tile = in_buf.shape[1]

            def make(at):
                def both():
                    mine = dot(lefts[0, :, at : at + tile], pre_ref[:, :hidden], ((0,), (0,)))
                    return mine + dot(lefts[1, :, at : at + tile], theirs_ref[...], ((0,), (0,)))

                return both

            fill_rows(in_ref, in_buf, in_sems, [(at, make(at)) for at in range(0, width, tile)])

    return kernel_call(
        kernel,
        [
            jax.ShapeDtypeStruct((hidden, width), BF),
            jax.ShapeDtypeStruct((width, hidden), BF),
        ],
        [SMEM] + [VMEM] * 6,
        [ANY] * 2,
        (2 * tokens * hidden * width, 2 * hidden * width),
        limit=20,
        scratch_shapes=[
            pltpu.VMEM((2, tokens, width), BF),
            pltpu.VMEM((2, hidden // 3, width), BF),
            pltpu.VMEM((2, width // 3, hidden), BF),
            pltpu.SemaphoreType.DMA((2,)),
            pltpu.SemaphoreType.DMA((2,)),
        ],
    )(place, acted, grad_all, pair, other, grad_pre, theirs)


def products_late(place, out_grad, in_grad, lead, blocks, mine, padded):
    tokens, width = lead.shape
    hidden = mine.shape[1]
    plane = hidden // 2

    def kernel(
        place_ref, out_was, in_was, lead_ref, blocks_ref, mine_ref, padded_ref,
        out_ref, in_ref, out_buf, in_buf, out_sems, in_sems,
    ):
        @pl.when(place_ref[0] == 0)
        def _():
            tile = in_buf.shape[1]

            def make(at):
                return lambda: dot(
                    lead_ref[:, at : at + tile], blocks_ref[:, :hidden], ((0,), (0,))
                )

            fill_rows(in_ref, in_buf, in_sems, [(at, make(at)) for at in range(0, width, tile)])

        @pl.when(place_ref[0] == 1)
        def _():
            tile = out_buf.shape[1]

            def make(ref, at):
                def both():
                    low = dot(ref[:, at : at + tile], padded_ref[0], ((0,), (0,)))
                    rest = dot(ref[:, plane + at : plane + at + tile], padded_ref[1], ((0,), (0,)))
                    return low + rest

                return both

            tiles = []
            for number, ref in enumerate((mine_ref, blocks_ref)):
                base = (place_ref[1] ^ number) * plane
                tiles += [
                    (pl.multiple_of(base + at, 16), make(ref, at)) for at in range(0, plane, tile)
                ]
            fill_rows(out_ref, out_buf, out_sems, tiles)

    return kernel_call(
        kernel,
        [
            jax.ShapeDtypeStruct((hidden, width), BF),
            jax.ShapeDtypeStruct((width, hidden), BF),
        ],
        [SMEM, ANY, ANY] + [VMEM] * 4,
        [ANY] * 2,
        (2 * tokens * hidden * width, 2 * hidden * width),
        limit=20,
        input_output_aliases={1: 0, 2: 1},
        scratch_shapes=[
            pltpu.VMEM((2, plane // 3, width), BF),
            pltpu.VMEM((2, width // 3, hidden), BF),
            pltpu.SemaphoreType.DMA((2,)),
            pltpu.SemaphoreType.DMA((2,)),
        ],
    )(place, out_grad, in_grad, lead, blocks, mine, padded)


def halves(values):
    top = lax.reduce_precision(values, 8, 7)
    return top.astype(BF), (values - top).astype(BF)


def pack(*columns):
    top, rest = halves(jnp.stack(columns, axis=1))
    both = jnp.concatenate([top, rest], axis=1)
    return jnp.pad(both, ((0, 0), (0, 128 - both.shape[1])))


def stack_rows(blocks):
    rows, width = blocks[0].shape

    def kernel(*refs):
        for number, ref in enumerate(refs[:-1]):
            refs[-1][number * rows : (number + 1) * rows, :] = ref[...]

    count = len(blocks)
    return kernel_call(
        kernel,
        jax.ShapeDtypeStruct((count * rows, width), BF),
        [VMEM] * count,
        VMEM,
        (0, 4 * count * rows * width),
    )(*blocks)


def gather_pairs(x):
    pair = stack_rows([x] + [send(x, along_z(k)) for k in (1, 2, 3)])
    return pair, send(pair, other_core)


def gather_tensor(x):
    return stack_rows(gather_pairs(x))


def swap_dp(blocks):
    return lax.all_to_all(blocks, "dp", 0, 0, tiled=True)


def sum_dp(value):
    total = value
    for k in (1, 2, 3):
        total = total + send(value, along_x(k))
    return total + send(total, other_y)


def one_hot(condition):
    return condition.astype(BF)


def after(value, *others):
    return lax.optimization_barrier((value, *others))[0]


def body(inputs, cotangent, w_first, w_second):
    w_in, w_out = w_first[0], w_second[0]
    rows, width = inputs.shape
    hidden = w_in.shape[1]
    part = width // 2
    tokens = 8 * rows
    first = lax.axis_index("section") == 0
    at = lax.axis_index("tensor")
    z_at, core_at = at // 2, at % 2
    half = at // 4

    slot_row = jnp.arange(tokens)
    slot_owner = ((z_at - slot_row // rows % 4) % 4) * 2 + (core_at ^ (slot_row // (4 * rows)))
    slot_token = slot_owner * rows + slot_row % rows

    place = jnp.stack([lax.axis_index("section"), half]).astype(jnp.int32)
    place_rows = jnp.arange(2 * rows)
    stored_token = (at % 4) * 2 * rows + 2 * (place_rows % rows) + place_rows // rows
    stored_order = one_hot(stored_token[:, None] == slot_token[None, :])

    block = 96
    index = jnp.arange(block)
    picked = 2 * (index % (block // 2)) + jnp.where(index < block // 2, half, 1 - half)
    pick = one_hot(index[None, :] == picked[:, None])
    sizes = [part // 6, part // 3, part // 3, part // 6]
    kept, *away = lax.cond(
        first,
        lambda: [blank(size, hidden) for size in (part, *sizes)],
        lambda: list(split_planes(w_in, pick, sizes)),
    )

    values = inputs.astype(F32)
    both = sum_dp(jnp.stack([jnp.sum(values, axis=1), jnp.sum(values * values, axis=1)]))
    mean_row = both[0] / D
    inv_first = lax.rsqrt(both[1] / D - mean_row * mean_row + EPSILON)
    normed_own = ((values - mean_row[:, None]) * inv_first[:, None]).astype(BF)
    none = jnp.zeros_like(mean_row)
    first_stats = pack(mean_row, inv_first, none, none)
    lead = gather_tensor(after(jnp.where(first, normed_own, cotangent), *away))
    came = [send(after(away[0], lead), other_half, LATER)]

    def lead_second():
        blocks = lead.reshape(2, 4, rows, 2, part)
        k_near = jnp.where(z_at % 2 == 0, 3, 1)
        near = lax.dynamic_index_in_dim(blocks, k_near, 1, keepdims=True)
        far = lax.dynamic_index_in_dim(blocks, 4 - k_near, 1, keepdims=True)
        mine = jnp.concatenate([blocks[:, :1], near], axis=1)
        rest = jnp.concatenate([blocks[:, 2:3], far], axis=1)

        def flat(group):
            return group.transpose(0, 1, 3, 2, 4).reshape(tokens, part)

        row = jnp.arange(tokens)
        e, j = row // (4 * rows), row // (2 * rows) % 2
        q, r = row // rows % 2, row % rows
        c_block = (z_at % 2 ^ j) * 2 + (core_at ^ e)
        token = c_block * 2 * rows + 2 * r + q
        order = one_hot(slot_token[:, None] == token[None, :])
        own = dot(order, flat(mine)).astype(BF)
        other = dot(order[:rows], flat(rest)).astype(BF)
        blanks = jnp.zeros_like(own)
        padded = jnp.stack(
            [jnp.concatenate([own, blanks], axis=1), jnp.concatenate([blanks, own], axis=1)]
        )
        spread = cot_spread(padded, w_out, half)
        cot_own = jnp.where(
            half == 0,
            jnp.concatenate([own[:rows], other], axis=1),
            jnp.concatenate([other, own[:rows]], axis=1),
        )
        return spread[0], spread[1], padded, cot_own

    def lead_first():
        made = weight_dot(lead, w_in)
        return made, blank(tokens, hidden), blank(2, tokens, width), blank(rows, width)

    part_a, part_b, cot_padded, cot_own = lax.cond(first, lead_first, lead_second)
    swapped = swap_dp(after(part_a, came[0]).reshape(8, rows, hidden))
    sum_a, ready = spread_first(place, swapped, part_b.reshape(8, rows, hidden))
    came.append(send(after(away[1], part_a), other_half, LATER))
    blocks = swap_dp(after(ready, came[1]))
    came.append(send(after(away[2], sum_a), other_half, LATER))
    acted_first = blocks.reshape(tokens, hidden)
    low, high, sum_b = branch_first(place, after(blocks, came[2]), w_out)
    came.append(send(after(away[3], blocks), other_half, LATER))
    w_parts = [kept, *came]
    branch = low.astype(F32) + send(high, other_core).astype(F32)
    stream = values
    for k in range(4):
        arrived = send(branch[k * rows : (k + 1) * rows].astype(BF), across_z(-k))
        stream = stream + arrived.astype(F32)
    stream_own = stream.astype(BF)
    grad_theirs = send(sum_b, other_half_row, LATER)

    pair, other = gather_pairs(stream_own)
    blocks = swap_dp(pre_later_part(place, pair, other, w_in, w_parts))
    ready, acted_mine, columns = grad_pre_later(blocks, sum_a, grad_theirs, width)
    grad_pre = swap_dp(ready).reshape(tokens, hidden + 128)
    mine, arrived = scatter_tensor(*back_part(place, 1, grad_pre, w_parts))
    later_grad = norm_back(mine, arrived, cot_own, stream_own, grad_pre[:rows, hidden:])
    acted_theirs = send(acted_mine, other_half_row, LATER)
    grad_pre_theirs = send(grad_pre[:, :hidden], other_half, LATER)

    returned = send(later_grad, other_section)
    own_grad = jnp.where(first, returned, later_grad)
    grad_all = gather_tensor(own_grad)
    blocks = swap_dp(grad_spread(place, grad_all, w_out, acted_mine))
    acted_mine_all = blocks.reshape(tokens, hidden)
    ready = grad_pre_first(place, blocks, sum_a, columns, acted_theirs)
    blocks = swap_dp(ready).reshape(tokens, hidden + 128)
    out_grad, in_grad = products_early(
        place, acted_first, grad_all, pair, other, grad_pre, grad_pre_theirs
    )
    mine, arrived = scatter_tensor(*back_part(place, 0, blocks, [w_in]))
    out_grad, in_grad = products_late(
        place, out_grad, in_grad, lead, blocks, acted_mine_all, cot_padded
    )
    result = norm_back(
        mine, arrived, own_grad, inputs, first_stats, (place, stored_order, grad_all)
    )
    return (result[None], in_grad[None], out_grad[None])


def solution(mesh):
    return jax.shard_map(
        body,
        mesh=mesh,
        in_specs=(
            P("tensor", "dp"),
            P("tensor", "dp"),
            P("section", "dp", "tensor"),
            P("section", "tensor", "dp"),
        ),
        out_specs=(
            P("section", "tensor", "dp"),
            P("section", "dp", "tensor"),
            P("section", "tensor", "dp"),
        ),
        check_vma=False,
    )
```

```python
import jax
import jax.numpy as jnp
from jax import lax
from jax.experimental import pallas as pl
from jax.experimental.layout import Layout, with_layout_constraint
from jax.experimental.pallas import tpu as pltpu
from jax.sharding import PartitionSpec as P

D = 9216
EPSILON = 1e-05
AXES = ("section", "dp", "tensor")
BF = jnp.bfloat16
F32 = jnp.float32
LATER = (1,)
BOTH = (0, 1)
MIB = 2**20


def by_rows(value):
    return with_layout_constraint(value, Layout(major_to_minor=tuple(range(value.ndim))))


def send(value, move, sections=BOTH):
    pairs = []
    for s in sections:
        for d in range(8):
            for t in range(8):
                s2, d2, t2 = move(s, d, t)
                pairs.append(((s * 8 + d) * 8 + t, (s2 * 8 + d2) * 8 + t2))
    return by_rows(lax.ppermute(by_rows(value), AXES, pairs))


def along_x(k):
    return lambda s, d, t: (s, d // 4 * 4 + (d + k) % 4, t)


def along_z(k):
    return lambda s, d, t: (s, d, (t + 2 * k) % 8)


def across_z(k):
    return lambda s, d, t: (1 - s, d, (t + 2 * k) % 8)


def other_y(s, d, t):
    return (s, d ^ 4, t)


def other_core(s, d, t):
    return (s, d, t ^ 1)


def other_half(s, d, t):
    return (s, d, t ^ 4)


def other_half_row(s, d, t):
    return (s, d // 4 * 4 + (d + 2) % 4, t ^ 4)


def other_section(s, d, t):
    return (1 - s, d, t)


def dot(left, right, dims=((1,), (0,))):
    return lax.dot_general(left, right, (dims, ((), ())), preferred_element_type=F32)


VMEM = pl.BlockSpec(memory_space=pltpu.VMEM)
ANY = pl.BlockSpec(memory_space=pl.ANY)
SMEM = pl.BlockSpec(memory_space=pltpu.SMEM)


def kernel_call(kernel, out_shape, in_specs, out_specs, work, limit=4, **more):
    flops, moved = work
    return pl.pallas_call(
        kernel,
        out_shape=out_shape,
        in_specs=in_specs,
        out_specs=out_specs,
        compiler_params=pltpu.CompilerParams(vmem_limit_bytes=limit * MIB),
        cost_estimate=pl.CostEstimate(flops=flops, bytes_accessed=moved, transcendentals=0),
        **more,
    )


def blank(*shape):
    return kernel_call(lambda out: None, jax.ShapeDtypeStruct(shape, BF), [], ANY, (0, 0))()


def stream_plan(parts, turned):
    rows = sum(part.shape[0] for part in parts)
    cols = parts[0].shape[1]
    width = rows if turned else cols
    ends = [width // 9, width // 3, 2 * width // 3, width]
    chunks = list(zip([0] + ends[:-1], ends))
    pieces = []
    for number, (at, end) in enumerate(chunks):
        row = 0
        for index, part in enumerate(parts):
            low, high = row, row + part.shape[0]
            row = high
            if turned:
                low, high = max(at, low), min(end, high)
            if low < high:
                pieces.append((number, index, low, high))
    return rows, cols, chunks, pieces, turned


def stream_copies(plan, parts, held, sems, turn=0):
    rows, cols, chunks, pieces, turned = plan
    first_rows = [0]
    for part in parts:
        first_rows.append(first_rows[-1] + part.shape[0])
    copies = []
    for sem, (number, index, low, high) in enumerate(pieces):
        at, end = (0, cols) if turned else chunks[number]
        begin = first_rows[index]
        to = low if isinstance(turn, int) else pl.multiple_of(lax.rem(low + turn, rows), 16)
        copy = pltpu.make_async_copy(
            parts[index].at[pl.ds(low - begin, high - low), pl.ds(at, end - at)],
            held.at[pl.ds(to, high - low), pl.ds(at, end - at)],
            sems.at[sem],
        )
        copies.append((number, copy))
    return copies


def grad_spread(place, x, w, own):
    plan = stream_plan([w], True)
    rows, cols, chunks, pieces, _ = plan
    tokens = x.shape[0]
    part = tokens // 8

    def kernel(place_ref, x_ref, w_ref, own_ref, out, held, buf, sems, out_sems):
        @pl.when(place_ref[0] == 0)
        def _():
            copies = stream_copies(plan, [w_ref], held, sems)
            for _, copy in copies:
                copy.start()
            left = x_ref[...]
            outs = []
            for number, (at, end) in enumerate(chunks):
                copies[number][1].wait()
                made = dot(left, held[at:end, :], ((1,), (1,))).astype(BF)
                buf[:, :, at:end] = made.reshape(8, part, end - at)
                lanes = pl.ds(at, end - at)
                copy = pltpu.make_async_copy(
                    buf.at[:, :, lanes], out.at[:, :, lanes], out_sems.at[number]
                )
                copy.start()
                outs.append(copy)
            for copy in outs:
                copy.wait()

        @pl.when(place_ref[0] == 1)
        def _():
            outs = [
                pltpu.make_async_copy(own_ref, out.at[j], out_sems.at[j]) for j in range(8)
            ]
            for copy in outs:
                copy.start()
            for copy in outs:
                copy.wait()

    return kernel_call(
        kernel,
        jax.ShapeDtypeStruct((8, part, rows), BF),
        [SMEM, VMEM, ANY, VMEM],
        ANY,
        (2 * tokens * rows * cols, 2 * (rows * cols + tokens * (rows + cols))),
        limit=10,
        scratch_shapes=[
            pltpu.VMEM((rows, cols), BF),
            pltpu.VMEM((8, part, rows), BF),
            pltpu.SemaphoreType.DMA((len(pieces),)),
            pltpu.SemaphoreType.DMA((8,)),
        ],
    )(place, x, w, own)


ROOT = 0.7978845608028654
CUBE = 0.044715


def gelu_parts(v):
    bent = jnp.tanh(ROOT * (v + CUBE * v * v * v))
    slope = 0.5 * (1.0 + bent) + 0.5 * v * (1.0 - bent * bent) * ROOT * (1.0 + 3.0 * CUBE * v * v)
    return 0.5 * v * (1.0 + bent), slope


def two_terms(value):
    top = value.astype(BF).astype(F32)
    return top, value - top


def lane_pack(columns):
    rows = columns[0].shape[0]
    lane = lax.broadcasted_iota(jnp.int32, (rows, 128), 1)
    block = jnp.zeros((rows, 128), F32)
    for number, column in enumerate(columns):
        block = jnp.where(lane == number, column, block)
    return block


def sums_pack(mean, inv, one, two):
    pairs = [two_terms(c) for c in (mean, inv, one, two)]
    return lane_pack([p[0] for p in pairs] + [p[1] for p in pairs]).astype(BF)


def stats_row(columns, rows):
    row = lax.broadcasted_iota(jnp.int32, (rows, 128), 0)
    lane = lax.broadcasted_iota(jnp.int32, (rows, 128), 1)
    block = jnp.zeros((rows, 128), F32)
    for number, column in enumerate(columns):
        block = jnp.where(lane == number * rows + row, column, block)
    return jnp.sum(block, axis=0, keepdims=True)


def norm_stats(beside, width, at):
    rows = beside.shape[1]
    row = lax.broadcasted_iota(jnp.int32, (rows, 128), 0)
    lane = lax.broadcasted_iota(jnp.int32, (rows, 128), 1)
    group = lane // rows

    def column(d, low, high):
        mask = (lane % rows == row) & (group >= low) & (group < high)
        line = jnp.broadcast_to(beside[d, at : at + 1, :], (rows, 128))
        return jnp.sum(jnp.where(mask, line, 0.0), axis=1, keepdims=True)

    shifts = [column(d, 0, 1) for d in range(8)]
    means = [column(d, 0, 2) for d in range(8)]
    mean = sum(means) / 8
    square = sum(column(d, 2, 4) + width * (means[d] - mean) ** 2 for d in range(8))
    inv = lax.rsqrt(square / D + EPSILON)
    return mean, inv, [shift - mean for shift in shifts]


def norm_sum(blocks_ref, beside, moves, inv, g):
    rows = beside.shape[1]
    lanes = slice(g * 128, (g + 1) * 128)
    pre = jnp.zeros((rows, 128), F32)
    columns = jnp.zeros((1, 128), F32)
    for d in range(8):
        column = beside[d, g : g + 1, :]
        columns = columns + column
        pre = pre + blocks_ref[d, :, lanes].astype(F32) + moves[d] * column
    return pre * inv, columns


def send_all(block, ready, sems):
    copies = [pltpu.make_async_copy(block, ready.at[j], sems.at[j]) for j in range(8)]
    for copy in copies:
        copy.start()
    for copy in copies:
        copy.wait()


def spread_first(place, swapped, part_b, width):
    _, rows, wide = swapped.shape
    hidden = wide - 128

    def kernel(place_ref, swapped_ref, part_ref, total_ref, ready_ref, columns_ref, held, sems):
        @pl.when(place_ref[0] == 0)
        def _():
            beside = swapped_ref[:, :, hidden:].astype(F32)
            mean, inv, moves = norm_stats(beside, width, hidden // 128)
            for g in range(hidden // 128):
                lanes = slice(g * 128, (g + 1) * 128)
                pre, columns = norm_sum(swapped_ref, beside, moves, inv, g)
                total_ref[:, lanes] = pre
                columns_ref[:, lanes] = jnp.broadcast_to(columns, (8, 128))
                held[:, lanes] = gelu_parts(pre)[0].astype(BF)
            held[:, hidden:] = sums_pack(mean, inv, mean, mean)
            send_all(held, ready_ref, sems)

        @pl.when(place_ref[0] == 1)
        def _():
            for g in range(hidden // 128):
                lanes = slice(g * 128, (g + 1) * 128)
                total = swapped_ref[0, :, lanes].astype(F32)
                for j in range(1, 8):
                    total = total + swapped_ref[j, :, lanes].astype(F32)
                total_ref[:, lanes] = total

    return kernel_call(
        kernel,
        [
            jax.ShapeDtypeStruct((rows, hidden), F32),
            jax.ShapeDtypeStruct((8, rows, hidden + 128), BF),
            jax.ShapeDtypeStruct((8, hidden), F32),
        ],
        [SMEM, VMEM, ANY],
        [VMEM, ANY, VMEM],
        (30 * rows * hidden, 40 * rows * hidden),
        input_output_aliases={2: 1},
        scratch_shapes=[
            pltpu.VMEM((rows, hidden + 128), BF),
            pltpu.SemaphoreType.DMA((8,)),
        ],
    )(place, swapped, part_b)


def branch_first(place, blocks, w_out):
    _, rows, wide = blocks.shape
    hidden = w_out.shape[0]
    tokens = 8 * rows
    plan = stream_plan([w_out], False)
    _, width, chunks, pieces, _ = plan

    def kernel(place_ref, x_ref, w_ref, low, high, total_ref, held, sems):
        @pl.when(place_ref[0] == 0)
        def _():
            copies = stream_copies(plan, [w_ref], held, sems)
            for _, copy in copies:
                copy.start()
            left = x_ref[:, :, :hidden].reshape(tokens, hidden)
            for number, (at, end) in enumerate(chunks):
                copies[number][1].wait()
                made = dot(left, held[:, at:end]).astype(BF)
                low[:, at:end] = made[: tokens // 2]
                high[:, at:end] = made[tokens // 2 :]

        @pl.when(place_ref[0] == 1)
        def _():
            for g in range(hidden // 128):
                lanes = slice(g * 128, (g + 1) * 128)
                total = x_ref[0, :, lanes].astype(F32)
                for j in range(1, 8):
                    total = total + x_ref[j, :, lanes].astype(F32)
                total_ref[:, lanes] = total.astype(BF)

    return kernel_call(
        kernel,
        [
            jax.ShapeDtypeStruct((tokens // 2, width), BF),
            jax.ShapeDtypeStruct((tokens // 2, width), BF),
            jax.ShapeDtypeStruct((rows, hidden), BF),
        ],
        [SMEM, VMEM, ANY],
        [VMEM] * 3,
        (2 * tokens * hidden * width, 2 * hidden * width),
        limit=9,
        scratch_shapes=[
            pltpu.VMEM((hidden, width), BF),
            pltpu.SemaphoreType.DMA((len(pieces),)),
        ],
    )(place, blocks, w_out)


def pre_part(place, section, pair, other, w_parts):
    quarter, width = pair.shape
    tokens = 2 * quarter
    rows = tokens // 8
    plan = stream_plan(w_parts, False)
    _, hidden, chunks, pieces, _ = plan

    def kernel(place_ref, pair_ref, other_ref, *refs):
        part_refs, (out, held, left, buf, sems, out_sems) = refs[: len(w_parts)], refs[len(w_parts) :]

        @pl.when(place_ref[0] == section)
        def _():
            turn = place_ref[1] * (width // 2) if section == 1 else 0
            copies = stream_copies(plan, part_refs, held, sems, turn)
            for _, copy in copies:
                copy.start()
            lines = []
            for e, ref in enumerate((pair_ref, other_ref)):
                spread = ref[...].astype(F32)
                mean = jnp.sum(spread, axis=1, keepdims=True) / width
                off = spread - mean
                square = jnp.sum(off * off, axis=1, keepdims=True)
                shift = mean.astype(BF).astype(F32)
                left[e * quarter : (e + 1) * quarter, :] = (spread - shift).astype(BF)
                columns = [*two_terms(mean), *two_terms(square)]
                for k in range(4):
                    part = slice(k * rows, (k + 1) * rows)
                    lines.append(stats_row([column[part] for column in columns], rows))
            left[tokens:, :] = jnp.ones((16, width), BF)
            tops, outs = [], []

            def leave(at, end):
                lanes = pl.ds(at, end - at)
                copy = pltpu.make_async_copy(
                    buf.at[:, :, lanes], out.at[:, :, lanes], out_sems.at[len(outs)]
                )
                copy.start()
                outs.append(copy)

            for number, (at, end) in enumerate(chunks):
                for begun, copy in copies:
                    if begun == number:
                        copy.wait()
                made = dot(left[...], held[:, at:end])
                buf[:, :, at:end] = made[:tokens].astype(BF).reshape(8, rows, end - at)
                leave(at, end)
                sums = made[tokens : tokens + 1]
                for g in range((end - at) // 128):
                    tops.append(sums[:, g * 128 : (g + 1) * 128])
            empty = jnp.zeros((rows - len(tops) - 1, 128), F32)
            for j in range(8):
                block = jnp.concatenate([*tops, lines[j], empty], axis=0)
                buf[j, :, hidden:] = block.astype(BF)
            leave(hidden, hidden + 128)
            for copy in outs:
                copy.wait()

    return kernel_call(
        kernel,
        jax.ShapeDtypeStruct((8, rows, hidden + 128), BF),
        [SMEM, VMEM, VMEM] + [ANY] * len(w_parts),
        ANY,
        (2 * tokens * hidden * width, 2 * hidden * width),
        limit=14,
        scratch_shapes=[
            pltpu.VMEM((width, hidden), BF),
            pltpu.VMEM((tokens + 16, width), BF),
            pltpu.VMEM((8, rows, hidden + 128), BF),
            pltpu.SemaphoreType.DMA((len(pieces),)),
            pltpu.SemaphoreType.DMA((len(chunks) + 1,)),
        ],
    )(place, pair, other, *w_parts)


def weave(turned):
    row = lax.broadcasted_iota(jnp.int32, (256, 256), 0)
    lane = lax.broadcasted_iota(jnp.int32, (256, 256), 1)
    if turned:
        row, lane = lane, row
    return jnp.where(lane == 2 * (row % 128) + row // 128, 1.0, 0.0).astype(BF)


def grad_pre_later(blocks, grad_mine, grad_theirs, width):
    _, rows, wide = blocks.shape
    hidden = wide - 128
    plane = hidden // 2

    def kernel(blocks_ref, mine_ref, theirs_ref, ready, acted_ref, grad_ref, held_ref, own, sems):
        order, back = weave(False), weave(True)
        for b in range(hidden // 256):
            pair = []
            for q in (0, 1):
                lanes = slice(q * plane + b * 128, q * plane + (b + 1) * 128)
                pair.append(mine_ref[:, lanes] + theirs_ref[:, lanes].astype(F32))
            top, rest = two_terms(jnp.concatenate(pair, axis=1))
            done = dot(top.astype(BF), order) + dot(rest.astype(BF), order)
            grad_ref[:, b * 256 : (b + 1) * 256] = done
        beside = blocks_ref[:, :, hidden:].astype(F32)
        mean, inv, moves = norm_stats(beside, width, hidden // 128)
        one = jnp.zeros((rows, 1), F32)
        two = jnp.zeros((rows, 1), F32)
        for g in range(hidden // 128):
            lanes = slice(g * 128, (g + 1) * 128)
            pre, columns = norm_sum(blocks_ref, beside, moves, inv, g)
            acted, slope = gelu_parts(pre)
            held_ref[:, lanes] = acted.astype(BF)
            grad = (grad_ref[:, lanes] * slope).astype(BF)
            own[:, lanes] = grad
            grad = grad.astype(F32)
            one = one + jnp.sum(grad * columns, axis=1, keepdims=True)
            two = two + jnp.sum(grad * pre, axis=1, keepdims=True)
        own[:, hidden:] = sums_pack(mean, inv, one, two)
        send_all(own, ready, sems)
        for b in range(hidden // 256):
            done = dot(held_ref[:, b * 256 : (b + 1) * 256], back).astype(BF)
            acted_ref[:, b * 128 : (b + 1) * 128] = done[:, :128]
            acted_ref[:, plane + b * 128 : plane + (b + 1) * 128] = done[:, 128:]

    return kernel_call(
        kernel,
        [
            jax.ShapeDtypeStruct((8, rows, hidden + 128), BF),
            jax.ShapeDtypeStruct((rows, hidden), BF),
        ],
        [VMEM] * 3,
        [ANY, VMEM],
        (80 * rows * hidden, 40 * rows * hidden),
        scratch_shapes=[
            pltpu.VMEM((rows, hidden), F32),
            pltpu.VMEM((rows, hidden), BF),
            pltpu.VMEM((rows, hidden + 128), BF),
            pltpu.SemaphoreType.DMA((8,)),
        ],
    )(blocks, grad_mine, grad_theirs)


def grad_pre_first(place, blocks, pre, columns, theirs):
    _, rows, hidden = blocks.shape

    def kernel(place_ref, blocks_ref, pre_ref, columns_ref, theirs_ref, ready, own, sems):
        @pl.when(place_ref[0] == 0)
        def _():
            one = jnp.zeros((rows, 1), F32)
            two = jnp.zeros((rows, 1), F32)
            for g in range(hidden // 128):
                lanes = slice(g * 128, (g + 1) * 128)
                total = blocks_ref[0, :, lanes].astype(F32)
                for j in range(1, 8):
                    total = total + blocks_ref[j, :, lanes].astype(F32)
                pre = pre_ref[:, lanes]
                grad = (total * gelu_parts(pre)[1]).astype(BF)
                own[:, lanes] = grad
                grad = grad.astype(F32)
                one = one + jnp.sum(grad * columns_ref[0:1, lanes], axis=1, keepdims=True)
                two = two + jnp.sum(grad * pre, axis=1, keepdims=True)
            own[:, hidden:] = sums_pack(one, one, one, two)

        @pl.when(place_ref[0] == 1)
        def _():
            own[:, :hidden] = theirs_ref[...]
            own[:, hidden:] = jnp.zeros((rows, 128), BF)

        send_all(own, ready, sems)

    return kernel_call(
        kernel,
        jax.ShapeDtypeStruct((8, rows, hidden + 128), BF),
        [SMEM] + [VMEM] * 4,
        ANY,
        (60 * rows * hidden, 40 * rows * hidden),
        scratch_shapes=[
            pltpu.VMEM((rows, hidden + 128), BF),
            pltpu.SemaphoreType.DMA((8,)),
        ],
    )(place, blocks, pre, columns, theirs)


def back_part(place, section, grad_pre, w_parts):
    tokens, wide = grad_pre.shape
    hidden = wide - 128
    plan = stream_plan(w_parts, True)
    width, _, chunks, pieces, _ = plan

    def kernel(place_ref, x_ref, *refs):
        w_refs, (low, high, held, made, sems) = refs[: len(w_parts)], refs[len(w_parts) :]

        @pl.when(place_ref[0] == section)
        def _():
            copies = stream_copies(plan, w_refs, held, sems)
            for _, copy in copies:
                copy.start()
            left = x_ref[:, :hidden]
            for number, (at, end) in enumerate(chunks):
                for begun, copy in copies:
                    if begun == number:
                        copy.wait()
                made[:, at:end] = dot(left, held[at:end, :], ((1,), (1,)))
            done = made[...]
            if section == 1:
                done = jnp.where(place_ref[1] == 0, done, pltpu.roll(done, width // 2, 1))
            done = done.astype(BF)
            for number, out in enumerate((low, high)):
                part = slice(number * tokens // 2, (number + 1) * tokens // 2)
                out[:, :width] = done[part]
                out[:, width:] = x_ref[part, hidden:]

    return kernel_call(
        kernel,
        [jax.ShapeDtypeStruct((tokens // 2, width + 128), BF)] * 2,
        [SMEM, VMEM] + [ANY] * len(w_parts),
        [VMEM] * 2,
        (2 * tokens * hidden * width, 2 * hidden * width),
        limit=12,
        scratch_shapes=[
            pltpu.VMEM((width, hidden), BF),
            pltpu.VMEM((tokens, width), F32),
            pltpu.SemaphoreType.DMA((len(pieces),)),
        ],
    )(place, grad_pre, *w_parts)


def joined_sums(block):
    return block + pltpu.roll(block, 124, 1)


def core_sum(low, arrived):
    quarter, wide = low.shape
    width = wide - 128
    rows = quarter // 4

    def kernel(low_ref, arrived_ref, mine, *ready):
        for k in range(4):
            part = slice(k * rows, (k + 1) * rows)
            total = low_ref[part, :width].astype(F32) + arrived_ref[part, :width].astype(F32)
            sums = joined_sums(low_ref[part, width:].astype(F32))
            sums = sums + joined_sums(arrived_ref[part, width:].astype(F32))
            if k == 0:
                mine[:, :width] = total
                mine[:, width:] = sums
            else:
                ready[k - 1][:, :width] = total.astype(BF)
                top, rest = two_terms(sums)
                lane = lax.broadcasted_iota(jnp.int32, (rows, 128), 1)
                ready[k - 1][:, width:] = jnp.where(lane < 4, top, pltpu.roll(rest, 4, 1)).astype(BF)

    return kernel_call(
        kernel,
        [jax.ShapeDtypeStruct((rows, wide), F32)] + [jax.ShapeDtypeStruct((rows, wide), BF)] * 3,
        [VMEM] * 2,
        [VMEM] * 4,
        (2 * quarter * wide, 8 * quarter * wide),
    )(low, arrived)


def norm_back(mine, arrived, grad_out, stream, stats, tail=None):
    rows, wide = mine.shape
    width = wide - 128
    extra = () if tail is None else tail

    def kernel(mine_ref, one, two, three, grad_ref, stream_ref, stats_ref, *refs):
        out = refs[-1]

        def fill():
            total = mine_ref[:, :width]
            sums = mine_ref[:, width:]
            for ref in (one, two, three):
                total = total + ref[:, :width].astype(F32)
                sums = sums + joined_sums(ref[:, width:].astype(F32))
            stats = joined_sums(stats_ref[...].astype(F32))
            mean, inv = stats[:, 0:1], stats[:, 1:2]
            centred = (stream_ref[...].astype(F32) - mean) * inv
            grad = total - sums[:, 2:3] / D - centred * (sums[:, 3:4] / D)
            out[...] = (grad_ref[...].astype(F32) + inv * grad).astype(BF)

        if tail is None:
            fill()
            return
        place_ref, order_ref, whole_ref = refs[:3]
        pl.when(place_ref[0] == 0)(fill)

        @pl.when(place_ref[0] == 1)
        def _():
            chosen = dot(order_ref[...], whole_ref[...])
            turned = pltpu.roll(chosen, width // 2, 1)
            lane = lax.broadcasted_iota(jnp.int32, (rows, width), 1)
            own = place_ref[1] == 0
            left = jnp.where(own, chosen[:rows], turned[:rows])
            right = jnp.where(own, turned[rows:], chosen[rows:])
            out[...] = jnp.where(lane < width // 2, left, right).astype(BF)

    specs = [VMEM] * 7 + ([SMEM, VMEM, VMEM] if extra else [])
    return kernel_call(
        kernel,
        jax.ShapeDtypeStruct((rows, width), BF),
        specs,
        VMEM,
        (20 * rows * wide, 20 * rows * wide),
    )(mine, *arrived, grad_out, stream, stats, *extra)


def scatter_tensor(low, high):
    mine, *ready = core_sum(low, send(high, other_core))
    return mine, [send(block, along_z(-k)) for k, block in zip((1, 2, 3), ready)]


def split_planes(w, pick, sizes):
    height, width = w.shape
    part = height // 2
    block = pick.shape[0]
    sub = block // 2

    def kernel(w_ref, pick_ref, kept, *refs):
        away, (held, planes, sems, out_sem) = refs[: len(sizes)], refs[len(sizes) :]
        steps = height // block
        copies = [
            pltpu.make_async_copy(
                w_ref.at[pl.ds(at * block, block)], held.at[pl.ds(at * block, block)], sems.at[at]
            )
            for at in range(steps)
        ]
        for copy in copies:
            copy.start()
        outs, piece, begun = [], 0, 0
        for at, copy in enumerate(copies):
            copy.wait()
            rows = dot(pick_ref[...], held[at * block : (at + 1) * block, :]).astype(BF)
            planes[0, at * sub : (at + 1) * sub, :] = rows[:sub]
            planes[1, at * sub : (at + 1) * sub, :] = rows[sub:]
            if (at + 1) * sub == begun + sizes[piece]:
                lines = pl.ds(begun, sizes[piece])
                for plane, ref in enumerate((kept.at[lines], away[piece])):
                    out = pltpu.make_async_copy(
                        planes.at[plane, lines], ref, out_sem.at[2 * piece + plane]
                    )
                    out.start()
                    outs.append(out)
                begun += sizes[piece]
                piece += 1
        for out in outs:
            out.wait()

    shapes = [jax.ShapeDtypeStruct((size, width), BF) for size in (part, *sizes)]
    return kernel_call(
        kernel,
        shapes,
        [ANY, VMEM],
        [ANY] * (1 + len(sizes)),
        (2 * height * width * block, 4 * height * width),
        limit=13,
        scratch_shapes=[
            pltpu.VMEM((height, width), BF),
            pltpu.VMEM((2, part, width), BF),
            pltpu.SemaphoreType.DMA((height // block,)),
            pltpu.SemaphoreType.DMA((2 * len(sizes),)),
        ],
    )(w, pick)


def cot_spread(place, pair, other, w_out, beside):
    quarter, width = pair.shape
    tokens = 2 * quarter
    hidden = w_out.shape[0]
    plane, part, rows = hidden // 2, width // 2, tokens // 8

    def kernel(
        place_ref, pair_ref, other_ref, w_ref, own, rest, padded, slot_ref,
        held, buf, made_ref, sems, out_sems,
    ):
        half, z_at, core_at = place_ref[1], place_ref[2], place_ref[3]
        copies = []
        for i in range(2):
            row = pl.multiple_of((half ^ i) * plane, 16)
            copy = pltpu.make_async_copy(w_ref.at[pl.ds(row, plane)], held.at[i], sems.at[i])
            copy.start()
            copies.append(copy)

        def chosen(count, near):
            to = lax.broadcasted_iota(jnp.int32, (count, quarter), 0)
            by = lax.broadcasted_iota(jnp.int32, (count, quarter), 1)
            to_z = (z_at + 4 - to // rows % 4) & 3
            to_token = (to_z * 2 + (core_at ^ (to // quarter))) * rows + to % rows
            by_z = (z_at + 4 - by // rows) & 3
            in_half = (by_z // 2) == (half if near else 1 - half)
            planes = []
            for q in (0, 1):
                total = jnp.zeros((count, width), F32)
                for e, ref in enumerate((pair_ref, other_ref)):
                    block = by_z % 2 * 2 + (core_at ^ e)
                    token = block * 2 * rows + 2 * (by % rows) + q
                    pick = jnp.where((token == to_token) & in_half, 1.0, 0.0).astype(BF)
                    total = total + dot(pick, ref[...])
                planes.append(total)
            lane = lax.broadcasted_iota(jnp.int32, (count, width), 1)
            return jnp.where(lane < part, planes[0] + pltpu.roll(planes[1], part, 1), 0.0)

        mine = chosen(tokens, True)
        made_ref[0] = mine.astype(BF)
        made_ref[1] = pltpu.roll(mine, part, 1).astype(BF)
        left, right = mine[:rows], chosen(rows, False)
        left, right = jnp.where(half == 0, left, right), jnp.where(half == 0, right, left)
        slot_ref[...] = (left + pltpu.roll(right, part, 1)).astype(BF)
        outs = [pltpu.make_async_copy(made_ref, padded, out_sems.at[2])]
        outs[0].start()
        for i, ref in enumerate((own, rest)):
            copies[i].wait()
            for q in (0, 1):
                made = dot(made_ref[q], held[i], ((1,), (1,))).astype(BF)
                buf[i, :, :, q * plane : (q + 1) * plane] = made.reshape(8, rows, plane)
            copy = pltpu.make_async_copy(buf.at[i], ref.at[:, :, pl.ds(0, hidden)], out_sems.at[i])
            copy.start()
            outs.append(copy)
        for copy in outs:
            copy.wait()

    return kernel_call(
        kernel,
        [jax.ShapeDtypeStruct((8, rows, hidden + extra), BF) for extra in beside]
        + [
            jax.ShapeDtypeStruct((2, tokens, width), BF),
            jax.ShapeDtypeStruct((rows, width), BF),
        ],
        [SMEM, VMEM, VMEM, ANY],
        [ANY, ANY, ANY, VMEM],
        (4 * tokens * hidden * width, 2 * hidden * width),
        limit=18,
        scratch_shapes=[
            pltpu.VMEM((2, plane, width), BF),
            pltpu.VMEM((2, 8, rows, hidden), BF),
            pltpu.VMEM((2, tokens, width), BF),
            pltpu.SemaphoreType.DMA((2,)),
            pltpu.SemaphoreType.DMA((3,)),
        ],
    )(place, pair, other, w_out)


def fill_rows(out, buf, sems, tiles):
    copies = []
    for number, (row, make) in enumerate(tiles):
        slot = number % 2
        if number >= 2:
            copies[number - 2].wait()
        buf[slot] = make().astype(BF)
        copy = pltpu.make_async_copy(
            buf.at[slot], out.at[pl.ds(row, buf.shape[1])], sems.at[slot]
        )
        copy.start()
        copies.append(copy)
    for copy in copies[-2:]:
        copy.wait()


def fetched(refs, bufs, sems):
    copies = [
        pltpu.make_async_copy(ref, buf, sems.at[number])
        for number, (ref, buf) in enumerate(zip(refs, bufs))
    ]
    for copy in copies:
        copy.start()
    for copy in copies:
        copy.wait()


def normed_rows(ref, beside, half):
    stats = joined_sums(beside.astype(F32))
    normed = (ref[...].astype(F32) - stats[:, 0:1]) * stats[:, 1:2]
    if half is not None:
        normed = jnp.where(half == 0, normed, pltpu.roll(normed, normed.shape[1] // 2, 1))
    return normed.astype(BF)


def products_early(place, acted, grad_all, pair, other, grad_pre, theirs):
    tokens, wide = acted.shape
    hidden = wide - 128
    width = grad_all.shape[1]
    part = width // 2
    quarter = tokens // 2

    def kernel(
        place_ref, acted_ref, grad_ref, pair_ref, other_ref, pre_ref, theirs_ref,
        out_ref, in_ref, hold_one, hold_two, hold_three, hold_pair, lefts,
        out_buf, in_buf, sems, out_sems, in_sems,
    ):
        @pl.when(place_ref[0] == 0)
        def _():
            fetched((acted_ref, grad_ref), (hold_one, hold_three), sems)
            tile = out_buf.shape[1]

            def make(at):
                return lambda: dot(hold_one[:, at : at + tile], hold_three[...], ((0,), (0,)))

            fill_rows(
                out_ref, out_buf, out_sems, [(at, make(at)) for at in range(0, hidden, tile)]
            )

        @pl.when(place_ref[0] == 1)
        def _():
            fetched(
                (pair_ref, other_ref, pre_ref, theirs_ref),
                (hold_pair.at[0], hold_pair.at[1], hold_one, hold_two),
                sems,
            )
            half = place_ref[1]
            row = lax.broadcasted_iota(jnp.int32, (128, 256), 0)
            lane = lax.broadcasted_iota(jnp.int32, (128, 256), 1)
            picks = [
                jnp.where(lane == 2 * row + plane, 1.0, 0.0).astype(BF)
                for plane in (half, 1 - half)
            ]
            for e in range(2):
                rows = slice(e * quarter, (e + 1) * quarter)
                normed = normed_rows(hold_pair.at[e], hold_one[rows, hidden:], half)
                for b in range(-(-part // 128)):
                    end = min(256 * (b + 1), width)
                    for number, pick in enumerate(picks):
                        made = dot(normed[:, 128 * b : 128 * (b + 1)], pick).astype(BF)
                        made = made[:, : end - 256 * b]
                        if number == 0:
                            lefts[0, rows, 256 * b : end] = made
                        else:
                            mid, at = quarter // 2, e * quarter
                            lefts[1, at + mid : at + quarter, 256 * b : end] = made[:mid]
                            lefts[1, at : at + mid, 256 * b : end] = made[mid:]
            tile = in_buf.shape[1]

            def make(at):
                def both():
                    mine = dot(lefts[0, :, at : at + tile], hold_one[:, :hidden], ((0,), (0,)))
                    return mine + dot(
                        lefts[1, :, at : at + tile], hold_two[:, :hidden], ((0,), (0,))
                    )

                return both

            fill_rows(in_ref, in_buf, in_sems, [(at, make(at)) for at in range(0, width, tile)])

    return kernel_call(
        kernel,
        [
            jax.ShapeDtypeStruct((hidden, width), BF),
            jax.ShapeDtypeStruct((width, hidden), BF),
        ],
        [SMEM] + [ANY] * 6,
        [ANY] * 2,
        (2 * tokens * hidden * width, 2 * hidden * width),
        limit=26,
        scratch_shapes=[
            pltpu.VMEM((tokens, wide), BF),
            pltpu.VMEM((tokens, wide), BF),
            pltpu.VMEM((tokens, width), BF),
            pltpu.VMEM((2, quarter, width), BF),
            pltpu.VMEM((2, tokens, width), BF),
            pltpu.VMEM((2, hidden // 3, width), BF),
            pltpu.VMEM((2, width // 3, hidden), BF),
            pltpu.SemaphoreType.DMA((4,)),
            pltpu.SemaphoreType.DMA((2,)),
            pltpu.SemaphoreType.DMA((2,)),
        ],
    )(place, acted, grad_all, pair, other, grad_pre, theirs)


def products_late(place, out_grad, in_grad, pair, other, acted, blocks, mine, padded):
    quarter, width = pair.shape
    tokens = 2 * quarter
    hidden = mine.shape[1]
    plane = hidden // 2

    def kernel(
        place_ref, out_was, in_was, pair_ref, other_ref, acted_ref, blocks_ref, mine_ref,
        padded_ref, out_ref, in_ref, hold_pair, hold_beside, hold_one, hold_two, left,
        hold_padded, out_buf, in_buf, sems, out_sems, in_sems,
    ):
        @pl.when(place_ref[0] == 0)
        def _():
            fetched(
                (pair_ref, other_ref, acted_ref.at[:, pl.ds(hidden, 128)], blocks_ref),
                (hold_pair.at[0], hold_pair.at[1], hold_beside, hold_one),
                sems,
            )
            for e in range(2):
                rows = slice(e * quarter, (e + 1) * quarter)
                left[rows, :] = normed_rows(hold_pair.at[e], hold_beside[rows], None)
            tile = in_buf.shape[1]

            def make(at):
                return lambda: dot(left[:, at : at + tile], hold_one[:, :hidden], ((0,), (0,)))

            fill_rows(in_ref, in_buf, in_sems, [(at, make(at)) for at in range(0, width, tile)])

        @pl.when(place_ref[0] == 1)
        def _():
            fetched((mine_ref, blocks_ref, padded_ref), (hold_two, hold_one, hold_padded), sems)
            tile = out_buf.shape[1]

            def make(ref, at):
                def both():
                    low = dot(ref[:, at : at + tile], hold_padded[0], ((0,), (0,)))
                    rest = dot(ref[:, plane + at : plane + at + tile], hold_padded[1], ((0,), (0,)))
                    return low + rest

                return both

            tiles = []
            for number, ref in enumerate((hold_two, hold_one)):
                base = (place_ref[1] ^ number) * plane
                tiles += [
                    (pl.multiple_of(base + at, 16), make(ref, at)) for at in range(0, plane, tile)
                ]
            fill_rows(out_ref, out_buf, out_sems, tiles)

    return kernel_call(
        kernel,
        [
            jax.ShapeDtypeStruct((hidden, width), BF),
            jax.ShapeDtypeStruct((width, hidden), BF),
        ],
        [SMEM] + [ANY] * 8,
        [ANY] * 2,
        (2 * tokens * hidden * width, 2 * hidden * width),
        limit=24,
        input_output_aliases={1: 0, 2: 1},
        scratch_shapes=[
            pltpu.VMEM((2, quarter, width), BF),
            pltpu.VMEM((tokens, 128), BF),
            pltpu.VMEM((tokens, hidden + 128), BF),
            pltpu.VMEM((tokens, hidden), BF),
            pltpu.VMEM((tokens, width), BF),
            pltpu.VMEM((2, tokens, width), BF),
            pltpu.VMEM((2, plane // 3, width), BF),
            pltpu.VMEM((2, width // 3, hidden), BF),
            pltpu.SemaphoreType.DMA((4,)),
            pltpu.SemaphoreType.DMA((2,)),
            pltpu.SemaphoreType.DMA((2,)),
        ],
    )(place, out_grad, in_grad, pair, other, acted, blocks, mine, padded)


def stack_rows(blocks):
    rows, width = blocks[0].shape

    def kernel(*refs):
        for number, ref in enumerate(refs[:-1]):
            refs[-1][number * rows : (number + 1) * rows, :] = ref[...]

    count = len(blocks)
    return kernel_call(
        kernel,
        jax.ShapeDtypeStruct((count * rows, width), BF),
        [VMEM] * count,
        VMEM,
        (0, 4 * count * rows * width),
    )(*blocks)


def gather_pairs(x):
    pair = stack_rows([x] + [send(x, along_z(k)) for k in (1, 2, 3)])
    return pair, send(pair, other_core)


def gather_tensor(x):
    return stack_rows(gather_pairs(x))


def swap_dp(blocks):
    return lax.all_to_all(blocks, "dp", 0, 0, tiled=True)


def one_hot(condition):
    return condition.astype(BF)


def after(value, *others):
    return lax.optimization_barrier((value, *others))[0]


def body(inputs, cotangent, w_first, w_second):
    w_in, w_out = w_first[0], w_second[0]
    rows, width = inputs.shape
    hidden = w_in.shape[1]
    part = width // 2
    tokens = 8 * rows
    first = lax.axis_index("section") == 0
    at = lax.axis_index("tensor")
    z_at, core_at = at // 2, at % 2
    half = at // 4

    slot_row = jnp.arange(tokens)
    slot_owner = ((z_at - slot_row // rows % 4) % 4) * 2 + (core_at ^ (slot_row // (4 * rows)))
    slot_token = slot_owner * rows + slot_row % rows

    place = jnp.stack([lax.axis_index("section"), half, z_at, core_at]).astype(jnp.int32)
    place_rows = jnp.arange(2 * rows)
    stored_token = (at % 4) * 2 * rows + 2 * (place_rows % rows) + place_rows // rows
    stored_order = one_hot(stored_token[:, None] == slot_token[None, :])

    block = 96
    index = jnp.arange(block)
    picked = 2 * (index % (block // 2)) + jnp.where(index < block // 2, half, 1 - half)
    pick = one_hot(index[None, :] == picked[:, None])
    sizes = [part // 4] * 4
    kept, *away = lax.cond(
        first,
        lambda: [blank(size, hidden) for size in (part, *sizes)],
        lambda: list(split_planes(w_in, pick, sizes)),
    )

    lead_pair, lead_other = gather_pairs(jnp.where(first, inputs, cotangent))
    came = [send(after(away[0], lead_other), other_half, LATER)]

    def lead_second():
        return list(cot_spread(place, lead_pair, lead_other, w_out, (128, 128)))

    def lead_first():
        made = pre_part(place, 0, lead_pair, lead_other, [w_in])
        return [made, blank(8, rows, hidden + 128), blank(2, tokens, width), blank(rows, width)]

    part_a, part_b, cot_padded, cot_own = lax.cond(first, lead_first, lead_second)
    swapped = swap_dp(after(part_a, came[0]))
    came.append(send(away[1], other_half, LATER))
    swapped = after(swapped, came[1])
    sum_a, ready, columns = spread_first(place, swapped, part_b, width)
    acted_first = swap_dp(ready)
    came.append(send(away[2], other_half, LATER))
    low, high, sum_b = branch_first(place, after(acted_first, came[2]), w_out)
    came.append(send(away[3], other_half, LATER))
    acted_first = acted_first.reshape(tokens, hidden + 128)
    w_parts = [kept, *came]
    grad_theirs = send(sum_b, other_half_row, LATER)
    branch = low.astype(F32) + send(high, other_core).astype(F32)
    stream = inputs.astype(F32)
    for k in range(4):
        arrived = send(branch[k * rows : (k + 1) * rows].astype(BF), across_z(-k))
        stream = stream + arrived.astype(F32)
    stream_own = after(stream.astype(BF), came[3], grad_theirs)

    pair, other = gather_pairs(stream_own)
    blocks = swap_dp(pre_part(place, 1, pair, other, w_parts))
    ready, acted_mine = grad_pre_later(blocks, sum_a, grad_theirs, width)
    grad_pre = swap_dp(ready).reshape(tokens, hidden + 128)
    mine, arrived = scatter_tensor(*back_part(place, 1, grad_pre, w_parts))
    later_grad = norm_back(mine, arrived, cot_own, stream_own, grad_pre[:rows, hidden:])
    acted_theirs = send(after(acted_mine, later_grad), other_half_row, LATER)

    returned = send(later_grad, other_section)
    own_grad = jnp.where(first, returned, later_grad)
    grad_all = gather_tensor(own_grad)
    grad_pre_theirs = send(after(grad_pre, grad_all), other_half, LATER)
    ready = grad_spread(place, grad_all, w_out, acted_mine)
    blocks = swap_dp(after(ready, acted_theirs))
    acted_mine_all = blocks.reshape(tokens, hidden)
    ready = grad_pre_first(place, blocks, sum_a, columns, acted_theirs)
    blocks = swap_dp(after(ready, grad_pre_theirs)).reshape(tokens, hidden + 128)
    out_grad, in_grad = products_early(
        place, acted_first, grad_all, pair, other, grad_pre, grad_pre_theirs
    )
    blocks = after(blocks, out_grad)
    mine, arrived = scatter_tensor(*back_part(place, 0, blocks, [w_in]))
    out_grad, in_grad = products_late(
        place, out_grad, in_grad, lead_pair, lead_other, acted_first, blocks, acted_mine_all,
        cot_padded,
    )
    result = norm_back(
        mine, arrived, own_grad, inputs, acted_first[:rows, hidden:],
        (place, stored_order, grad_all),
    )
    return (result[None], in_grad[None], out_grad[None])


def solution(mesh):
    return jax.shard_map(
        body,
        mesh=mesh,
        in_specs=(
            P("tensor", "dp"),
            P("tensor", "dp"),
            P("section", "dp", "tensor"),
            P("section", "tensor", "dp"),
        ),
        out_specs=(
            P("section", "tensor", "dp"),
            P("section", "dp", "tensor"),
            P("section", "tensor", "dp"),
        ),
        check_vma=False,
    )
```

```python
import jax
import jax.numpy as jnp
from jax import lax
from jax.experimental import pallas as pl
from jax.experimental.layout import Layout, with_layout_constraint
from jax.experimental.pallas import tpu as pltpu
from jax.sharding import PartitionSpec as P

D = 9216
EPSILON = 1e-05
AXES = ("section", "dp", "tensor")
BF = jnp.bfloat16
F32 = jnp.float32
FIRST = (0,)
LATER = (1,)
BOTH = (0, 1)
MIB = 2**20


def by_rows(value):
    return with_layout_constraint(value, Layout(major_to_minor=tuple(range(value.ndim))))


def send(value, move, sections=BOTH):
    pairs = []
    for s in sections:
        for d in range(8):
            for t in range(8):
                s2, d2, t2 = move(s, d, t)
                pairs.append(((s * 8 + d) * 8 + t, (s2 * 8 + d2) * 8 + t2))
    return by_rows(lax.ppermute(by_rows(value), AXES, pairs))


def along_x(k):
    return lambda s, d, t: (s, d // 4 * 4 + (d + k) % 4, t)


def along_z(k):
    return lambda s, d, t: (s, d, (t + 2 * k) % 8)


def other_core(s, d, t):
    return (s, d, t ^ 1)


def other_half(s, d, t):
    return (s, d, t ^ 4)


def other_half_row(s, d, t):
    return (s, d // 4 * 4 + (d + 2) % 4, t ^ 4)


def other_section(s, d, t):
    return (1 - s, d, t)


def dot(left, right, dims=((1,), (0,))):
    return lax.dot_general(left, right, (dims, ((), ())), preferred_element_type=F32)


VMEM = pl.BlockSpec(memory_space=pltpu.VMEM)
HBM = pl.BlockSpec(memory_space=pltpu.HBM)
SMEM = pl.BlockSpec(memory_space=pltpu.SMEM)


def kernel_call(kernel, out_shape, in_specs, out_specs, work, limit=4, **more):
    flops, moved = work
    return pl.pallas_call(
        kernel,
        out_shape=out_shape,
        in_specs=in_specs,
        out_specs=out_specs,
        compiler_params=pltpu.CompilerParams(vmem_limit_bytes=limit * MIB),
        cost_estimate=pl.CostEstimate(flops=flops, bytes_accessed=moved, transcendentals=0),
        **more,
    )


def blank(*shape):
    return kernel_call(lambda out: None, jax.ShapeDtypeStruct(shape, BF), [], HBM, (0, 0))()


def stream_plan(parts, turned):
    rows = sum(part.shape[0] for part in parts)
    cols = parts[0].shape[1]
    width = rows if turned else cols
    ends = [width // 3 if width > 1536 else 4 * width // 9, width]
    chunks = list(zip([0] + ends[:-1], ends))
    pieces = []
    for number, (at, end) in enumerate(chunks):
        row = 0
        for index, part in enumerate(parts):
            low, high = row, row + part.shape[0]
            row = high
            if turned:
                low, high = max(at, low), min(end, high)
            if low < high:
                pieces.append((number, index, low, high))
    return rows, cols, chunks, pieces, turned


def stream_copies(plan, parts, held, sems, turn=0):
    rows, cols, chunks, pieces, turned = plan
    first_rows = [0]
    for part in parts:
        first_rows.append(first_rows[-1] + part.shape[0])
    copies = []
    for sem, (number, index, low, high) in enumerate(pieces):
        at, end = (0, cols) if turned else chunks[number]
        begin = first_rows[index]
        to = low if isinstance(turn, int) else pl.multiple_of(lax.rem(low + turn, rows), 16)
        copy = pltpu.make_async_copy(
            parts[index].at[pl.ds(low - begin, high - low), pl.ds(at, end - at)],
            held.at[pl.ds(to, high - low), pl.ds(at, end - at)],
            sems.at[sem],
        )
        copies.append((number, copy))
    return copies


def grad_spread(place, x, w, own):
    plan = stream_plan([w], True)
    rows, cols, chunks, pieces, _ = plan
    tokens = x.shape[0]
    part = tokens // 8

    def kernel(place_ref, x_ref, w_ref, own_ref, out, held, buf, sems, out_sems):
        @pl.when(place_ref[0] == 0)
        def _():
            copies = stream_copies(plan, [w_ref], held, sems)
            for _, copy in copies:
                copy.start()
            left = x_ref[...]
            outs = []
            for number, (at, end) in enumerate(chunks):
                copies[number][1].wait()
                made = dot(left, held[at:end, :], ((1,), (1,))).astype(BF)
                buf[:, :, at:end] = made.reshape(8, part, end - at)
                lanes = pl.ds(at, end - at)
                copy = pltpu.make_async_copy(
                    buf.at[:, :, lanes], out.at[:, :, lanes], out_sems.at[number]
                )
                copy.start()
                outs.append(copy)
            for copy in outs:
                copy.wait()

        @pl.when(place_ref[0] == 1)
        def _():
            outs = [
                pltpu.make_async_copy(own_ref, out.at[j], out_sems.at[j]) for j in range(8)
            ]
            for copy in outs:
                copy.start()
            for copy in outs:
                copy.wait()

    return kernel_call(
        kernel,
        jax.ShapeDtypeStruct((8, part, rows), BF),
        [SMEM, VMEM, HBM, VMEM],
        HBM,
        (2 * tokens * rows * cols, 2 * (rows * cols + tokens * (rows + cols))),
        limit=10,
        scratch_shapes=[
            pltpu.VMEM((rows, cols), BF),
            pltpu.VMEM((8, part, rows), BF),
            pltpu.SemaphoreType.DMA((len(pieces),)),
            pltpu.SemaphoreType.DMA((8,)),
        ],
    )(place, x, w, own)


ROOT = 0.7978845608028654
CUBE = 0.044715


def gelu_parts(v):
    bent = jnp.tanh(ROOT * (v + CUBE * v * v * v))
    slope = 0.5 * (1.0 + bent) + 0.5 * v * (1.0 - bent * bent) * ROOT * (1.0 + 3.0 * CUBE * v * v)
    return 0.5 * v * (1.0 + bent), slope


def two_terms(value):
    top = value.astype(BF).astype(F32)
    return top, value - top


def lane_pack(columns):
    rows = columns[0].shape[0]
    lane = lax.broadcasted_iota(jnp.int32, (rows, 128), 1)
    block = jnp.zeros((rows, 128), F32)
    for number, column in enumerate(columns):
        block = jnp.where(lane == number, column, block)
    return block


def sums_pack(mean, inv, one, two):
    pairs = [two_terms(c) for c in (mean, inv, one, two)]
    return lane_pack([p[0] for p in pairs] + [p[1] for p in pairs]).astype(BF)


def stats_row(columns, rows):
    row = lax.broadcasted_iota(jnp.int32, (rows, 128), 0)
    lane = lax.broadcasted_iota(jnp.int32, (rows, 128), 1)
    block = jnp.zeros((rows, 128), F32)
    for number, column in enumerate(columns):
        block = jnp.where(lane == number * rows + row, column, block)
    return jnp.sum(block, axis=0, keepdims=True)


def norm_stats(beside, width, at):
    rows = beside.shape[1]
    row = lax.broadcasted_iota(jnp.int32, (rows, 128), 0)
    lane = lax.broadcasted_iota(jnp.int32, (rows, 128), 1)
    group = lane // rows

    def column(d, low, high):
        mask = (lane % rows == row) & (group >= low) & (group < high)
        line = jnp.broadcast_to(beside[d, at : at + 1, :], (rows, 128))
        return jnp.sum(jnp.where(mask, line, 0.0), axis=1, keepdims=True)

    shifts = [column(d, 0, 1) for d in range(8)]
    means = [column(d, 0, 2) for d in range(8)]
    mean = sum(means) / 8
    square = sum(column(d, 2, 4) + width * (means[d] - mean) ** 2 for d in range(8))
    inv = lax.rsqrt(square / D + EPSILON)
    return mean, inv, [shift - mean for shift in shifts]


def norm_sum(blocks_ref, beside, moves, inv, g):
    rows = beside.shape[1]
    lanes = slice(g * 128, (g + 1) * 128)
    pre = jnp.zeros((rows, 128), F32)
    columns = jnp.zeros((1, 128), F32)
    for d in range(8):
        column = beside[d, g : g + 1, :]
        columns = columns + column
        pre = pre + blocks_ref[d, :, lanes].astype(F32) + moves[d] * column
    return pre * inv, columns


def send_all(block, ready, sems):
    copies = [pltpu.make_async_copy(block, ready.at[j], sems.at[j]) for j in range(8)]
    for copy in copies:
        copy.start()
    for copy in copies:
        copy.wait()


def spread_first(place, swapped, part_b, width):
    _, rows, wide = swapped.shape
    hidden = wide - 128

    def kernel(
        place_ref, swapped_ref, part_ref, total_out, ready_ref, columns_out, sum_ref,
        total_ref, columns_ref, held, sems, out_sems,
    ):
        @pl.when(place_ref[0] == 0)
        def _():
            beside = swapped_ref[:, :, hidden:].astype(F32)
            mean, inv, moves = norm_stats(beside, width, hidden // 128)
            for g in range(hidden // 128):
                lanes = slice(g * 128, (g + 1) * 128)
                pre, columns = norm_sum(swapped_ref, beside, moves, inv, g)
                total_ref[:, lanes] = pre
                columns_ref[:, lanes] = jnp.broadcast_to(columns, (8, 128))
                held[:, lanes] = gelu_parts(pre)[0].astype(BF)
            held[:, hidden:] = sums_pack(mean, inv, mean, mean)
            copies = [
                pltpu.make_async_copy(total_ref, total_out, out_sems.at[0]),
                pltpu.make_async_copy(columns_ref, columns_out, out_sems.at[1]),
            ]
            for copy in copies:
                copy.start()
            send_all(held, ready_ref, sems)
            for copy in copies:
                copy.wait()

        @pl.when(place_ref[0] == 1)
        def _():
            for g in range(hidden // 128):
                lanes = slice(g * 128, (g + 1) * 128)
                total = swapped_ref[0, :, lanes].astype(F32)
                for j in range(1, 8):
                    total = total + swapped_ref[j, :, lanes].astype(F32)
                sum_ref[:, lanes] = total.astype(BF)

    return kernel_call(
        kernel,
        [
            jax.ShapeDtypeStruct((rows, hidden), F32),
            jax.ShapeDtypeStruct((8, rows, hidden + 128), BF),
            jax.ShapeDtypeStruct((8, hidden), F32),
            jax.ShapeDtypeStruct((rows, hidden), BF),
        ],
        [SMEM, VMEM, HBM],
        [HBM, HBM, HBM, VMEM],
        (30 * rows * hidden, 40 * rows * hidden),
        input_output_aliases={2: 1},
        scratch_shapes=[
            pltpu.VMEM((rows, hidden), F32),
            pltpu.VMEM((8, hidden), F32),
            pltpu.VMEM((rows, hidden + 128), BF),
            pltpu.SemaphoreType.DMA((8,)),
            pltpu.SemaphoreType.DMA((2,)),
        ],
    )(place, swapped, part_b)


def branch_first(place, blocks, w_out):
    _, rows, wide = blocks.shape
    hidden = w_out.shape[0]
    tokens = 8 * rows
    plan = stream_plan([w_out], False)
    _, width, chunks, pieces, _ = plan

    def kernel(place_ref, x_ref, w_ref, low, high, total_ref, held, sems):
        @pl.when(place_ref[0] == 0)
        def _():
            copies = stream_copies(plan, [w_ref], held, sems)
            for _, copy in copies:
                copy.start()
            left = x_ref[:, :, :hidden].reshape(tokens, hidden)
            for number, (at, end) in enumerate(chunks):
                copies[number][1].wait()
                made = dot(left, held[:, at:end]).astype(BF)
                low[:, at:end] = made[: tokens // 2]
                high[:, at:end] = made[tokens // 2 :]

        @pl.when(place_ref[0] == 1)
        def _():
            for g in range(hidden // 128):
                lanes = slice(g * 128, (g + 1) * 128)
                total = x_ref[0, :, lanes].astype(F32)
                for j in range(1, 8):
                    total = total + x_ref[j, :, lanes].astype(F32)
                total_ref[:, lanes] = total

    return kernel_call(
        kernel,
        [
            jax.ShapeDtypeStruct((tokens // 2, width), BF),
            jax.ShapeDtypeStruct((tokens // 2, width), BF),
            jax.ShapeDtypeStruct((rows, hidden), F32),
        ],
        [SMEM, VMEM, HBM],
        [VMEM] * 3,
        (2 * tokens * hidden * width, 2 * hidden * width),
        limit=9,
        scratch_shapes=[
            pltpu.VMEM((hidden, width), BF),
            pltpu.SemaphoreType.DMA((len(pieces),)),
        ],
    )(place, blocks, w_out)


def pre_part(place, section, pair, other, w_parts):
    quarter, width = pair.shape
    tokens = 2 * quarter
    rows = tokens // 8
    plan = stream_plan(w_parts, False)
    _, hidden, chunks, pieces, _ = plan

    def kernel(place_ref, pair_ref, other_ref, *refs):
        part_refs, (out, held, left, buf, sems, out_sems) = refs[: len(w_parts)], refs[len(w_parts) :]

        @pl.when(place_ref[0] == section)
        def _():
            turn = place_ref[1] * (width // 2) if section == 1 else 0
            copies = stream_copies(plan, part_refs, held, sems, turn)
            for _, copy in copies:
                copy.start()
            lines = []
            for e, ref in enumerate((pair_ref, other_ref)):
                spread = ref[...].astype(F32)
                mean = jnp.sum(spread, axis=1, keepdims=True) / width
                off = spread - mean
                square = jnp.sum(off * off, axis=1, keepdims=True)
                shift = mean.astype(BF).astype(F32)
                left[e * quarter : (e + 1) * quarter, :] = (spread - shift).astype(BF)
                columns = [*two_terms(mean), *two_terms(square)]
                for k in range(4):
                    part = slice(k * rows, (k + 1) * rows)
                    lines.append(stats_row([column[part] for column in columns], rows))
            left[tokens:, :] = jnp.ones((16, width), BF)
            tops, outs = [], []

            def leave(at, end):
                lanes = pl.ds(at, end - at)
                copy = pltpu.make_async_copy(
                    buf.at[:, :, lanes], out.at[:, :, lanes], out_sems.at[len(outs)]
                )
                copy.start()
                outs.append(copy)

            for number, (at, end) in enumerate(chunks):
                for begun, copy in copies:
                    if begun == number:
                        copy.wait()
                made = dot(left[...], held[:, at:end])
                buf[:, :, at:end] = made[:tokens].astype(BF).reshape(8, rows, end - at)
                leave(at, end)
                sums = made[tokens : tokens + 1]
                for g in range((end - at) // 128):
                    tops.append(sums[:, g * 128 : (g + 1) * 128])
            empty = jnp.zeros((rows - len(tops) - 1, 128), F32)
            for j in range(8):
                block = jnp.concatenate([*tops, lines[j], empty], axis=0)
                buf[j, :, hidden:] = block.astype(BF)
            leave(hidden, hidden + 128)
            for copy in outs:
                copy.wait()

    return kernel_call(
        kernel,
        jax.ShapeDtypeStruct((8, rows, hidden + 128), BF),
        [SMEM, VMEM, VMEM] + [HBM] * len(w_parts),
        HBM,
        (2 * tokens * hidden * width, 2 * hidden * width),
        limit=14,
        scratch_shapes=[
            pltpu.VMEM((width, hidden), BF),
            pltpu.VMEM((tokens + 16, width), BF),
            pltpu.VMEM((8, rows, hidden + 128), BF),
            pltpu.SemaphoreType.DMA((len(pieces),)),
            pltpu.SemaphoreType.DMA((len(chunks) + 1,)),
        ],
    )(place, pair, other, *w_parts)


def weave(turned):
    row = lax.broadcasted_iota(jnp.int32, (256, 256), 0)
    lane = lax.broadcasted_iota(jnp.int32, (256, 256), 1)
    if turned:
        row, lane = lane, row
    return jnp.where(lane == 2 * (row % 128) + row // 128, 1.0, 0.0).astype(BF)


def grad_pre_later(blocks, grad_mine, grad_theirs, width):
    _, rows, wide = blocks.shape
    hidden = wide - 128
    plane = hidden // 2

    def kernel(blocks_ref, mine_ref, theirs_ref, ready, acted_ref, grad_ref, held_ref, own, sems):
        order, back = weave(False), weave(True)
        for b in range(hidden // 256):
            pair = []
            for q in (0, 1):
                lanes = slice(q * plane + b * 128, q * plane + (b + 1) * 128)
                pair.append(mine_ref[:, lanes] + theirs_ref[:, lanes].astype(F32))
            top, rest = two_terms(jnp.concatenate(pair, axis=1))
            done = dot(top.astype(BF), order) + dot(rest.astype(BF), order)
            grad_ref[:, b * 256 : (b + 1) * 256] = done
        beside = blocks_ref[:, :, hidden:].astype(F32)
        mean, inv, moves = norm_stats(beside, width, hidden // 128)
        one = jnp.zeros((rows, 1), F32)
        two = jnp.zeros((rows, 1), F32)
        for g in range(hidden // 128):
            lanes = slice(g * 128, (g + 1) * 128)
            pre, columns = norm_sum(blocks_ref, beside, moves, inv, g)
            acted, slope = gelu_parts(pre)
            held_ref[:, lanes] = acted.astype(BF)
            grad = (grad_ref[:, lanes] * slope).astype(BF)
            own[:, lanes] = grad
            grad = grad.astype(F32)
            one = one + jnp.sum(grad * columns, axis=1, keepdims=True)
            two = two + jnp.sum(grad * pre, axis=1, keepdims=True)
        own[:, hidden:] = sums_pack(mean, inv, one, two)
        send_all(own, ready, sems)
        for b in range(hidden // 256):
            done = dot(held_ref[:, b * 256 : (b + 1) * 256], back).astype(BF)
            acted_ref[:, b * 128 : (b + 1) * 128] = done[:, :128]
            acted_ref[:, plane + b * 128 : plane + (b + 1) * 128] = done[:, 128:]

    return kernel_call(
        kernel,
        [
            jax.ShapeDtypeStruct((8, rows, hidden + 128), BF),
            jax.ShapeDtypeStruct((rows, hidden), BF),
        ],
        [VMEM] * 3,
        [HBM, VMEM],
        (80 * rows * hidden, 40 * rows * hidden),
        scratch_shapes=[
            pltpu.VMEM((rows, hidden), F32),
            pltpu.VMEM((rows, hidden), BF),
            pltpu.VMEM((rows, hidden + 128), BF),
            pltpu.SemaphoreType.DMA((8,)),
        ],
    )(blocks, grad_mine, grad_theirs)


def grad_pre_first(place, blocks, pre, columns, theirs):
    _, rows, hidden = blocks.shape

    def kernel(
        place_ref, blocks_ref, pre_in, columns_in, theirs_ref, ready,
        pre_ref, columns_ref, own, sems,
    ):
        @pl.when(place_ref[0] == 0)
        def _():
            fetched((pre_in, columns_in), (pre_ref, columns_ref), sems)
            one = jnp.zeros((rows, 1), F32)
            two = jnp.zeros((rows, 1), F32)
            for g in range(hidden // 128):
                lanes = slice(g * 128, (g + 1) * 128)
                total = blocks_ref[0, :, lanes].astype(F32)
                for j in range(1, 8):
                    total = total + blocks_ref[j, :, lanes].astype(F32)
                pre = pre_ref[:, lanes]
                grad = (total * gelu_parts(pre)[1]).astype(BF)
                own[:, lanes] = grad
                grad = grad.astype(F32)
                one = one + jnp.sum(grad * columns_ref[0:1, lanes], axis=1, keepdims=True)
                two = two + jnp.sum(grad * pre, axis=1, keepdims=True)
            own[:, hidden:] = sums_pack(one, one, one, two)

        @pl.when(place_ref[0] == 1)
        def _():
            fetched((theirs_ref,), (own.at[:, pl.ds(0, hidden)],), sems)
            own[:, hidden:] = jnp.zeros((rows, 128), BF)

        send_all(own, ready, sems)

    return kernel_call(
        kernel,
        jax.ShapeDtypeStruct((8, rows, hidden + 128), BF),
        [SMEM, VMEM] + [HBM] * 3,
        HBM,
        (60 * rows * hidden, 40 * rows * hidden),
        scratch_shapes=[
            pltpu.VMEM((rows, hidden), F32),
            pltpu.VMEM((8, hidden), F32),
            pltpu.VMEM((rows, hidden + 128), BF),
            pltpu.SemaphoreType.DMA((8,)),
        ],
    )(place, blocks, pre, columns, theirs)


def back_part(place, section, grad_pre, w_parts):
    tokens, wide = grad_pre.shape
    hidden = wide - 128
    plan = stream_plan(w_parts, True)
    width, _, chunks, pieces, _ = plan

    def kernel(place_ref, x_ref, *refs):
        w_refs, (low, high, held, made, sems) = refs[: len(w_parts)], refs[len(w_parts) :]

        @pl.when(place_ref[0] == section)
        def _():
            copies = stream_copies(plan, w_refs, held, sems)
            for _, copy in copies:
                copy.start()
            left = x_ref[:, :hidden]
            for number, (at, end) in enumerate(chunks):
                for begun, copy in copies:
                    if begun == number:
                        copy.wait()
                made[:, at:end] = dot(left, held[at:end, :], ((1,), (1,)))
            done = made[...]
            if section == 1:
                done = jnp.where(place_ref[1] == 0, done, pltpu.roll(done, width // 2, 1))
            done = done.astype(BF)
            for number, out in enumerate((low, high)):
                part = slice(number * tokens // 2, (number + 1) * tokens // 2)
                out[:, :width] = done[part]
                out[:, width:] = x_ref[part, hidden:]

    return kernel_call(
        kernel,
        [jax.ShapeDtypeStruct((tokens // 2, width + 128), BF)] * 2,
        [SMEM, VMEM] + [HBM] * len(w_parts),
        [VMEM] * 2,
        (2 * tokens * hidden * width, 2 * hidden * width),
        limit=12,
        scratch_shapes=[
            pltpu.VMEM((width, hidden), BF),
            pltpu.VMEM((tokens, width), F32),
            pltpu.SemaphoreType.DMA((len(pieces),)),
        ],
    )(place, grad_pre, *w_parts)


def joined_sums(block):
    return block + pltpu.roll(block, 124, 1)


def core_sum(low, arrived):
    quarter, wide = low.shape
    width = wide - 128
    rows = quarter // 4

    def kernel(low_ref, arrived_ref, mine, *ready):
        for k in range(4):
            part = slice(k * rows, (k + 1) * rows)
            total = low_ref[part, :width].astype(F32) + arrived_ref[part, :width].astype(F32)
            sums = joined_sums(low_ref[part, width:].astype(F32))
            sums = sums + joined_sums(arrived_ref[part, width:].astype(F32))
            if k == 0:
                mine[:, :width] = total
                mine[:, width:] = sums
            else:
                ready[k - 1][:, :width] = total.astype(BF)
                top, rest = two_terms(sums)
                lane = lax.broadcasted_iota(jnp.int32, (rows, 128), 1)
                ready[k - 1][:, width:] = jnp.where(lane < 4, top, pltpu.roll(rest, 4, 1)).astype(BF)

    return kernel_call(
        kernel,
        [jax.ShapeDtypeStruct((rows, wide), F32)] + [jax.ShapeDtypeStruct((rows, wide), BF)] * 3,
        [VMEM] * 2,
        [VMEM] * 4,
        (2 * quarter * wide, 8 * quarter * wide),
    )(low, arrived)


def norm_back(mine, arrived, grad_out, stream, stats, tail=None):
    rows, wide = mine.shape
    width = wide - 128
    extra = () if tail is None else tail

    def kernel(mine_ref, one, two, three, grad_ref, stream_ref, stats_ref, *refs):
        out = refs[-1]

        def fill():
            total = mine_ref[:, :width]
            sums = mine_ref[:, width:]
            for ref in (one, two, three):
                total = total + ref[:, :width].astype(F32)
                sums = sums + joined_sums(ref[:, width:].astype(F32))
            stats = joined_sums(stats_ref[...].astype(F32))
            mean, inv = stats[:, 0:1], stats[:, 1:2]
            centred = (stream_ref[...].astype(F32) - mean) * inv
            grad = total - sums[:, 2:3] / D - centred * (sums[:, 3:4] / D)
            out[...] = (grad_ref[...].astype(F32) + inv * grad).astype(BF)

        if tail is None:
            fill()
            return
        place_ref, order_ref, whole_ref = refs[:3]
        pl.when(place_ref[0] == 0)(fill)

        @pl.when(place_ref[0] == 1)
        def _():
            chosen = dot(order_ref[...], whole_ref[...])
            turned = pltpu.roll(chosen, width // 2, 1)
            lane = lax.broadcasted_iota(jnp.int32, (rows, width), 1)
            own = place_ref[1] == 0
            left = jnp.where(own, chosen[:rows], turned[:rows])
            right = jnp.where(own, turned[rows:], chosen[rows:])
            out[...] = jnp.where(lane < width // 2, left, right).astype(BF)

    specs = [VMEM] * 7 + ([SMEM, VMEM, VMEM] if extra else [])
    return kernel_call(
        kernel,
        jax.ShapeDtypeStruct((rows, width), BF),
        specs,
        VMEM,
        (20 * rows * wide, 20 * rows * wide),
    )(mine, *arrived, grad_out, stream, stats, *extra)


def scatter_tensor(low, high):
    mine, *ready = core_sum(low, send(high, other_core))
    return mine, [send(block, along_z(-k)) for k, block in zip((1, 2, 3), ready)]


def split_planes(w, pick, sizes):
    height, width = w.shape
    part = height // 2
    block = pick.shape[0]
    sub = block // 2

    def kernel(w_ref, pick_ref, kept, *refs):
        away, (held, planes, sems, out_sem) = refs[: len(sizes)], refs[len(sizes) :]
        steps = height // block
        copies = [
            pltpu.make_async_copy(
                w_ref.at[pl.ds(at * block, block)], held.at[pl.ds(at * block, block)], sems.at[at]
            )
            for at in range(steps)
        ]
        for copy in copies:
            copy.start()
        outs, piece, begun = [], 0, 0
        for at, copy in enumerate(copies):
            copy.wait()
            rows = dot(pick_ref[...], held[at * block : (at + 1) * block, :]).astype(BF)
            planes[0, at * sub : (at + 1) * sub, :] = rows[:sub]
            planes[1, at * sub : (at + 1) * sub, :] = rows[sub:]
            if (at + 1) * sub == begun + sizes[piece]:
                lines = pl.ds(begun, sizes[piece])
                for plane, ref in enumerate((kept.at[lines], away[piece])):
                    out = pltpu.make_async_copy(
                        planes.at[plane, lines], ref, out_sem.at[2 * piece + plane]
                    )
                    out.start()
                    outs.append(out)
                begun += sizes[piece]
                piece += 1
        for out in outs:
            out.wait()

    shapes = [jax.ShapeDtypeStruct((size, width), BF) for size in (part, *sizes)]
    return kernel_call(
        kernel,
        shapes,
        [HBM, VMEM],
        [HBM] * (1 + len(sizes)),
        (2 * height * width * block, 4 * height * width),
        limit=13,
        scratch_shapes=[
            pltpu.VMEM((height, width), BF),
            pltpu.VMEM((2, part, width), BF),
            pltpu.SemaphoreType.DMA((height // block,)),
            pltpu.SemaphoreType.DMA((2 * len(sizes),)),
        ],
    )(w, pick)


def cot_spread(place, pair, other, w_out, beside):
    quarter, width = pair.shape
    tokens = 2 * quarter
    hidden = w_out.shape[0]
    plane, part, rows = hidden // 2, width // 2, tokens // 8

    def kernel(
        place_ref, pair_ref, other_ref, w_ref, rest, own, padded, slot_ref,
        held, buf, made_ref, sems, out_sems,
    ):
        half, z_at, core_at = place_ref[1], place_ref[2], place_ref[3]
        copies = []
        for i in range(2):
            row = pl.multiple_of((half ^ (1 - i)) * plane, 16)
            copy = pltpu.make_async_copy(w_ref.at[pl.ds(row, plane)], held.at[i], sems.at[i])
            copy.start()
            copies.append(copy)

        def chosen(count, near):
            to = lax.broadcasted_iota(jnp.int32, (count, quarter), 0)
            by = lax.broadcasted_iota(jnp.int32, (count, quarter), 1)
            to_z = (z_at + 4 - to // rows % 4) & 3
            to_token = (to_z * 2 + (core_at ^ (to // quarter))) * rows + to % rows
            by_z = (z_at + 4 - by // rows) & 3
            in_half = (by_z // 2) == (half if near else 1 - half)
            planes = []
            for q in (0, 1):
                total = jnp.zeros((count, width), F32)
                for e, ref in enumerate((pair_ref, other_ref)):
                    block = by_z % 2 * 2 + (core_at ^ e)
                    token = block * 2 * rows + 2 * (by % rows) + q
                    pick = jnp.where((token == to_token) & in_half, 1.0, 0.0).astype(BF)
                    total = total + dot(pick, ref[...])
                planes.append(total)
            lane = lax.broadcasted_iota(jnp.int32, (count, width), 1)
            return jnp.where(lane < part, planes[0] + pltpu.roll(planes[1], part, 1), 0.0)

        mine = chosen(tokens, True)
        made_ref[0] = mine.astype(BF)
        made_ref[1] = pltpu.roll(mine, part, 1).astype(BF)
        left, right = mine[:rows], chosen(rows, False)
        left, right = jnp.where(half == 0, left, right), jnp.where(half == 0, right, left)
        slot_ref[...] = (left + pltpu.roll(right, part, 1)).astype(BF)
        outs = [pltpu.make_async_copy(made_ref, padded, out_sems.at[2])]
        outs[0].start()
        for i, ref in enumerate((rest, own)):
            copies[i].wait()
            for q in (0, 1):
                made = dot(made_ref[q], held[i], ((1,), (1,))).astype(BF)
                buf[i, :, :, q * plane : (q + 1) * plane] = made.reshape(8, rows, plane)
            copy = pltpu.make_async_copy(buf.at[i], ref.at[:, :, pl.ds(0, hidden)], out_sems.at[i])
            copy.start()
            outs.append(copy)
        for copy in outs:
            copy.wait()

    return kernel_call(
        kernel,
        [jax.ShapeDtypeStruct((8, rows, hidden + extra), BF) for extra in beside]
        + [
            jax.ShapeDtypeStruct((2, tokens, width), BF),
            jax.ShapeDtypeStruct((rows, width), BF),
        ],
        [SMEM, VMEM, VMEM, HBM],
        [HBM, HBM, HBM, VMEM],
        (4 * tokens * hidden * width, 2 * hidden * width),
        limit=18,
        scratch_shapes=[
            pltpu.VMEM((2, plane, width), BF),
            pltpu.VMEM((2, 8, rows, hidden), BF),
            pltpu.VMEM((2, tokens, width), BF),
            pltpu.SemaphoreType.DMA((2,)),
            pltpu.SemaphoreType.DMA((3,)),
        ],
    )(place, pair, other, w_out)


def fill_rows(out, buf, sems, tiles):
    copies = []
    for number, (row, count, make) in enumerate(tiles):
        slot = number % 2
        if number >= 2:
            copies[number - 2].wait()
        lines = pl.ds(0, count)
        buf[slot, 0:count, :] = make().astype(BF)
        copy = pltpu.make_async_copy(buf.at[slot, lines], out.at[pl.ds(row, count)], sems.at[slot])
        copy.start()
        copies.append(copy)
    for copy in copies[-2:]:
        copy.wait()


def two_tiles(width):
    cut = (width // 128 + 1) // 2 * 128 if width >= 512 else width // 2
    return [(0, cut), (cut, width)]


def fetched(refs, bufs, sems):
    copies = [
        pltpu.make_async_copy(ref, buf, sems.at[number])
        for number, (ref, buf) in enumerate(zip(refs, bufs))
    ]
    for copy in copies:
        copy.start()
    for copy in copies:
        copy.wait()


def normed_rows(ref, beside, half):
    stats = joined_sums(beside.astype(F32))
    normed = (ref[...].astype(F32) - stats[:, 0:1]) * stats[:, 1:2]
    if half is not None:
        normed = jnp.where(half == 0, normed, pltpu.roll(normed, normed.shape[1] // 2, 1))
    return normed.astype(BF)


def products_early(place, acted, grad_all, pair, other, grad_pre, theirs):
    tokens, wide = acted.shape
    hidden = wide - 128
    width = grad_all.shape[1]
    part = width // 2
    quarter = tokens // 2

    def kernel(
        place_ref, acted_ref, grad_ref, pair_ref, other_ref, pre_ref, theirs_ref,
        out_ref, in_ref, hold_one, hold_two, hold_three, hold_pair, lefts,
        out_buf, in_buf, sems, out_sems, in_sems,
    ):
        @pl.when(place_ref[0] == 0)
        def _():
            fetched((acted_ref, grad_ref), (hold_one, hold_three), sems)
            def make(at, end):
                return lambda: dot(hold_one[:, at:end], hold_three[...], ((0,), (0,)))

            cuts = two_tiles(hidden)
            fill_rows(
                out_ref, out_buf, out_sems, [(at, end - at, make(at, end)) for at, end in cuts]
            )

        @pl.when(place_ref[0] == 1)
        def _():
            fetched(
                (pair_ref, other_ref, pre_ref, theirs_ref),
                (hold_pair.at[0], hold_pair.at[1], hold_one, hold_two),
                sems,
            )
            half = place_ref[1]
            row = lax.broadcasted_iota(jnp.int32, (128, 256), 0)
            lane = lax.broadcasted_iota(jnp.int32, (128, 256), 1)
            picks = [
                jnp.where(lane == 2 * row + plane, 1.0, 0.0).astype(BF)
                for plane in (half, 1 - half)
            ]
            for e in range(2):
                rows = slice(e * quarter, (e + 1) * quarter)
                normed = normed_rows(hold_pair.at[e], hold_one[rows, hidden:], half)
                for b in range(-(-part // 128)):
                    end = min(256 * (b + 1), width)
                    for number, pick in enumerate(picks):
                        made = dot(normed[:, 128 * b : 128 * (b + 1)], pick).astype(BF)
                        made = made[:, : end - 256 * b]
                        if number == 0:
                            lefts[0, rows, 256 * b : end] = made
                        else:
                            mid, at = quarter // 2, e * quarter
                            lefts[1, at + mid : at + quarter, 256 * b : end] = made[:mid]
                            lefts[1, at : at + mid, 256 * b : end] = made[mid:]
            def make(at, end):
                def both():
                    mine = dot(lefts[0, :, at:end], hold_one[:, :hidden], ((0,), (0,)))
                    return mine + dot(lefts[1, :, at:end], hold_two[:, :hidden], ((0,), (0,)))

                return both

            cuts = two_tiles(width)
            fill_rows(in_ref, in_buf, in_sems, [(at, end - at, make(at, end)) for at, end in cuts])

    return kernel_call(
        kernel,
        [
            jax.ShapeDtypeStruct((hidden, width), BF),
            jax.ShapeDtypeStruct((width, hidden), BF),
        ],
        [SMEM] + [HBM] * 6,
        [HBM] * 2,
        (2 * tokens * hidden * width, 2 * hidden * width),
        limit=36,
        scratch_shapes=[
            pltpu.VMEM((tokens, wide), BF),
            pltpu.VMEM((tokens, wide), BF),
            pltpu.VMEM((tokens, width), BF),
            pltpu.VMEM((2, quarter, width), BF),
            pltpu.VMEM((2, tokens, width), BF),
            pltpu.VMEM((2, two_tiles(hidden)[0][1], width), BF),
            pltpu.VMEM((2, two_tiles(width)[0][1], hidden), BF),
            pltpu.SemaphoreType.DMA((4,)),
            pltpu.SemaphoreType.DMA((2,)),
            pltpu.SemaphoreType.DMA((2,)),
        ],
    )(place, acted, grad_all, pair, other, grad_pre, theirs)


def products_late(place, out_grad, in_grad, pair, other, acted, blocks, mine, padded):
    quarter, width = pair.shape
    tokens = 2 * quarter
    hidden = mine.shape[1]
    plane = hidden // 2

    def kernel(
        place_ref, out_was, in_was, pair_ref, other_ref, acted_ref, blocks_ref, mine_ref,
        padded_ref, out_ref, in_ref, hold_pair, hold_beside, hold_one, hold_two, left,
        hold_padded, out_buf, in_buf, sems, out_sems, in_sems,
    ):
        @pl.when(place_ref[0] == 0)
        def _():
            fetched(
                (pair_ref, other_ref, acted_ref.at[:, pl.ds(hidden, 128)], blocks_ref),
                (hold_pair.at[0], hold_pair.at[1], hold_beside, hold_one),
                sems,
            )
            for e in range(2):
                rows = slice(e * quarter, (e + 1) * quarter)
                left[rows, :] = normed_rows(hold_pair.at[e], hold_beside[rows], None)
            def make(at, end):
                return lambda: dot(left[:, at:end], hold_one[:, :hidden], ((0,), (0,)))

            cuts = two_tiles(width)
            fill_rows(in_ref, in_buf, in_sems, [(at, end - at, make(at, end)) for at, end in cuts])

        @pl.when(place_ref[0] == 1)
        def _():
            fetched((mine_ref, blocks_ref, padded_ref), (hold_two, hold_one, hold_padded), sems)
            def make(ref):
                def both():
                    low = dot(ref[:, :plane], hold_padded[0], ((0,), (0,)))
                    return low + dot(ref[:, plane:hidden], hold_padded[1], ((0,), (0,)))

                return both

            tiles = []
            for number, ref in enumerate((hold_two, hold_one)):
                row = pl.multiple_of((place_ref[1] ^ number) * plane, 16)
                tiles.append((row, plane, make(ref)))
            fill_rows(out_ref, out_buf, out_sems, tiles)

    return kernel_call(
        kernel,
        [
            jax.ShapeDtypeStruct((hidden, width), BF),
            jax.ShapeDtypeStruct((width, hidden), BF),
        ],
        [SMEM] + [HBM] * 8,
        [HBM] * 2,
        (2 * tokens * hidden * width, 2 * hidden * width),
        limit=36,
        input_output_aliases={1: 0, 2: 1},
        scratch_shapes=[
            pltpu.VMEM((2, quarter, width), BF),
            pltpu.VMEM((tokens, 128), BF),
            pltpu.VMEM((tokens, hidden + 128), BF),
            pltpu.VMEM((tokens, hidden), BF),
            pltpu.VMEM((tokens, width), BF),
            pltpu.VMEM((2, tokens, width), BF),
            pltpu.VMEM((2, plane, width), BF),
            pltpu.VMEM((2, two_tiles(width)[0][1], hidden), BF),
            pltpu.SemaphoreType.DMA((4,)),
            pltpu.SemaphoreType.DMA((2,)),
            pltpu.SemaphoreType.DMA((2,)),
        ],
    )(place, out_grad, in_grad, pair, other, acted, blocks, mine, padded)


def stack_rows(blocks):
    rows, width = blocks[0].shape

    def kernel(*refs):
        for number, ref in enumerate(refs[:-1]):
            refs[-1][number * rows : (number + 1) * rows, :] = ref[...]

    count = len(blocks)
    return kernel_call(
        kernel,
        jax.ShapeDtypeStruct((count * rows, width), BF),
        [VMEM] * count,
        VMEM,
        (0, 4 * count * rows * width),
    )(*blocks)


def gather_pairs(x, *others):
    pair = stack_rows([after(x, *others)] + [send(x, along_z(k)) for k in (1, 2, 3)])
    return pair, send(pair, other_core)


def gather_tensor(x):
    return stack_rows(gather_pairs(x))


def swap_dp(blocks):
    return lax.all_to_all(blocks, "dp", 0, 0, tiled=True)


def one_hot(condition):
    return condition.astype(BF)


def after(value, *others):
    return lax.optimization_barrier((value, *others))[0]


def body(inputs, cotangent, w_first, w_second):
    w_in, w_out = w_first[0], w_second[0]
    rows, width = inputs.shape
    hidden = w_in.shape[1]
    part = width // 2
    tokens = 8 * rows
    first = lax.axis_index("section") == 0
    at = lax.axis_index("tensor")
    z_at, core_at = at // 2, at % 2
    half = at // 4

    slot_row = jnp.arange(tokens)
    slot_owner = ((z_at - slot_row // rows % 4) % 4) * 2 + (core_at ^ (slot_row // (4 * rows)))
    slot_token = slot_owner * rows + slot_row % rows

    place = jnp.stack([lax.axis_index("section"), half, z_at, core_at]).astype(jnp.int32)
    place_rows = jnp.arange(2 * rows)
    stored_token = (at % 4) * 2 * rows + 2 * (place_rows % rows) + place_rows // rows
    stored_order = one_hot(stored_token[:, None] == slot_token[None, :])

    unit = part // 12
    block = 2 * unit
    index = jnp.arange(block)
    picked = 2 * (index % (block // 2)) + jnp.where(index < block // 2, half, 1 - half)
    pick = one_hot(index[None, :] == picked[:, None])
    sizes = [2 * unit, 3 * unit, 3 * unit, 4 * unit]
    kept, *away = lax.cond(
        first,
        lambda: [blank(size, hidden) for size in (part, *sizes)],
        lambda: list(split_planes(w_in, pick, sizes)),
    )

    lead_pair, lead_other = gather_pairs(jnp.where(first, inputs, cotangent), *away)
    came = [send(after(away[0], lead_other), other_half, LATER)]

    def lead_second():
        return list(cot_spread(place, lead_pair, lead_other, w_out, (128, 128)))

    def lead_first():
        made = pre_part(place, 0, lead_pair, lead_other, [w_in])
        return [made, blank(8, rows, hidden + 128), blank(2, tokens, width), blank(rows, width)]

    part_a, part_b, cot_padded, cot_own = lax.cond(first, lead_first, lead_second)
    swapped = swap_dp(after(part_a, came[0]))
    came.append(send(away[1], other_half, LATER))
    swapped = after(swapped, came[1])
    pre_first, ready, columns, sum_theirs = spread_first(place, swapped, part_b, width)
    grad_theirs = send(sum_theirs, other_half_row, LATER)
    acted_first = swap_dp(ready)
    came.append(send(away[2], other_half, LATER))
    acted_first = after(acted_first, came[2], grad_theirs)
    low, high, grad_mine = branch_first(place, acted_first, w_out)
    came.append(send(away[3], other_half, LATER))
    acted_first = acted_first.reshape(tokens, hidden + 128)
    w_parts = [kept, *came]
    branch = low.astype(F32) + send(high, other_core).astype(F32)
    stream = inputs.astype(F32) + branch[:rows]
    for k in (1, 2, 3):
        block = branch[k * rows : (k + 1) * rows].astype(BF)
        stream = stream + send(block, along_z(-k), FIRST).astype(F32)
    stream = stream.astype(BF)
    pair = stack_rows([stream] + [send(stream, along_z(k), FIRST) for k in (1, 2, 3)])

    pair = send(pair, other_section)
    other = send(pair, other_core)
    stream_own = pair[:rows]
    other = after(other, came[3])
    blocks = swap_dp(pre_part(place, 1, pair, other, w_parts))
    ready, acted_mine = grad_pre_later(blocks, grad_mine, grad_theirs, width)
    grad_pre = swap_dp(ready).reshape(tokens, hidden + 128)
    mine, arrived = scatter_tensor(*back_part(place, 1, grad_pre, w_parts))
    later_grad = norm_back(mine, arrived, cot_own, stream_own, grad_pre[:rows, hidden:])

    returned = send(later_grad, other_section)
    own_grad = jnp.where(first, returned, later_grad)
    grad_all = gather_tensor(own_grad)
    acted_theirs = send(after(acted_mine, grad_all), other_half_row, LATER)
    grad_pre_theirs = send(after(grad_pre, grad_all), other_half, LATER)
    ready = grad_spread(place, grad_all, w_out, acted_mine)
    blocks = swap_dp(ready)
    acted_mine_all = blocks.reshape(tokens, hidden)
    ready = grad_pre_first(place, blocks, pre_first, columns, acted_theirs)
    blocks = swap_dp(after(ready, grad_pre_theirs)).reshape(tokens, hidden + 128)
    out_grad, in_grad = products_early(
        place, acted_first, grad_all, pair, other, grad_pre, grad_pre_theirs
    )
    blocks = after(blocks, out_grad)
    mine, arrived = scatter_tensor(*back_part(place, 0, blocks, [w_in]))
    out_grad, in_grad = products_late(
        place, out_grad, in_grad, lead_pair, lead_other, acted_first, blocks, acted_mine_all,
        cot_padded,
    )
    result = norm_back(
        mine, arrived, own_grad, inputs, acted_first[:rows, hidden:],
        (place, stored_order, grad_all),
    )
    return (result[None], in_grad[None], out_grad[None])


def solution(mesh):
    return jax.shard_map(
        body,
        mesh=mesh,
        in_specs=(
            P("tensor", "dp"),
            P("tensor", "dp"),
            P("section", "dp", "tensor"),
            P("section", "tensor", "dp"),
        ),
        out_specs=(
            P("section", "tensor", "dp"),
            P("section", "dp", "tensor"),
            P("section", "tensor", "dp"),
        ),
        check_vma=False,
    )
```

```python
import jax
import jax.numpy as jnp
from jax import lax
from jax.experimental import pallas as pl
from jax.experimental.layout import Layout, with_layout_constraint
from jax.experimental.pallas import tpu as pltpu
from jax.sharding import PartitionSpec as P

D = 9216
EPSILON = 1e-05
AXES = ("section", "dp", "tensor")
BF = jnp.bfloat16
F32 = jnp.float32
FIRST = (0,)
LATER = (1,)
BOTH = (0, 1)
MIB = 2**20


def by_rows(value):
    return with_layout_constraint(value, Layout(major_to_minor=tuple(range(value.ndim))))


def send(value, move, sections=BOTH):
    pairs = []
    for s in sections:
        for d in range(8):
            for t in range(8):
                s2, d2, t2 = move(s, d, t)
                pairs.append(((s * 8 + d) * 8 + t, (s2 * 8 + d2) * 8 + t2))
    return by_rows(lax.ppermute(by_rows(value), AXES, pairs))


def along_x(k):
    return lambda s, d, t: (s, d // 4 * 4 + (d + k) % 4, t)


def along_z(k):
    return lambda s, d, t: (s, d, (t + 2 * k) % 8)


def other_core(s, d, t):
    return (s, d, t ^ 1)


def other_half(s, d, t):
    return (s, d, t ^ 4)


def other_half_row(s, d, t):
    return (s, d // 4 * 4 + (d + 2) % 4, t ^ 4)


def other_section(s, d, t):
    return (1 - s, d, t)


def dot(left, right, dims=((1,), (0,))):
    return lax.dot_general(left, right, (dims, ((), ())), preferred_element_type=F32)


VMEM = pl.BlockSpec(memory_space=pltpu.VMEM)
HBM = pl.BlockSpec(memory_space=pltpu.HBM)
SMEM = pl.BlockSpec(memory_space=pltpu.SMEM)


def kernel_call(kernel, out_shape, in_specs, out_specs, work, limit=4, **more):
    flops, moved = work
    return pl.pallas_call(
        kernel,
        out_shape=out_shape,
        in_specs=in_specs,
        out_specs=out_specs,
        compiler_params=pltpu.CompilerParams(vmem_limit_bytes=limit * MIB),
        cost_estimate=pl.CostEstimate(flops=flops, bytes_accessed=moved, transcendentals=0),
        **more,
    )


def blank(*shape):
    return kernel_call(lambda out: None, jax.ShapeDtypeStruct(shape, BF), [], HBM, (0, 0))()


def stream_plan(parts, turned):
    rows = sum(part.shape[0] for part in parts)
    cols = parts[0].shape[1]
    width = rows if turned else cols
    ends = [width // 3 if width > 1536 else 4 * width // 9, width]
    chunks = list(zip([0] + ends[:-1], ends))
    pieces = []
    for number, (at, end) in enumerate(chunks):
        row = 0
        for index, part in enumerate(parts):
            low, high = row, row + part.shape[0]
            row = high
            if turned:
                low, high = max(at, low), min(end, high)
            if low < high:
                pieces.append((number, index, low, high))
    return rows, cols, chunks, pieces, turned


def stream_copies(plan, parts, held, sems, turn=0):
    rows, cols, chunks, pieces, turned = plan
    first_rows = [0]
    for part in parts:
        first_rows.append(first_rows[-1] + part.shape[0])
    copies = []
    for sem, (number, index, low, high) in enumerate(pieces):
        at, end = (0, cols) if turned else chunks[number]
        begin = first_rows[index]
        to = low if isinstance(turn, int) else pl.multiple_of(lax.rem(low + turn, rows), 16)
        copy = pltpu.make_async_copy(
            parts[index].at[pl.ds(low - begin, high - low), pl.ds(at, end - at)],
            held.at[pl.ds(to, high - low), pl.ds(at, end - at)],
            sems.at[sem],
        )
        copies.append((number, copy))
    return copies


def grad_spread(place, x, w, own):
    plan = stream_plan([w], True)
    rows, cols, chunks, pieces, _ = plan
    tokens = x.shape[0]
    part = tokens // 8

    def kernel(place_ref, x_ref, w_ref, own_ref, out, held, buf, sems, out_sems):
        @pl.when(place_ref[0] == 0)
        def _():
            copies = stream_copies(plan, [w_ref], held, sems)
            for _, copy in copies:
                copy.start()
            left = x_ref[...]
            outs = []
            for number, (at, end) in enumerate(chunks):
                copies[number][1].wait()
                made = dot(left, held[at:end, :], ((1,), (1,))).astype(BF)
                buf[:, :, at:end] = made.reshape(8, part, end - at)
                lanes = pl.ds(at, end - at)
                copy = pltpu.make_async_copy(
                    buf.at[:, :, lanes], out.at[:, :, lanes], out_sems.at[number]
                )
                copy.start()
                outs.append(copy)
            for copy in outs:
                copy.wait()

        @pl.when(place_ref[0] == 1)
        def _():
            outs = [
                pltpu.make_async_copy(own_ref, out.at[j], out_sems.at[j]) for j in range(8)
            ]
            for copy in outs:
                copy.start()
            for copy in outs:
                copy.wait()

    return kernel_call(
        kernel,
        jax.ShapeDtypeStruct((8, part, rows), BF),
        [SMEM, VMEM, HBM, VMEM],
        HBM,
        (2 * tokens * rows * cols, 2 * (rows * cols + tokens * (rows + cols))),
        limit=10,
        scratch_shapes=[
            pltpu.VMEM((rows, cols), BF),
            pltpu.VMEM((8, part, rows), BF),
            pltpu.SemaphoreType.DMA((len(pieces),)),
            pltpu.SemaphoreType.DMA((8,)),
        ],
    )(place, x, w, own)


ROOT = 0.7978845608028654
CUBE = 0.044715


def gelu_parts(v):
    bent = jnp.tanh(ROOT * (v + CUBE * v * v * v))
    slope = 0.5 * (1.0 + bent) + 0.5 * v * (1.0 - bent * bent) * ROOT * (1.0 + 3.0 * CUBE * v * v)
    return 0.5 * v * (1.0 + bent), slope


def two_terms(value):
    top = value.astype(BF).astype(F32)
    return top, value - top


def lane_pack(columns):
    rows = columns[0].shape[0]
    lane = lax.broadcasted_iota(jnp.int32, (rows, 128), 1)
    block = jnp.zeros((rows, 128), F32)
    for number, column in enumerate(columns):
        block = jnp.where(lane == number, column, block)
    return block


def sums_pack(mean, inv, one, two):
    pairs = [two_terms(c) for c in (mean, inv, one, two)]
    return lane_pack([p[0] for p in pairs] + [p[1] for p in pairs]).astype(BF)


def stats_row(columns, rows):
    row = lax.broadcasted_iota(jnp.int32, (rows, 128), 0)
    lane = lax.broadcasted_iota(jnp.int32, (rows, 128), 1)
    block = jnp.zeros((rows, 128), F32)
    for number, column in enumerate(columns):
        block = jnp.where(lane == number * rows + row, column, block)
    return jnp.sum(block, axis=0, keepdims=True)


def norm_stats(beside, width, at):
    rows = beside.shape[1]
    row = lax.broadcasted_iota(jnp.int32, (rows, 128), 0)
    lane = lax.broadcasted_iota(jnp.int32, (rows, 128), 1)
    group = lane // rows

    def column(d, low, high):
        mask = (lane % rows == row) & (group >= low) & (group < high)
        line = jnp.broadcast_to(beside[d, at : at + 1, :], (rows, 128))
        return jnp.sum(jnp.where(mask, line, 0.0), axis=1, keepdims=True)

    shifts = [column(d, 0, 1) for d in range(8)]
    means = [column(d, 0, 2) for d in range(8)]
    mean = sum(means) / 8
    square = sum(column(d, 2, 4) + width * (means[d] - mean) ** 2 for d in range(8))
    inv = lax.rsqrt(square / D + EPSILON)
    return mean, inv, [shift - mean for shift in shifts]


def norm_sum(blocks_ref, beside, moves, inv, g):
    rows = beside.shape[1]
    lanes = slice(g * 128, (g + 1) * 128)
    pre = jnp.zeros((rows, 128), F32)
    columns = jnp.zeros((1, 128), F32)
    for d in range(8):
        column = beside[d, g : g + 1, :]
        columns = columns + column
        pre = pre + blocks_ref[d, :, lanes].astype(F32) + moves[d] * column
    return pre * inv, columns


def send_all(block, ready, sems, meanwhile=None):
    copies = [pltpu.make_async_copy(block, ready.at[j], sems.at[j]) for j in range(8)]
    for copy in copies:
        copy.start()
    if meanwhile is not None:
        meanwhile()
    for copy in copies:
        copy.wait()


def spread_first(place, swapped, part_b, width):
    _, rows, wide = swapped.shape
    hidden = wide - 128

    def kernel(
        place_ref, swapped_ref, part_ref, kept_out, ready_ref, sum_ref,
        total_ref, columns_ref, held, sems, out_sems,
    ):
        @pl.when(place_ref[0] == 0)
        def _():
            beside = swapped_ref[:, :, hidden:].astype(F32)
            mean, inv, moves = norm_stats(beside, width, hidden // 128)
            for g in range(hidden // 128):
                lanes = slice(g * 128, (g + 1) * 128)
                pre, columns = norm_sum(swapped_ref, beside, moves, inv, g)
                total_ref[:, lanes] = pre
                columns_ref[:, lanes] = jnp.broadcast_to(columns, (8, 128))
                held[:, lanes] = gelu_parts(pre)[0].astype(BF)
            held[:, hidden:] = sums_pack(mean, inv, mean, mean)
            copies = [
                pltpu.make_async_copy(total_ref, kept_out.at[pl.ds(0, rows)], out_sems.at[0]),
                pltpu.make_async_copy(columns_ref, kept_out.at[pl.ds(rows, 8)], out_sems.at[1]),
            ]
            for copy in copies:
                copy.start()
            send_all(held, ready_ref, sems)
            for copy in copies:
                copy.wait()

        @pl.when(place_ref[0] == 1)
        def _():
            for g in range(hidden // 128):
                lanes = slice(g * 128, (g + 1) * 128)
                total = swapped_ref[0, :, lanes].astype(F32)
                for j in range(1, 8):
                    total = total + swapped_ref[j, :, lanes].astype(F32)
                sum_ref[:, lanes] = total.astype(BF)

    return kernel_call(
        kernel,
        [
            jax.ShapeDtypeStruct((240 * rows, hidden), F32),
            jax.ShapeDtypeStruct((8, rows, hidden + 128), BF),
            jax.ShapeDtypeStruct((rows, hidden), BF),
        ],
        [SMEM, VMEM, HBM],
        [HBM, HBM, VMEM],
        (30 * rows * hidden, 40 * rows * hidden),
        input_output_aliases={2: 1},
        scratch_shapes=[
            pltpu.VMEM((rows, hidden), F32),
            pltpu.VMEM((8, hidden), F32),
            pltpu.VMEM((rows, hidden + 128), BF),
            pltpu.SemaphoreType.DMA((8,)),
            pltpu.SemaphoreType.DMA((2,)),
        ],
    )(place, swapped, part_b)


def branch_first(place, blocks, w_out):
    _, rows, wide = blocks.shape
    hidden = w_out.shape[0]
    tokens = 8 * rows
    plan = stream_plan([w_out], False)
    _, width, chunks, pieces, _ = plan

    def kernel(place_ref, x_ref, w_ref, low, high, total_ref, held, sems):
        @pl.when(place_ref[0] == 0)
        def _():
            copies = stream_copies(plan, [w_ref], held, sems)
            for _, copy in copies:
                copy.start()
            left = x_ref[:, :, :hidden].reshape(tokens, hidden)
            for number, (at, end) in enumerate(chunks):
                copies[number][1].wait()
                made = dot(left, held[:, at:end]).astype(BF)
                low[:, at:end] = made[: tokens // 2]
                high[:, at:end] = made[tokens // 2 :]

        @pl.when(place_ref[0] == 1)
        def _():
            for g in range(hidden // 128):
                lanes = slice(g * 128, (g + 1) * 128)
                total = x_ref[0, :, lanes].astype(F32)
                for j in range(1, 8):
                    total = total + x_ref[j, :, lanes].astype(F32)
                total_ref[:, lanes] = total

    return kernel_call(
        kernel,
        [
            jax.ShapeDtypeStruct((tokens // 2, width), BF),
            jax.ShapeDtypeStruct((tokens // 2, width), BF),
            jax.ShapeDtypeStruct((rows, hidden), F32),
        ],
        [SMEM, VMEM, HBM],
        [VMEM] * 3,
        (2 * tokens * hidden * width, 2 * hidden * width),
        limit=9,
        scratch_shapes=[
            pltpu.VMEM((hidden, width), BF),
            pltpu.SemaphoreType.DMA((len(pieces),)),
        ],
    )(place, blocks, w_out)


def pre_part(place, section, pair, other, w_parts):
    quarter, width = pair.shape
    tokens = 2 * quarter
    rows = tokens // 8
    plan = stream_plan(w_parts, False)
    _, hidden, chunks, pieces, _ = plan

    def kernel(place_ref, pair_ref, other_ref, *refs):
        part_refs, (out, held, left, buf, sems, out_sems) = refs[: len(w_parts)], refs[len(w_parts) :]

        @pl.when(place_ref[0] == section)
        def _():
            turn = place_ref[1] * (width // 2) if section == 1 else 0
            copies = stream_copies(plan, part_refs, held, sems, turn)
            for _, copy in copies:
                copy.start()
            lines = []
            for e, ref in enumerate((pair_ref, other_ref)):
                spread = ref[...].astype(F32)
                mean = jnp.sum(spread, axis=1, keepdims=True) / width
                off = spread - mean
                square = jnp.sum(off * off, axis=1, keepdims=True)
                shift = mean.astype(BF).astype(F32)
                left[e * quarter : (e + 1) * quarter, :] = (spread - shift).astype(BF)
                columns = [*two_terms(mean), *two_terms(square)]
                for k in range(4):
                    part = slice(k * rows, (k + 1) * rows)
                    lines.append(stats_row([column[part] for column in columns], rows))
            left[tokens:, :] = jnp.ones((16, width), BF)
            tops, outs = [], []

            def leave(at, end):
                lanes = pl.ds(at, end - at)
                copy = pltpu.make_async_copy(
                    buf.at[:, :, lanes], out.at[:, :, lanes], out_sems.at[len(outs)]
                )
                copy.start()
                outs.append(copy)

            for number, (at, end) in enumerate(chunks):
                for begun, copy in copies:
                    if begun == number:
                        copy.wait()
                made = dot(left[...], held[:, at:end])
                buf[:, :, at:end] = made[:tokens].astype(BF).reshape(8, rows, end - at)
                leave(at, end)
                sums = made[tokens : tokens + 1]
                for g in range((end - at) // 128):
                    tops.append(sums[:, g * 128 : (g + 1) * 128])
            empty = jnp.zeros((rows - len(tops) - 1, 128), F32)
            for j in range(8):
                block = jnp.concatenate([*tops, lines[j], empty], axis=0)
                buf[j, :, hidden:] = block.astype(BF)
            leave(hidden, hidden + 128)
            for copy in outs:
                copy.wait()

    return kernel_call(
        kernel,
        jax.ShapeDtypeStruct((8, rows, hidden + 128), BF),
        [SMEM, VMEM, VMEM] + [HBM] * len(w_parts),
        HBM,
        (2 * tokens * hidden * width, 2 * hidden * width),
        limit=14,
        scratch_shapes=[
            pltpu.VMEM((width, hidden), BF),
            pltpu.VMEM((tokens + 16, width), BF),
            pltpu.VMEM((8, rows, hidden + 128), BF),
            pltpu.SemaphoreType.DMA((len(pieces),)),
            pltpu.SemaphoreType.DMA((len(chunks) + 1,)),
        ],
    )(place, pair, other, *w_parts)


def weave(turned):
    row = lax.broadcasted_iota(jnp.int32, (256, 256), 0)
    lane = lax.broadcasted_iota(jnp.int32, (256, 256), 1)
    if turned:
        row, lane = lane, row
    return jnp.where(lane == 2 * (row % 128) + row // 128, 1.0, 0.0).astype(BF)


def grad_pre_later(blocks, grad_mine, grad_theirs, width):
    _, rows, wide = blocks.shape
    hidden = wide - 128
    plane = hidden // 2

    def kernel(blocks_ref, mine_ref, theirs_ref, ready, acted_ref, grad_ref, held_ref, own, sems):
        order, back = weave(False), weave(True)
        for b in range(hidden // 256):
            pair = []
            for q in (0, 1):
                lanes = slice(q * plane + b * 128, q * plane + (b + 1) * 128)
                pair.append(mine_ref[:, lanes] + theirs_ref[:, lanes].astype(F32))
            top, rest = two_terms(jnp.concatenate(pair, axis=1))
            done = dot(top.astype(BF), order) + dot(rest.astype(BF), order)
            grad_ref[:, b * 256 : (b + 1) * 256] = done
        beside = blocks_ref[:, :, hidden:].astype(F32)
        mean, inv, moves = norm_stats(beside, width, hidden // 128)
        one = jnp.zeros((rows, 1), F32)
        two = jnp.zeros((rows, 1), F32)
        for g in range(hidden // 128):
            lanes = slice(g * 128, (g + 1) * 128)
            pre, columns = norm_sum(blocks_ref, beside, moves, inv, g)
            acted, slope = gelu_parts(pre)
            held_ref[:, lanes] = acted.astype(BF)
            grad = (grad_ref[:, lanes] * slope).astype(BF)
            own[:, lanes] = grad
            grad = grad.astype(F32)
            one = one + jnp.sum(grad * columns, axis=1, keepdims=True)
            two = two + jnp.sum(grad * pre, axis=1, keepdims=True)
        own[:, hidden:] = sums_pack(mean, inv, one, two)

        def reorder():
            for b in range(hidden // 256):
                done = dot(held_ref[:, b * 256 : (b + 1) * 256], back).astype(BF)
                acted_ref[:, b * 128 : (b + 1) * 128] = done[:, :128]
                acted_ref[:, plane + b * 128 : plane + (b + 1) * 128] = done[:, 128:]

        send_all(own, ready, sems, reorder)

    return kernel_call(
        kernel,
        [
            jax.ShapeDtypeStruct((8, rows, hidden + 128), BF),
            jax.ShapeDtypeStruct((rows, hidden), BF),
        ],
        [VMEM] * 3,
        [HBM, VMEM],
        (80 * rows * hidden, 40 * rows * hidden),
        scratch_shapes=[
            pltpu.VMEM((rows, hidden), F32),
            pltpu.VMEM((rows, hidden), BF),
            pltpu.VMEM((rows, hidden + 128), BF),
            pltpu.SemaphoreType.DMA((8,)),
        ],
    )(blocks, grad_mine, grad_theirs)


def grad_pre_first(place, blocks, kept, theirs):
    _, rows, hidden = blocks.shape

    def kernel(
        place_ref, blocks_ref, kept_ref, theirs_ref, ready,
        pre_ref, columns_ref, own, sems,
    ):
        @pl.when(place_ref[0] == 0)
        def _():
            fetched(
                (kept_ref.at[pl.ds(0, rows)], kept_ref.at[pl.ds(rows, 8)]),
                (pre_ref, columns_ref),
                sems,
            )
            one = jnp.zeros((rows, 1), F32)
            two = jnp.zeros((rows, 1), F32)
            for g in range(hidden // 128):
                lanes = slice(g * 128, (g + 1) * 128)
                total = blocks_ref[0, :, lanes].astype(F32)
                for j in range(1, 8):
                    total = total + blocks_ref[j, :, lanes].astype(F32)
                pre = pre_ref[:, lanes]
                grad = (total * gelu_parts(pre)[1]).astype(BF)
                own[:, lanes] = grad
                grad = grad.astype(F32)
                one = one + jnp.sum(grad * columns_ref[0:1, lanes], axis=1, keepdims=True)
                two = two + jnp.sum(grad * pre, axis=1, keepdims=True)
            own[:, hidden:] = sums_pack(one, one, one, two)

        @pl.when(place_ref[0] == 1)
        def _():
            fetched((theirs_ref,), (own.at[:, pl.ds(0, hidden)],), sems)
            own[:, hidden:] = jnp.zeros((rows, 128), BF)

        send_all(own, ready, sems)

    return kernel_call(
        kernel,
        jax.ShapeDtypeStruct((8, rows, hidden + 128), BF),
        [SMEM, VMEM] + [HBM] * 2,
        HBM,
        (60 * rows * hidden, 40 * rows * hidden),
        scratch_shapes=[
            pltpu.VMEM((rows, hidden), F32),
            pltpu.VMEM((8, hidden), F32),
            pltpu.VMEM((rows, hidden + 128), BF),
            pltpu.SemaphoreType.DMA((8,)),
        ],
    )(place, blocks, kept, theirs)


def back_part(place, section, grad_pre, w_parts):
    tokens, wide = grad_pre.shape
    hidden = wide - 128
    plan = stream_plan(w_parts, True)
    width, _, chunks, pieces, _ = plan

    def kernel(place_ref, x_ref, *refs):
        w_refs, (low, high, held, made, sems) = refs[: len(w_parts)], refs[len(w_parts) :]

        @pl.when(place_ref[0] == section)
        def _():
            copies = stream_copies(plan, w_refs, held, sems)
            for _, copy in copies:
                copy.start()
            left = x_ref[:, :hidden]
            for number, (at, end) in enumerate(chunks):
                for begun, copy in copies:
                    if begun == number:
                        copy.wait()
                made[:, at:end] = dot(left, held[at:end, :], ((1,), (1,)))
            done = made[...]
            if section == 1:
                done = jnp.where(place_ref[1] == 0, done, pltpu.roll(done, width // 2, 1))
            done = done.astype(BF)
            for number, out in enumerate((low, high)):
                part = slice(number * tokens // 2, (number + 1) * tokens // 2)
                out[:, :width] = done[part]
                out[:, width:] = x_ref[part, hidden:]

    return kernel_call(
        kernel,
        [jax.ShapeDtypeStruct((tokens // 2, width + 128), BF)] * 2,
        [SMEM, VMEM] + [HBM] * len(w_parts),
        [VMEM] * 2,
        (2 * tokens * hidden * width, 2 * hidden * width),
        limit=12,
        scratch_shapes=[
            pltpu.VMEM((width, hidden), BF),
            pltpu.VMEM((tokens, width), F32),
            pltpu.SemaphoreType.DMA((len(pieces),)),
        ],
    )(place, grad_pre, *w_parts)


def joined_sums(block):
    return block + pltpu.roll(block, 124, 1)


def core_sum(low, arrived):
    quarter, wide = low.shape
    width = wide - 128
    rows = quarter // 4

    def kernel(low_ref, arrived_ref, mine, stats, *ready):
        stats[...] = low_ref[:rows, width:]
        for k in range(4):
            part = slice(k * rows, (k + 1) * rows)
            total = low_ref[part, :width].astype(F32) + arrived_ref[part, :width].astype(F32)
            sums = joined_sums(low_ref[part, width:].astype(F32))
            sums = sums + joined_sums(arrived_ref[part, width:].astype(F32))
            if k == 0:
                mine[:, :width] = total
                mine[:, width:] = sums
            else:
                ready[k - 1][:, :width] = total.astype(BF)
                top, rest = two_terms(sums)
                lane = lax.broadcasted_iota(jnp.int32, (rows, 128), 1)
                ready[k - 1][:, width:] = jnp.where(lane < 4, top, pltpu.roll(rest, 4, 1)).astype(BF)

    return kernel_call(
        kernel,
        [jax.ShapeDtypeStruct((rows, wide), F32), jax.ShapeDtypeStruct((rows, 128), BF)]
        + [jax.ShapeDtypeStruct((rows, wide), BF)] * 3,
        [VMEM] * 2,
        [VMEM] * 5,
        (2 * quarter * wide, 8 * quarter * wide),
    )(low, arrived)


def norm_back(mine, arrived, grad_out, stream, stats, tail=None):
    rows, wide = mine.shape
    width = wide - 128
    extra = () if tail is None else tail

    def kernel(mine_ref, one, two, three, grad_ref, stream_ref, stats_ref, *refs):
        out = refs[-1]

        def fill():
            total = mine_ref[:, :width]
            sums = mine_ref[:, width:]
            for ref in (one, two, three):
                total = total + ref[:, :width].astype(F32)
                sums = sums + joined_sums(ref[:, width:].astype(F32))
            stats = joined_sums(stats_ref[...].astype(F32))
            mean, inv = stats[:, 0:1], stats[:, 1:2]
            centred = (stream_ref[...].astype(F32) - mean) * inv
            grad = total - sums[:, 2:3] / D - centred * (sums[:, 3:4] / D)
            out[...] = (grad_ref[...].astype(F32) + inv * grad).astype(BF)

        if tail is None:
            fill()
            return
        place_ref, order_ref, whole_ref = refs[:3]
        pl.when(place_ref[0] == 0)(fill)

        @pl.when(place_ref[0] == 1)
        def _():
            chosen = dot(order_ref[...], whole_ref[...])
            turned = pltpu.roll(chosen, width // 2, 1)
            lane = lax.broadcasted_iota(jnp.int32, (rows, width), 1)
            own = place_ref[1] == 0
            left = jnp.where(own, chosen[:rows], turned[:rows])
            right = jnp.where(own, turned[rows:], chosen[rows:])
            out[...] = jnp.where(lane < width // 2, left, right).astype(BF)

    specs = [VMEM] * 7 + ([SMEM, VMEM, VMEM] if extra else [])
    return kernel_call(
        kernel,
        jax.ShapeDtypeStruct((rows, width), BF),
        specs,
        VMEM,
        (20 * rows * wide, 20 * rows * wide),
    )(mine, *arrived, grad_out, stream, stats, *extra)


def scatter_tensor(low, high):
    mine, stats, *ready = core_sum(low, send(high, other_core))
    return mine, stats, [send(block, along_z(-k)) for k, block in zip((1, 2, 3), ready)]


def split_planes(w, pick, sizes):
    height, width = w.shape
    part = height // 2
    block = pick.shape[0]
    sub = block // 2

    def kernel(w_ref, pick_ref, kept, *refs):
        away, (held, planes, sems, out_sem) = refs[: len(sizes)], refs[len(sizes) :]
        steps = height // block
        copies = [
            pltpu.make_async_copy(
                w_ref.at[pl.ds(at * block, block)], held.at[pl.ds(at * block, block)], sems.at[at]
            )
            for at in range(steps)
        ]
        for copy in copies:
            copy.start()
        outs, piece, begun = [], 0, 0
        for at, copy in enumerate(copies):
            copy.wait()
            rows = dot(pick_ref[...], held[at * block : (at + 1) * block, :]).astype(BF)
            planes[0, at * sub : (at + 1) * sub, :] = rows[:sub]
            planes[1, at * sub : (at + 1) * sub, :] = rows[sub:]
            if (at + 1) * sub == begun + sizes[piece]:
                lines = pl.ds(begun, sizes[piece])
                for plane, ref in enumerate((kept.at[lines], away[piece])):
                    out = pltpu.make_async_copy(
                        planes.at[plane, lines], ref, out_sem.at[2 * piece + plane]
                    )
                    out.start()
                    outs.append(out)
                begun += sizes[piece]
                piece += 1
        for out in outs:
            out.wait()

    shapes = [jax.ShapeDtypeStruct((size, width), BF) for size in (part, *sizes)]
    return kernel_call(
        kernel,
        shapes,
        [HBM, VMEM],
        [HBM] * (1 + len(sizes)),
        (2 * height * width * block, 4 * height * width),
        limit=13,
        scratch_shapes=[
            pltpu.VMEM((height, width), BF),
            pltpu.VMEM((2, part, width), BF),
            pltpu.SemaphoreType.DMA((height // block,)),
            pltpu.SemaphoreType.DMA((2 * len(sizes),)),
        ],
    )(w, pick)


def cot_spread(place, pair, other, w_out, beside):
    quarter, width = pair.shape
    tokens = 2 * quarter
    hidden = w_out.shape[0]
    plane, part, rows = hidden // 2, width // 2, tokens // 8

    def kernel(
        place_ref, pair_ref, other_ref, w_ref, rest, own, padded, slot_ref,
        held, buf, made_ref, sems, out_sems,
    ):
        half, z_at, core_at = place_ref[1], place_ref[2], place_ref[3]
        copies = []
        for i in range(2):
            row = pl.multiple_of((half ^ (1 - i)) * plane, 16)
            copy = pltpu.make_async_copy(w_ref.at[pl.ds(row, plane)], held.at[i], sems.at[i])
            copy.start()
            copies.append(copy)

        def chosen(count, near):
            to = lax.broadcasted_iota(jnp.int32, (count, quarter), 0)
            by = lax.broadcasted_iota(jnp.int32, (count, quarter), 1)
            to_z = (z_at + 4 - to // rows % 4) & 3
            to_token = (to_z * 2 + (core_at ^ (to // quarter))) * rows + to % rows
            by_z = (z_at + 4 - by // rows) & 3
            in_half = (by_z // 2) == (half if near else 1 - half)
            planes = []
            for q in (0, 1):
                total = jnp.zeros((count, width), F32)
                for e, ref in enumerate((pair_ref, other_ref)):
                    block = by_z % 2 * 2 + (core_at ^ e)
                    token = block * 2 * rows + 2 * (by % rows) + q
                    pick = jnp.where((token == to_token) & in_half, 1.0, 0.0).astype(BF)
                    total = total + dot(pick, ref[...])
                planes.append(total)
            lane = lax.broadcasted_iota(jnp.int32, (count, width), 1)
            return jnp.where(lane < part, planes[0] + pltpu.roll(planes[1], part, 1), 0.0)

        mine = chosen(tokens, True)
        made_ref[0] = mine.astype(BF)
        made_ref[1] = pltpu.roll(mine, part, 1).astype(BF)
        left, right = mine[:rows], chosen(rows, False)
        left, right = jnp.where(half == 0, left, right), jnp.where(half == 0, right, left)
        slot_ref[...] = (left + pltpu.roll(right, part, 1)).astype(BF)
        outs = [pltpu.make_async_copy(made_ref, padded, out_sems.at[2])]
        outs[0].start()
        for i, ref in enumerate((rest, own)):
            copies[i].wait()
            for q in (0, 1):
                made = dot(made_ref[q], held[i], ((1,), (1,))).astype(BF)
                buf[i, :, :, q * plane : (q + 1) * plane] = made.reshape(8, rows, plane)
            copy = pltpu.make_async_copy(buf.at[i], ref.at[:, :, pl.ds(0, hidden)], out_sems.at[i])
            copy.start()
            outs.append(copy)
        for copy in outs:
            copy.wait()

    return kernel_call(
        kernel,
        [jax.ShapeDtypeStruct((8, rows, hidden + extra), BF) for extra in beside]
        + [
            jax.ShapeDtypeStruct((2, tokens, width), BF),
            jax.ShapeDtypeStruct((rows, width), BF),
        ],
        [SMEM, VMEM, VMEM, HBM],
        [HBM, HBM, HBM, VMEM],
        (4 * tokens * hidden * width, 2 * hidden * width),
        limit=18,
        scratch_shapes=[
            pltpu.VMEM((2, plane, width), BF),
            pltpu.VMEM((2, 8, rows, hidden), BF),
            pltpu.VMEM((2, tokens, width), BF),
            pltpu.SemaphoreType.DMA((2,)),
            pltpu.SemaphoreType.DMA((3,)),
        ],
    )(place, pair, other, w_out)


def fill_rows(out, buf, sems, tiles):
    copies = []
    for number, (row, count, make) in enumerate(tiles):
        slot = number % 2
        if number >= 2:
            copies[number - 2].wait()
        lines = pl.ds(0, count)
        buf[slot, 0:count, :] = make().astype(BF)
        copy = pltpu.make_async_copy(buf.at[slot, lines], out.at[pl.ds(row, count)], sems.at[slot])
        copy.start()
        copies.append(copy)
    for copy in copies[-2:]:
        copy.wait()


def two_tiles(width):
    cut = (width // 128 + 1) // 2 * 128 if width >= 512 else width // 2
    return [(0, cut), (cut, width)]


def fetched(refs, bufs, sems):
    copies = [
        pltpu.make_async_copy(ref, buf, sems.at[number])
        for number, (ref, buf) in enumerate(zip(refs, bufs))
    ]
    for copy in copies:
        copy.start()
    for copy in copies:
        copy.wait()


def normed_rows(ref, beside, half):
    stats = joined_sums(beside.astype(F32))
    normed = (ref[...].astype(F32) - stats[:, 0:1]) * stats[:, 1:2]
    if half is not None:
        normed = jnp.where(half == 0, normed, pltpu.roll(normed, normed.shape[1] // 2, 1))
    return normed.astype(BF)


def products_early(place, acted, grad_all, pair, other, grad_pre, theirs):
    tokens, wide = acted.shape
    hidden = wide - 128
    width = grad_all.shape[1]
    part = width // 2
    quarter = tokens // 2

    def kernel(
        place_ref, acted_ref, grad_ref, pair_ref, other_ref, pre_ref, theirs_ref,
        out_ref, in_ref, hold_one, hold_two, hold_three, hold_pair, lefts,
        out_buf, in_buf, sems, out_sems, in_sems,
    ):
        @pl.when(place_ref[0] == 0)
        def _():
            fetched((acted_ref, grad_ref), (hold_one, hold_three), sems)
            def make(at, end):
                return lambda: dot(hold_one[:, at:end], hold_three[...], ((0,), (0,)))

            cuts = two_tiles(hidden)
            fill_rows(
                out_ref, out_buf, out_sems, [(at, end - at, make(at, end)) for at, end in cuts]
            )

        @pl.when(place_ref[0] == 1)
        def _():
            fetched(
                (pair_ref, other_ref, pre_ref, theirs_ref),
                (hold_pair.at[0], hold_pair.at[1], hold_one, hold_two),
                sems,
            )
            half = place_ref[1]
            row = lax.broadcasted_iota(jnp.int32, (128, 256), 0)
            lane = lax.broadcasted_iota(jnp.int32, (128, 256), 1)
            picks = [
                jnp.where(lane == 2 * row + plane, 1.0, 0.0).astype(BF)
                for plane in (half, 1 - half)
            ]
            for e in range(2):
                rows = slice(e * quarter, (e + 1) * quarter)
                normed = normed_rows(hold_pair.at[e], hold_one[rows, hidden:], half)
                for b in range(-(-part // 128)):
                    end = min(256 * (b + 1), width)
                    for number, pick in enumerate(picks):
                        made = dot(normed[:, 128 * b : 128 * (b + 1)], pick).astype(BF)
                        made = made[:, : end - 256 * b]
                        if number == 0:
                            lefts[0, rows, 256 * b : end] = made
                        else:
                            mid, at = quarter // 2, e * quarter
                            lefts[1, at + mid : at + quarter, 256 * b : end] = made[:mid]
                            lefts[1, at : at + mid, 256 * b : end] = made[mid:]
            def make(at, end):
                def both():
                    mine = dot(lefts[0, :, at:end], hold_one[:, :hidden], ((0,), (0,)))
                    return mine + dot(lefts[1, :, at:end], hold_two[:, :hidden], ((0,), (0,)))

                return both

            cuts = two_tiles(width)
            fill_rows(in_ref, in_buf, in_sems, [(at, end - at, make(at, end)) for at, end in cuts])

    return kernel_call(
        kernel,
        [
            jax.ShapeDtypeStruct((hidden, width), BF),
            jax.ShapeDtypeStruct((width, hidden), BF),
        ],
        [SMEM] + [HBM] * 6,
        [HBM] * 2,
        (2 * tokens * hidden * width, 2 * hidden * width),
        limit=36,
        scratch_shapes=[
            pltpu.VMEM((tokens, wide), BF),
            pltpu.VMEM((tokens, wide), BF),
            pltpu.VMEM((tokens, width), BF),
            pltpu.VMEM((2, quarter, width), BF),
            pltpu.VMEM((2, tokens, width), BF),
            pltpu.VMEM((2, two_tiles(hidden)[0][1], width), BF),
            pltpu.VMEM((2, two_tiles(width)[0][1], hidden), BF),
            pltpu.SemaphoreType.DMA((4,)),
            pltpu.SemaphoreType.DMA((2,)),
            pltpu.SemaphoreType.DMA((2,)),
        ],
    )(place, acted, grad_all, pair, other, grad_pre, theirs)


def products_late(place, out_grad, in_grad, pair, other, acted, blocks, mine, padded):
    quarter, width = pair.shape
    tokens = 2 * quarter
    hidden = mine.shape[1]
    plane = hidden // 2

    def kernel(
        place_ref, out_was, in_was, pair_ref, other_ref, acted_ref, blocks_ref, mine_ref,
        padded_ref, out_ref, in_ref, hold_pair, hold_beside, hold_one, hold_two, left,
        hold_padded, out_buf, in_buf, sems, out_sems, in_sems,
    ):
        @pl.when(place_ref[0] == 0)
        def _():
            fetched(
                (pair_ref, other_ref, acted_ref.at[:, pl.ds(hidden, 128)], blocks_ref),
                (hold_pair.at[0], hold_pair.at[1], hold_beside, hold_one),
                sems,
            )
            for e in range(2):
                rows = slice(e * quarter, (e + 1) * quarter)
                left[rows, :] = normed_rows(hold_pair.at[e], hold_beside[rows], None)
            def make(at, end):
                return lambda: dot(left[:, at:end], hold_one[:, :hidden], ((0,), (0,)))

            cuts = two_tiles(width)
            fill_rows(in_ref, in_buf, in_sems, [(at, end - at, make(at, end)) for at, end in cuts])

        @pl.when(place_ref[0] == 1)
        def _():
            fetched((mine_ref, blocks_ref, padded_ref), (hold_two, hold_one, hold_padded), sems)
            def make(ref):
                def both():
                    low = dot(ref[:, :plane], hold_padded[0], ((0,), (0,)))
                    return low + dot(ref[:, plane:hidden], hold_padded[1], ((0,), (0,)))

                return both

            tiles = []
            for number, ref in enumerate((hold_two, hold_one)):
                row = pl.multiple_of((place_ref[1] ^ number) * plane, 16)
                tiles.append((row, plane, make(ref)))
            fill_rows(out_ref, out_buf, out_sems, tiles)

    return kernel_call(
        kernel,
        [
            jax.ShapeDtypeStruct((hidden, width), BF),
            jax.ShapeDtypeStruct((width, hidden), BF),
        ],
        [SMEM] + [HBM] * 8,
        [HBM] * 2,
        (2 * tokens * hidden * width, 2 * hidden * width),
        limit=36,
        input_output_aliases={1: 0, 2: 1},
        scratch_shapes=[
            pltpu.VMEM((2, quarter, width), BF),
            pltpu.VMEM((tokens, 128), BF),
            pltpu.VMEM((tokens, hidden + 128), BF),
            pltpu.VMEM((tokens, hidden), BF),
            pltpu.VMEM((tokens, width), BF),
            pltpu.VMEM((2, tokens, width), BF),
            pltpu.VMEM((2, plane, width), BF),
            pltpu.VMEM((2, two_tiles(width)[0][1], hidden), BF),
            pltpu.SemaphoreType.DMA((4,)),
            pltpu.SemaphoreType.DMA((2,)),
            pltpu.SemaphoreType.DMA((2,)),
        ],
    )(place, out_grad, in_grad, pair, other, acted, blocks, mine, padded)


def stack_rows(blocks):
    rows, width = blocks[0].shape

    def kernel(*refs):
        for number, ref in enumerate(refs[:-1]):
            refs[-1][number * rows : (number + 1) * rows, :] = ref[...]

    count = len(blocks)
    return kernel_call(
        kernel,
        jax.ShapeDtypeStruct((count * rows, width), BF),
        [VMEM] * count,
        VMEM,
        (0, 4 * count * rows * width),
    )(*blocks)


def gather_pairs(x, *others):
    pair = stack_rows([after(x, *others)] + [send(x, along_z(k)) for k in (1, 2, 3)])
    return pair, send(pair, other_core)


def gather_tensor(x):
    return stack_rows(gather_pairs(x))


def swap_dp(blocks):
    return lax.all_to_all(blocks, "dp", 0, 0, tiled=True)


def one_hot(condition):
    return condition.astype(BF)


def after(value, *others):
    return lax.optimization_barrier((value, *others))[0]


def body(inputs, cotangent, w_first, w_second):
    w_in, w_out = w_first[0], w_second[0]
    rows, width = inputs.shape
    hidden = w_in.shape[1]
    part = width // 2
    tokens = 8 * rows
    first = lax.axis_index("section") == 0
    at = lax.axis_index("tensor")
    z_at, core_at = at // 2, at % 2
    half = at // 4

    slot_row = jnp.arange(tokens)
    slot_owner = ((z_at - slot_row // rows % 4) % 4) * 2 + (core_at ^ (slot_row // (4 * rows)))
    slot_token = slot_owner * rows + slot_row % rows

    place = jnp.stack([lax.axis_index("section"), half, z_at, core_at]).astype(jnp.int32)
    place_rows = jnp.arange(2 * rows)
    stored_token = (at % 4) * 2 * rows + 2 * (place_rows % rows) + place_rows // rows
    stored_order = one_hot(stored_token[:, None] == slot_token[None, :])

    unit = part // 12
    block = 2 * unit
    index = jnp.arange(block)
    picked = 2 * (index % (block // 2)) + jnp.where(index < block // 2, half, 1 - half)
    pick = one_hot(index[None, :] == picked[:, None])
    sizes = [2 * unit, 3 * unit, 3 * unit, 4 * unit]
    kept, *away = lax.cond(
        first,
        lambda: [blank(size, hidden) for size in (part, *sizes)],
        lambda: list(split_planes(w_in, pick, sizes)),
    )

    lead_pair, lead_other = gather_pairs(jnp.where(first, inputs, cotangent), *away)
    came = [send(after(away[0], lead_other), other_half, LATER)]

    def lead_second():
        return list(cot_spread(place, lead_pair, lead_other, w_out, (128, 128)))

    def lead_first():
        made = pre_part(place, 0, lead_pair, lead_other, [w_in])
        return [made, blank(8, rows, hidden + 128), blank(2, tokens, width), blank(rows, width)]

    part_a, part_b, cot_padded, cot_own = lax.cond(first, lead_first, lead_second)
    swapped = swap_dp(after(part_a, came[0]))
    came.append(send(away[1], other_half, LATER))
    swapped = after(swapped, came[1])
    kept_first, ready, sum_theirs = spread_first(place, swapped, part_b, width)
    grad_theirs = send(sum_theirs, other_half_row, LATER)
    acted_first = swap_dp(ready)
    came.append(send(away[2], other_half, LATER))
    acted_first = after(acted_first, came[2], grad_theirs)
    low, high, grad_mine = branch_first(place, acted_first, w_out)
    came.append(send(away[3], other_half, LATER))
    acted_first = acted_first.reshape(tokens, hidden + 128)
    w_parts = [kept, *came]
    branch = low.astype(F32) + send(high, other_core).astype(F32)
    stream = inputs.astype(F32) + branch[:rows]
    for k in (1, 2, 3):
        block = branch[k * rows : (k + 1) * rows].astype(BF)
        stream = stream + send(block, along_z(-k), FIRST).astype(F32)
    stream = stream.astype(BF)
    pair = stack_rows([stream] + [send(stream, along_z(k), FIRST) for k in (1, 2, 3)])

    pair = send(pair, other_section)
    other = send(pair, other_core)
    stream_own = pair[:rows]
    other = after(other, came[3])
    blocks = swap_dp(pre_part(place, 1, pair, other, w_parts))
    ready, acted_mine = grad_pre_later(blocks, grad_mine, grad_theirs, width)
    grad_pre = swap_dp(ready).reshape(tokens, hidden + 128)
    mine, stats, arrived = scatter_tensor(*back_part(place, 1, grad_pre, w_parts))
    later_grad = norm_back(mine, arrived, cot_own, stream_own, stats)

    returned = send(later_grad, other_section)
    own_grad = jnp.where(first, returned, later_grad)
    grad_all = gather_tensor(own_grad)
    acted_theirs = send(after(acted_mine, grad_all), other_half_row, LATER)
    grad_pre_theirs = send(after(grad_pre, grad_all), other_half, LATER)
    ready = grad_spread(place, grad_all, w_out, acted_mine)
    blocks = swap_dp(ready)
    acted_mine_all = blocks.reshape(tokens, hidden)
    ready = grad_pre_first(place, blocks, kept_first, acted_theirs)
    blocks = swap_dp(after(ready, grad_pre_theirs)).reshape(tokens, hidden + 128)
    out_grad, in_grad = products_early(
        place, acted_first, grad_all, pair, other, grad_pre, grad_pre_theirs
    )
    blocks = after(blocks, out_grad)
    mine, _, arrived = scatter_tensor(*back_part(place, 0, blocks, [w_in]))
    out_grad, in_grad = products_late(
        place, out_grad, in_grad, lead_pair, lead_other, acted_first, blocks, acted_mine_all,
        cot_padded,
    )
    result = norm_back(
        mine, arrived, own_grad, inputs, acted_first[:rows, hidden:],
        (place, stored_order, grad_all),
    )
    return (result[None], in_grad[None], out_grad[None])


def solution(mesh):
    return jax.shard_map(
        body,
        mesh=mesh,
        in_specs=(
            P("tensor", "dp"),
            P("tensor", "dp"),
            P("section", "dp", "tensor"),
            P("section", "tensor", "dp"),
        ),
        out_specs=(
            P("section", "tensor", "dp"),
            P("section", "dp", "tensor"),
            P("section", "tensor", "dp"),
        ),
        check_vma=False,
    )
```

```python
import jax
import jax.numpy as jnp
from jax import lax
from jax.experimental import pallas as pl
from jax.experimental.layout import Layout, with_layout_constraint
from jax.experimental.pallas import tpu as pltpu
from jax.sharding import PartitionSpec as P

D = 9216
EPSILON = 1e-05
AXES = ("section", "dp", "tensor")
BF = jnp.bfloat16
F32 = jnp.float32
FIRST = (0,)
LATER = (1,)
BOTH = (0, 1)
MIB = 2**20


def by_rows(value):
    return with_layout_constraint(value, Layout(major_to_minor=tuple(range(value.ndim))))


def send(value, move, sections=BOTH):
    pairs = []
    for s in sections:
        for d in range(8):
            for t in range(8):
                s2, d2, t2 = move(s, d, t)
                pairs.append(((s * 8 + d) * 8 + t, (s2 * 8 + d2) * 8 + t2))
    return by_rows(lax.ppermute(by_rows(value), AXES, pairs))


def along_x(k):
    return lambda s, d, t: (s, d // 4 * 4 + (d + k) % 4, t)


def along_z(k, sections=BOTH):
    return lambda s, d, t: (s, d, (t + 2 * k) % 8 if s in sections else t ^ 1)


def other_core(s, d, t):
    return (s, d, t ^ 1)


def other_half(s, d, t):
    return (s, d, t ^ 4)


def other_half_row(s, d, t):
    return (s, d // 4 * 4 + (d + 2) % 4, t ^ 4)


def other_section(s, d, t):
    return (1 - s, d, t)


def dot(left, right, dims=((1,), (0,))):
    return lax.dot_general(left, right, (dims, ((), ())), preferred_element_type=F32)


VMEM = pl.BlockSpec(memory_space=pltpu.VMEM)
HBM = pl.BlockSpec(memory_space=pltpu.HBM)
SMEM = pl.BlockSpec(memory_space=pltpu.SMEM)


def kernel_call(kernel, out_shape, in_specs, out_specs, work, limit=4, **more):
    flops, moved = work
    return pl.pallas_call(
        kernel,
        out_shape=out_shape,
        in_specs=in_specs,
        out_specs=out_specs,
        compiler_params=pltpu.CompilerParams(vmem_limit_bytes=limit * MIB),
        cost_estimate=pl.CostEstimate(flops=flops, bytes_accessed=moved, transcendentals=0),
        **more,
    )


def blank(*shape):
    return kernel_call(lambda out: None, jax.ShapeDtypeStruct(shape, BF), [], HBM, (0, 0))()


def stream_plan(parts, turned):
    rows = sum(part.shape[0] for part in parts)
    cols = parts[0].shape[1]
    width = rows if turned else cols
    ends = [width // 3 if width > 1536 else 4 * width // 9, width]
    chunks = list(zip([0] + ends[:-1], ends))
    pieces = []
    for number, (at, end) in enumerate(chunks):
        row = 0
        for index, part in enumerate(parts):
            low, high = row, row + part.shape[0]
            row = high
            if turned:
                low, high = max(at, low), min(end, high)
            if low < high:
                pieces.append((number, index, low, high))
    return rows, cols, chunks, pieces, turned


def stream_copies(plan, parts, held, sems, turn=0):
    rows, cols, chunks, pieces, turned = plan
    first_rows = [0]
    for part in parts:
        first_rows.append(first_rows[-1] + part.shape[0])
    copies = []
    for sem, (number, index, low, high) in enumerate(pieces):
        at, end = (0, cols) if turned else chunks[number]
        begin = first_rows[index]
        to = low if isinstance(turn, int) else pl.multiple_of(lax.rem(low + turn, rows), 16)
        copy = pltpu.make_async_copy(
            parts[index].at[pl.ds(low - begin, high - low), pl.ds(at, end - at)],
            held.at[pl.ds(to, high - low), pl.ds(at, end - at)],
            sems.at[sem],
        )
        copies.append((number, copy))
    return copies


def grad_spread(place, x, w, own):
    plan = stream_plan([w], True)
    rows, cols, chunks, pieces, _ = plan
    tokens = x.shape[0]
    part = tokens // 8

    def kernel(place_ref, x_ref, w_ref, own_ref, out, held, buf, sems, out_sems):
        @pl.when(place_ref[0] == 0)
        def _():
            copies = stream_copies(plan, [w_ref], held, sems)
            for _, copy in copies:
                copy.start()
            left = x_ref[...]
            outs = []
            for number, (at, end) in enumerate(chunks):
                copies[number][1].wait()
                made = dot(left, held[at:end, :], ((1,), (1,))).astype(BF)
                buf[:, :, at:end] = made.reshape(8, part, end - at)
                lanes = pl.ds(at, end - at)
                copy = pltpu.make_async_copy(
                    buf.at[:, :, lanes], out.at[:, :, lanes], out_sems.at[number]
                )
                copy.start()
                outs.append(copy)
            for copy in outs:
                copy.wait()

        @pl.when(place_ref[0] == 1)
        def _():
            outs = [
                pltpu.make_async_copy(own_ref, out.at[j], out_sems.at[j]) for j in range(8)
            ]
            for copy in outs:
                copy.start()
            for copy in outs:
                copy.wait()

    return kernel_call(
        kernel,
        jax.ShapeDtypeStruct((8, part, rows), BF),
        [SMEM, VMEM, HBM, VMEM],
        HBM,
        (2 * tokens * rows * cols, 2 * (rows * cols + tokens * (rows + cols))),
        limit=10,
        scratch_shapes=[
            pltpu.VMEM((rows, cols), BF),
            pltpu.VMEM((8, part, rows), BF),
            pltpu.SemaphoreType.DMA((len(pieces),)),
            pltpu.SemaphoreType.DMA((8,)),
        ],
    )(place, x, w, own)


ROOT = 0.7978845608028654
CUBE = 0.044715


def gelu_parts(v):
    bent = jnp.tanh(ROOT * (v + CUBE * v * v * v))
    slope = 0.5 * (1.0 + bent) + 0.5 * v * (1.0 - bent * bent) * ROOT * (1.0 + 3.0 * CUBE * v * v)
    return 0.5 * v * (1.0 + bent), slope


def two_terms(value):
    top = value.astype(BF).astype(F32)
    return top, value - top


def lane_pack(columns):
    rows = columns[0].shape[0]
    lane = lax.broadcasted_iota(jnp.int32, (rows, 128), 1)
    block = jnp.zeros((rows, 128), F32)
    for number, column in enumerate(columns):
        block = jnp.where(lane == number, column, block)
    return block


def sums_pack(mean, inv, one, two):
    pairs = [two_terms(c) for c in (mean, inv, one, two)]
    return lane_pack([p[0] for p in pairs] + [p[1] for p in pairs]).astype(BF)


def stats_row(columns, rows):
    row = lax.broadcasted_iota(jnp.int32, (rows, 128), 0)
    lane = lax.broadcasted_iota(jnp.int32, (rows, 128), 1)
    block = jnp.zeros((rows, 128), F32)
    for number, column in enumerate(columns):
        block = jnp.where(lane == number * rows + row, column, block)
    return jnp.sum(block, axis=0, keepdims=True)


def norm_stats(beside, width, at):
    rows = beside.shape[1]
    row = lax.broadcasted_iota(jnp.int32, (rows, 128), 0)
    lane = lax.broadcasted_iota(jnp.int32, (rows, 128), 1)
    group = lane // rows

    def column(d, low, high):
        mask = (lane % rows == row) & (group >= low) & (group < high)
        line = jnp.broadcast_to(beside[d, at : at + 1, :], (rows, 128))
        return jnp.sum(jnp.where(mask, line, 0.0), axis=1, keepdims=True)

    shifts = [column(d, 0, 1) for d in range(8)]
    means = [column(d, 0, 2) for d in range(8)]
    mean = sum(means) / 8
    square = sum(column(d, 2, 4) + width * (means[d] - mean) ** 2 for d in range(8))
    inv = lax.rsqrt(square / D + EPSILON)
    return mean, inv, [shift - mean for shift in shifts]


def norm_sum(blocks_ref, beside, moves, inv, g):
    rows = beside.shape[1]
    lanes = slice(g * 128, (g + 1) * 128)
    pre = jnp.zeros((rows, 128), F32)
    columns = jnp.zeros((1, 128), F32)
    for d in range(8):
        column = beside[d, g : g + 1, :]
        columns = columns + column
        pre = pre + blocks_ref[d, :, lanes].astype(F32) + moves[d] * column
    return pre * inv, columns


def send_all(block, ready, sems, meanwhile=None):
    copies = [pltpu.make_async_copy(block, ready.at[j], sems.at[j]) for j in range(8)]
    for copy in copies:
        copy.start()
    if meanwhile is not None:
        meanwhile()
    for copy in copies:
        copy.wait()


def spread_first(place, swapped, part_b, width):
    _, rows, wide = swapped.shape
    hidden = wide - 128

    def kernel(
        place_ref, swapped_ref, part_ref, kept_out, ready_ref, sum_ref,
        total_ref, columns_ref, held, sems, out_sems,
    ):
        @pl.when(place_ref[0] == 0)
        def _():
            beside = swapped_ref[:, :, hidden:].astype(F32)
            mean, inv, moves = norm_stats(beside, width, hidden // 128)
            for g in range(hidden // 128):
                lanes = slice(g * 128, (g + 1) * 128)
                pre, columns = norm_sum(swapped_ref, beside, moves, inv, g)
                total_ref[:, lanes] = pre
                columns_ref[:, lanes] = jnp.broadcast_to(columns, (8, 128))
                held[:, lanes] = gelu_parts(pre)[0].astype(BF)
            held[:, hidden:] = sums_pack(mean, inv, mean, mean)
            copies = [
                pltpu.make_async_copy(total_ref, kept_out.at[pl.ds(0, rows)], out_sems.at[0]),
                pltpu.make_async_copy(columns_ref, kept_out.at[pl.ds(rows, 8)], out_sems.at[1]),
            ]
            for copy in copies:
                copy.start()
            send_all(held, ready_ref, sems)
            for copy in copies:
                copy.wait()

        @pl.when(place_ref[0] == 1)
        def _():
            for g in range(hidden // 128):
                lanes = slice(g * 128, (g + 1) * 128)
                total = swapped_ref[0, :, lanes].astype(F32)
                for j in range(1, 8):
                    total = total + swapped_ref[j, :, lanes].astype(F32)
                sum_ref[:, lanes] = total.astype(BF)

    return kernel_call(
        kernel,
        [
            jax.ShapeDtypeStruct((240 * rows, hidden), F32),
            jax.ShapeDtypeStruct((8, rows, hidden + 128), BF),
            jax.ShapeDtypeStruct((rows, hidden), BF),
        ],
        [SMEM, VMEM, HBM],
        [HBM, HBM, VMEM],
        (30 * rows * hidden, 40 * rows * hidden),
        input_output_aliases={2: 1},
        scratch_shapes=[
            pltpu.VMEM((rows, hidden), F32),
            pltpu.VMEM((8, hidden), F32),
            pltpu.VMEM((rows, hidden + 128), BF),
            pltpu.SemaphoreType.DMA((8,)),
            pltpu.SemaphoreType.DMA((2,)),
        ],
    )(place, swapped, part_b)


def branch_first(place, blocks, w_out):
    _, rows, wide = blocks.shape
    hidden = w_out.shape[0]
    tokens = 8 * rows
    plan = stream_plan([w_out], False)
    _, width, chunks, pieces, _ = plan

    def kernel(place_ref, x_ref, w_ref, low, high, total_ref, held, sems):
        @pl.when(place_ref[0] == 0)
        def _():
            copies = stream_copies(plan, [w_ref], held, sems)
            for _, copy in copies:
                copy.start()
            left = x_ref[:, :, :hidden].reshape(tokens, hidden)
            for number, (at, end) in enumerate(chunks):
                copies[number][1].wait()
                made = dot(left, held[:, at:end]).astype(BF)
                low[:, at:end] = made[: tokens // 2]
                high[:, at:end] = made[tokens // 2 :]

        @pl.when(place_ref[0] == 1)
        def _():
            for g in range(hidden // 128):
                lanes = slice(g * 128, (g + 1) * 128)
                total = x_ref[0, :, lanes].astype(F32)
                for j in range(1, 8):
                    total = total + x_ref[j, :, lanes].astype(F32)
                total_ref[:, lanes] = total

    return kernel_call(
        kernel,
        [
            jax.ShapeDtypeStruct((tokens // 2, width), BF),
            jax.ShapeDtypeStruct((tokens // 2, width), BF),
            jax.ShapeDtypeStruct((rows, hidden), F32),
        ],
        [SMEM, VMEM, HBM],
        [VMEM] * 3,
        (2 * tokens * hidden * width, 2 * hidden * width),
        limit=9,
        scratch_shapes=[
            pltpu.VMEM((hidden, width), BF),
            pltpu.SemaphoreType.DMA((len(pieces),)),
        ],
    )(place, blocks, w_out)


def pre_part(place, section, pair, other, w_parts):
    quarter, width = pair.shape
    tokens = 2 * quarter
    rows = tokens // 8
    plan = stream_plan(w_parts, False)
    _, hidden, chunks, pieces, _ = plan

    def kernel(place_ref, pair_ref, other_ref, *refs):
        part_refs, (out, held, left, buf, sems, out_sems) = refs[: len(w_parts)], refs[len(w_parts) :]

        @pl.when(place_ref[0] == section)
        def _():
            turn = place_ref[1] * (width // 2) if section == 1 else 0
            copies = stream_copies(plan, part_refs, held, sems, turn)
            for _, copy in copies:
                copy.start()
            lines = []
            for e, ref in enumerate((pair_ref, other_ref)):
                spread = ref[...].astype(F32)
                mean = jnp.sum(spread, axis=1, keepdims=True) / width
                off = spread - mean
                square = jnp.sum(off * off, axis=1, keepdims=True)
                shift = mean.astype(BF).astype(F32)
                left[e * quarter : (e + 1) * quarter, :] = (spread - shift).astype(BF)
                columns = [*two_terms(mean), *two_terms(square)]
                for k in range(4):
                    part = slice(k * rows, (k + 1) * rows)
                    lines.append(stats_row([column[part] for column in columns], rows))
            left[tokens:, :] = jnp.ones((16, width), BF)
            tops, outs = [], []

            def leave(at, end):
                lanes = pl.ds(at, end - at)
                copy = pltpu.make_async_copy(
                    buf.at[:, :, lanes], out.at[:, :, lanes], out_sems.at[len(outs)]
                )
                copy.start()
                outs.append(copy)

            for number, (at, end) in enumerate(chunks):
                for begun, copy in copies:
                    if begun == number:
                        copy.wait()
                made = dot(left[...], held[:, at:end])
                buf[:, :, at:end] = made[:tokens].astype(BF).reshape(8, rows, end - at)
                leave(at, end)
                sums = made[tokens : tokens + 1]
                for g in range((end - at) // 128):
                    tops.append(sums[:, g * 128 : (g + 1) * 128])
            empty = jnp.zeros((rows - len(tops) - 1, 128), F32)
            for j in range(8):
                block = jnp.concatenate([*tops, lines[j], empty], axis=0)
                buf[j, :, hidden:] = block.astype(BF)
            leave(hidden, hidden + 128)
            for copy in outs:
                copy.wait()

    return kernel_call(
        kernel,
        jax.ShapeDtypeStruct((8, rows, hidden + 128), BF),
        [SMEM, VMEM, VMEM] + [HBM] * len(w_parts),
        HBM,
        (2 * tokens * hidden * width, 2 * hidden * width),
        limit=14,
        scratch_shapes=[
            pltpu.VMEM((width, hidden), BF),
            pltpu.VMEM((tokens + 16, width), BF),
            pltpu.VMEM((8, rows, hidden + 128), BF),
            pltpu.SemaphoreType.DMA((len(pieces),)),
            pltpu.SemaphoreType.DMA((len(chunks) + 1,)),
        ],
    )(place, pair, other, *w_parts)


def weave(turned):
    row = lax.broadcasted_iota(jnp.int32, (256, 256), 0)
    lane = lax.broadcasted_iota(jnp.int32, (256, 256), 1)
    if turned:
        row, lane = lane, row
    return jnp.where(lane == 2 * (row % 128) + row // 128, 1.0, 0.0).astype(BF)


def grad_pre_later(blocks, grad_mine, grad_theirs, width):
    _, rows, wide = blocks.shape
    hidden = wide - 128
    plane = hidden // 2

    def kernel(blocks_ref, mine_ref, theirs_ref, ready, acted_ref, grad_ref, held_ref, own, sems):
        order, back = weave(False), weave(True)
        for b in range(hidden // 256):
            pair = []
            for q in (0, 1):
                lanes = slice(q * plane + b * 128, q * plane + (b + 1) * 128)
                pair.append(mine_ref[:, lanes] + theirs_ref[:, lanes].astype(F32))
            top, rest = two_terms(jnp.concatenate(pair, axis=1))
            done = dot(top.astype(BF), order) + dot(rest.astype(BF), order)
            grad_ref[:, b * 256 : (b + 1) * 256] = done
        beside = blocks_ref[:, :, hidden:].astype(F32)
        mean, inv, moves = norm_stats(beside, width, hidden // 128)
        one = jnp.zeros((rows, 1), F32)
        two = jnp.zeros((rows, 1), F32)
        for g in range(hidden // 128):
            lanes = slice(g * 128, (g + 1) * 128)
            pre, columns = norm_sum(blocks_ref, beside, moves, inv, g)
            acted, slope = gelu_parts(pre)
            held_ref[:, lanes] = acted.astype(BF)
            grad = (grad_ref[:, lanes] * slope).astype(BF)
            own[:, lanes] = grad
            grad = grad.astype(F32)
            one = one + jnp.sum(grad * columns, axis=1, keepdims=True)
            two = two + jnp.sum(grad * pre, axis=1, keepdims=True)
        own[:, hidden:] = sums_pack(mean, inv, one, two)

        def reorder():
            for b in range(hidden // 256):
                done = dot(held_ref[:, b * 256 : (b + 1) * 256], back).astype(BF)
                acted_ref[:, b * 128 : (b + 1) * 128] = done[:, :128]
                acted_ref[:, plane + b * 128 : plane + (b + 1) * 128] = done[:, 128:]

        send_all(own, ready, sems, reorder)

    return kernel_call(
        kernel,
        [
            jax.ShapeDtypeStruct((8, rows, hidden + 128), BF),
            jax.ShapeDtypeStruct((rows, hidden), BF),
        ],
        [VMEM] * 3,
        [HBM, VMEM],
        (80 * rows * hidden, 40 * rows * hidden),
        scratch_shapes=[
            pltpu.VMEM((rows, hidden), F32),
            pltpu.VMEM((rows, hidden), BF),
            pltpu.VMEM((rows, hidden + 128), BF),
            pltpu.SemaphoreType.DMA((8,)),
        ],
    )(blocks, grad_mine, grad_theirs)


def grad_pre_first(place, blocks, kept, theirs):
    _, rows, hidden = blocks.shape

    def kernel(
        place_ref, blocks_ref, kept_ref, theirs_ref, ready,
        pre_ref, columns_ref, own, sems,
    ):
        @pl.when(place_ref[0] == 0)
        def _():
            fetched(
                (kept_ref.at[pl.ds(0, rows)], kept_ref.at[pl.ds(rows, 8)]),
                (pre_ref, columns_ref),
                sems,
            )
            one = jnp.zeros((rows, 1), F32)
            two = jnp.zeros((rows, 1), F32)
            for g in range(hidden // 128):
                lanes = slice(g * 128, (g + 1) * 128)
                total = blocks_ref[0, :, lanes].astype(F32)
                for j in range(1, 8):
                    total = total + blocks_ref[j, :, lanes].astype(F32)
                pre = pre_ref[:, lanes]
                grad = (total * gelu_parts(pre)[1]).astype(BF)
                own[:, lanes] = grad
                grad = grad.astype(F32)
                one = one + jnp.sum(grad * columns_ref[0:1, lanes], axis=1, keepdims=True)
                two = two + jnp.sum(grad * pre, axis=1, keepdims=True)
            own[:, hidden:] = sums_pack(one, one, one, two)

        @pl.when(place_ref[0] == 1)
        def _():
            fetched((theirs_ref,), (own.at[:, pl.ds(0, hidden)],), sems)
            own[:, hidden:] = jnp.zeros((rows, 128), BF)

        send_all(own, ready, sems)

    return kernel_call(
        kernel,
        jax.ShapeDtypeStruct((8, rows, hidden + 128), BF),
        [SMEM, VMEM] + [HBM] * 2,
        HBM,
        (60 * rows * hidden, 40 * rows * hidden),
        scratch_shapes=[
            pltpu.VMEM((rows, hidden), F32),
            pltpu.VMEM((8, hidden), F32),
            pltpu.VMEM((rows, hidden + 128), BF),
            pltpu.SemaphoreType.DMA((8,)),
        ],
    )(place, blocks, kept, theirs)


def back_part(place, section, grad_pre, w_parts):
    tokens, wide = grad_pre.shape
    hidden = wide - 128
    plan = stream_plan(w_parts, True)
    width, _, chunks, pieces, _ = plan

    def kernel(place_ref, x_ref, *refs):
        w_refs, (low, high, held, made, sems) = refs[: len(w_parts)], refs[len(w_parts) :]

        @pl.when(place_ref[0] == section)
        def _():
            copies = stream_copies(plan, w_refs, held, sems)
            for _, copy in copies:
                copy.start()
            left = x_ref[:, :hidden]
            for number, (at, end) in enumerate(chunks):
                for begun, copy in copies:
                    if begun == number:
                        copy.wait()
                made[:, at:end] = dot(left, held[at:end, :], ((1,), (1,)))
            done = made[...]
            if section == 1:
                done = jnp.where(place_ref[1] == 0, done, pltpu.roll(done, width // 2, 1))
            done = done.astype(BF)
            for number, out in enumerate((low, high)):
                part = slice(number * tokens // 2, (number + 1) * tokens // 2)
                out[:, :width] = done[part]
                out[:, width:] = x_ref[part, hidden:]

    return kernel_call(
        kernel,
        [jax.ShapeDtypeStruct((tokens // 2, width + 128), BF)] * 2,
        [SMEM, VMEM] + [HBM] * len(w_parts),
        [VMEM] * 2,
        (2 * tokens * hidden * width, 2 * hidden * width),
        limit=12,
        scratch_shapes=[
            pltpu.VMEM((width, hidden), BF),
            pltpu.VMEM((tokens, width), F32),
            pltpu.SemaphoreType.DMA((len(pieces),)),
        ],
    )(place, grad_pre, *w_parts)


def joined_sums(block):
    return block + pltpu.roll(block, 124, 1)


def core_sum(low, arrived):
    quarter, wide = low.shape
    width = wide - 128
    rows = quarter // 4

    def kernel(low_ref, arrived_ref, mine, stats, *ready):
        stats[...] = low_ref[:rows, width:]
        for k in range(4):
            part = slice(k * rows, (k + 1) * rows)
            total = low_ref[part, :width].astype(F32) + arrived_ref[part, :width].astype(F32)
            sums = joined_sums(low_ref[part, width:].astype(F32))
            sums = sums + joined_sums(arrived_ref[part, width:].astype(F32))
            if k == 0:
                mine[:, :width] = total
                mine[:, width:] = sums
            else:
                ready[k - 1][:, :width] = total.astype(BF)
                top, rest = two_terms(sums)
                lane = lax.broadcasted_iota(jnp.int32, (rows, 128), 1)
                ready[k - 1][:, width:] = jnp.where(lane < 4, top, pltpu.roll(rest, 4, 1)).astype(BF)

    return kernel_call(
        kernel,
        [jax.ShapeDtypeStruct((rows, wide), F32), jax.ShapeDtypeStruct((rows, 128), BF)]
        + [jax.ShapeDtypeStruct((rows, wide), BF)] * 3,
        [VMEM] * 2,
        [VMEM] * 5,
        (2 * quarter * wide, 8 * quarter * wide),
    )(low, arrived)


def norm_back(mine, arrived, grad_out, stream, stats, tail=None):
    rows, wide = mine.shape
    width = wide - 128
    extra = () if tail is None else tail

    def kernel(mine_ref, one, two, three, grad_ref, stream_ref, stats_ref, *refs):
        out = refs[-1]

        def fill():
            total = mine_ref[:, :width]
            sums = mine_ref[:, width:]
            for ref in (one, two, three):
                total = total + ref[:, :width].astype(F32)
                sums = sums + joined_sums(ref[:, width:].astype(F32))
            stats = joined_sums(stats_ref[...].astype(F32))
            mean, inv = stats[:, 0:1], stats[:, 1:2]
            centred = (stream_ref[...].astype(F32) - mean) * inv
            grad = total - sums[:, 2:3] / D - centred * (sums[:, 3:4] / D)
            out[...] = (grad_ref[...].astype(F32) + inv * grad).astype(BF)

        if tail is None:
            fill()
            return
        place_ref, order_ref, whole_ref = refs[:3]
        pl.when(place_ref[0] == 0)(fill)

        @pl.when(place_ref[0] == 1)
        def _():
            chosen = dot(order_ref[...], whole_ref[...])
            turned = pltpu.roll(chosen, width // 2, 1)
            lane = lax.broadcasted_iota(jnp.int32, (rows, width), 1)
            own = place_ref[1] == 0
            left = jnp.where(own, chosen[:rows], turned[:rows])
            right = jnp.where(own, turned[rows:], chosen[rows:])
            out[...] = jnp.where(lane < width // 2, left, right).astype(BF)

    specs = [VMEM] * 7 + ([SMEM, VMEM, VMEM] if extra else [])
    return kernel_call(
        kernel,
        jax.ShapeDtypeStruct((rows, width), BF),
        specs,
        VMEM,
        (20 * rows * wide, 20 * rows * wide),
    )(mine, *arrived, grad_out, stream, stats, *extra)


def scatter_tensor(low, high):
    mine, stats, *ready = core_sum(low, send(high, other_core))
    return mine, stats, [send(block, along_z(-k)) for k, block in zip((1, 2, 3), ready)]


def split_planes(w, pick, sizes):
    height, width = w.shape
    part = height // 2
    block = pick.shape[0]
    sub = block // 2

    def kernel(w_ref, pick_ref, kept, *refs):
        away, (held, planes, sems, out_sem) = refs[: len(sizes)], refs[len(sizes) :]
        steps = height // block
        copies = [
            pltpu.make_async_copy(
                w_ref.at[pl.ds(at * block, block)], held.at[pl.ds(at * block, block)], sems.at[at]
            )
            for at in range(steps)
        ]
        for copy in copies:
            copy.start()
        outs, piece, begun = [], 0, 0
        for at, copy in enumerate(copies):
            copy.wait()
            rows = dot(pick_ref[...], held[at * block : (at + 1) * block, :]).astype(BF)
            planes[0, at * sub : (at + 1) * sub, :] = rows[:sub]
            planes[1, at * sub : (at + 1) * sub, :] = rows[sub:]
            if (at + 1) * sub == begun + sizes[piece]:
                lines = pl.ds(begun, sizes[piece])
                for plane, ref in enumerate((kept.at[lines], away[piece])):
                    out = pltpu.make_async_copy(
                        planes.at[plane, lines], ref, out_sem.at[2 * piece + plane]
                    )
                    out.start()
                    outs.append(out)
                begun += sizes[piece]
                piece += 1
        for out in outs:
            out.wait()

    shapes = [jax.ShapeDtypeStruct((size, width), BF) for size in (part, *sizes)]
    return kernel_call(
        kernel,
        shapes,
        [HBM, VMEM],
        [HBM] * (1 + len(sizes)),
        (2 * height * width * block, 4 * height * width),
        limit=13,
        scratch_shapes=[
            pltpu.VMEM((height, width), BF),
            pltpu.VMEM((2, part, width), BF),
            pltpu.SemaphoreType.DMA((height // block,)),
            pltpu.SemaphoreType.DMA((2 * len(sizes),)),
        ],
    )(w, pick)


def cot_spread(place, pair, other, w_out, beside):
    quarter, width = pair.shape
    tokens = 2 * quarter
    hidden = w_out.shape[0]
    plane, part, rows = hidden // 2, width // 2, tokens // 8

    def kernel(
        place_ref, pair_ref, other_ref, w_ref, rest, own, padded, slot_ref,
        held, buf, made_ref, sems, out_sems,
    ):
        half, z_at, core_at = place_ref[1], place_ref[2], place_ref[3]
        copies = []
        for i in range(2):
            row = pl.multiple_of((half ^ (1 - i)) * plane, 16)
            copy = pltpu.make_async_copy(w_ref.at[pl.ds(row, plane)], held.at[i], sems.at[i])
            copy.start()
            copies.append(copy)

        def chosen(count, near):
            to = lax.broadcasted_iota(jnp.int32, (count, quarter), 0)
            by = lax.broadcasted_iota(jnp.int32, (count, quarter), 1)
            to_z = (z_at + 4 - to // rows % 4) & 3
            to_token = (to_z * 2 + (core_at ^ (to // quarter))) * rows + to % rows
            by_z = (z_at + 4 - by // rows) & 3
            in_half = (by_z // 2) == (half if near else 1 - half)
            planes = []
            for q in (0, 1):
                total = jnp.zeros((count, width), F32)
                for e, ref in enumerate((pair_ref, other_ref)):
                    block = by_z % 2 * 2 + (core_at ^ e)
                    token = block * 2 * rows + 2 * (by % rows) + q
                    pick = jnp.where((token == to_token) & in_half, 1.0, 0.0).astype(BF)
                    total = total + dot(pick, ref[...])
                planes.append(total)
            lane = lax.broadcasted_iota(jnp.int32, (count, width), 1)
            return jnp.where(lane < part, planes[0] + pltpu.roll(planes[1], part, 1), 0.0)

        mine = chosen(tokens, True)
        made_ref[0] = mine.astype(BF)
        made_ref[1] = pltpu.roll(mine, part, 1).astype(BF)
        left, right = mine[:rows], chosen(rows, False)
        left, right = jnp.where(half == 0, left, right), jnp.where(half == 0, right, left)
        slot_ref[...] = (left + pltpu.roll(right, part, 1)).astype(BF)
        outs = [pltpu.make_async_copy(made_ref, padded, out_sems.at[2])]
        outs[0].start()
        for i, ref in enumerate((rest, own)):
            copies[i].wait()
            for q in (0, 1):
                made = dot(made_ref[q], held[i], ((1,), (1,))).astype(BF)
                buf[i, :, :, q * plane : (q + 1) * plane] = made.reshape(8, rows, plane)
            copy = pltpu.make_async_copy(buf.at[i], ref.at[:, :, pl.ds(0, hidden)], out_sems.at[i])
            copy.start()
            outs.append(copy)
        for copy in outs:
            copy.wait()

    return kernel_call(
        kernel,
        [jax.ShapeDtypeStruct((8, rows, hidden + extra), BF) for extra in beside]
        + [
            jax.ShapeDtypeStruct((2, tokens, width), BF),
            jax.ShapeDtypeStruct((rows, width), BF),
        ],
        [SMEM, VMEM, VMEM, HBM],
        [HBM, HBM, HBM, VMEM],
        (4 * tokens * hidden * width, 2 * hidden * width),
        limit=18,
        scratch_shapes=[
            pltpu.VMEM((2, plane, width), BF),
            pltpu.VMEM((2, 8, rows, hidden), BF),
            pltpu.VMEM((2, tokens, width), BF),
            pltpu.SemaphoreType.DMA((2,)),
            pltpu.SemaphoreType.DMA((3,)),
        ],
    )(place, pair, other, w_out)


def fill_rows(out, buf, sems, tiles):
    copies = []
    for number, (row, count, make) in enumerate(tiles):
        slot = number % 2
        if number >= 2:
            copies[number - 2].wait()
        lines = pl.ds(0, count)
        buf[slot, 0:count, :] = make().astype(BF)
        copy = pltpu.make_async_copy(buf.at[slot, lines], out.at[pl.ds(row, count)], sems.at[slot])
        copy.start()
        copies.append(copy)
    for copy in copies[-2:]:
        copy.wait()


def two_tiles(width):
    cut = (width // 128 + 1) // 2 * 128 if width >= 512 else width // 2
    return [(0, cut), (cut, width)]


def fetched(refs, bufs, sems):
    copies = [
        pltpu.make_async_copy(ref, buf, sems.at[number])
        for number, (ref, buf) in enumerate(zip(refs, bufs))
    ]
    for copy in copies:
        copy.start()
    for copy in copies:
        copy.wait()


def normed_rows(ref, beside, half):
    stats = joined_sums(beside.astype(F32))
    normed = (ref[...].astype(F32) - stats[:, 0:1]) * stats[:, 1:2]
    if half is not None:
        normed = jnp.where(half == 0, normed, pltpu.roll(normed, normed.shape[1] // 2, 1))
    return normed.astype(BF)


def products_early(place, acted, grad_all, pair, other, grad_pre, theirs):
    tokens, wide = acted.shape
    hidden = wide - 128
    width = grad_all.shape[1]
    part = width // 2
    quarter = tokens // 2

    def kernel(
        place_ref, acted_ref, grad_ref, pair_ref, other_ref, pre_ref, theirs_ref,
        out_ref, in_ref, hold_one, hold_two, hold_three, hold_pair, lefts,
        out_buf, in_buf, sems, out_sems, in_sems,
    ):
        @pl.when(place_ref[0] == 0)
        def _():
            fetched((acted_ref, grad_ref), (hold_one, hold_three), sems)
            def make(at, end):
                return lambda: dot(hold_one[:, at:end], hold_three[...], ((0,), (0,)))

            cuts = two_tiles(hidden)
            fill_rows(
                out_ref, out_buf, out_sems, [(at, end - at, make(at, end)) for at, end in cuts]
            )

        @pl.when(place_ref[0] == 1)
        def _():
            fetched(
                (pair_ref, other_ref, pre_ref, theirs_ref),
                (hold_pair.at[0], hold_pair.at[1], hold_one, hold_two),
                sems,
            )
            half = place_ref[1]
            row = lax.broadcasted_iota(jnp.int32, (128, 256), 0)
            lane = lax.broadcasted_iota(jnp.int32, (128, 256), 1)
            picks = [
                jnp.where(lane == 2 * row + plane, 1.0, 0.0).astype(BF)
                for plane in (half, 1 - half)
            ]
            for e in range(2):
                rows = slice(e * quarter, (e + 1) * quarter)
                normed = normed_rows(hold_pair.at[e], hold_one[rows, hidden:], half)
                for b in range(-(-part // 128)):
                    end = min(256 * (b + 1), width)
                    for number, pick in enumerate(picks):
                        made = dot(normed[:, 128 * b : 128 * (b + 1)], pick).astype(BF)
                        made = made[:, : end - 256 * b]
                        if number == 0:
                            lefts[0, rows, 256 * b : end] = made
                        else:
                            mid, at = quarter // 2, e * quarter
                            lefts[1, at + mid : at + quarter, 256 * b : end] = made[:mid]
                            lefts[1, at : at + mid, 256 * b : end] = made[mid:]
            def make(at, end):
                def both():
                    mine = dot(lefts[0, :, at:end], hold_one[:, :hidden], ((0,), (0,)))
                    return mine + dot(lefts[1, :, at:end], hold_two[:, :hidden], ((0,), (0,)))

                return both

            cuts = two_tiles(width)
            fill_rows(in_ref, in_buf, in_sems, [(at, end - at, make(at, end)) for at, end in cuts])

    return kernel_call(
        kernel,
        [
            jax.ShapeDtypeStruct((hidden, width), BF),
            jax.ShapeDtypeStruct((width, hidden), BF),
        ],
        [SMEM] + [HBM] * 6,
        [HBM] * 2,
        (2 * tokens * hidden * width, 2 * hidden * width),
        limit=36,
        scratch_shapes=[
            pltpu.VMEM((tokens, wide), BF),
            pltpu.VMEM((tokens, wide), BF),
            pltpu.VMEM((tokens, width), BF),
            pltpu.VMEM((2, quarter, width), BF),
            pltpu.VMEM((2, tokens, width), BF),
            pltpu.VMEM((2, two_tiles(hidden)[0][1], width), BF),
            pltpu.VMEM((2, two_tiles(width)[0][1], hidden), BF),
            pltpu.SemaphoreType.DMA((4,)),
            pltpu.SemaphoreType.DMA((2,)),
            pltpu.SemaphoreType.DMA((2,)),
        ],
    )(place, acted, grad_all, pair, other, grad_pre, theirs)


def products_late(place, out_grad, in_grad, pair, other, acted, blocks, mine, padded):
    quarter, width = pair.shape
    tokens = 2 * quarter
    hidden = mine.shape[1]
    plane = hidden // 2

    def kernel(
        place_ref, out_was, in_was, pair_ref, other_ref, acted_ref, blocks_ref, mine_ref,
        padded_ref, out_ref, in_ref, hold_pair, hold_beside, hold_one, hold_two, left,
        hold_padded, out_buf, in_buf, sems, out_sems, in_sems,
    ):
        @pl.when(place_ref[0] == 0)
        def _():
            fetched(
                (pair_ref, other_ref, acted_ref.at[:, pl.ds(hidden, 128)], blocks_ref),
                (hold_pair.at[0], hold_pair.at[1], hold_beside, hold_one),
                sems,
            )
            for e in range(2):
                rows = slice(e * quarter, (e + 1) * quarter)
                left[rows, :] = normed_rows(hold_pair.at[e], hold_beside[rows], None)
            def make(at, end):
                return lambda: dot(left[:, at:end], hold_one[:, :hidden], ((0,), (0,)))

            cuts = two_tiles(width)
            fill_rows(in_ref, in_buf, in_sems, [(at, end - at, make(at, end)) for at, end in cuts])

        @pl.when(place_ref[0] == 1)
        def _():
            fetched((mine_ref, blocks_ref, padded_ref), (hold_two, hold_one, hold_padded), sems)
            def make(ref):
                def both():
                    low = dot(ref[:, :plane], hold_padded[0], ((0,), (0,)))
                    return low + dot(ref[:, plane:hidden], hold_padded[1], ((0,), (0,)))

                return both

            tiles = []
            for number, ref in enumerate((hold_two, hold_one)):
                row = pl.multiple_of((place_ref[1] ^ number) * plane, 16)
                tiles.append((row, plane, make(ref)))
            fill_rows(out_ref, out_buf, out_sems, tiles)

    return kernel_call(
        kernel,
        [
            jax.ShapeDtypeStruct((hidden, width), BF),
            jax.ShapeDtypeStruct((width, hidden), BF),
        ],
        [SMEM] + [HBM] * 8,
        [HBM] * 2,
        (2 * tokens * hidden * width, 2 * hidden * width),
        limit=36,
        input_output_aliases={1: 0, 2: 1},
        scratch_shapes=[
            pltpu.VMEM((2, quarter, width), BF),
            pltpu.VMEM((tokens, 128), BF),
            pltpu.VMEM((tokens, hidden + 128), BF),
            pltpu.VMEM((tokens, hidden), BF),
            pltpu.VMEM((tokens, width), BF),
            pltpu.VMEM((2, tokens, width), BF),
            pltpu.VMEM((2, plane, width), BF),
            pltpu.VMEM((2, two_tiles(width)[0][1], hidden), BF),
            pltpu.SemaphoreType.DMA((4,)),
            pltpu.SemaphoreType.DMA((2,)),
            pltpu.SemaphoreType.DMA((2,)),
        ],
    )(place, out_grad, in_grad, pair, other, acted, blocks, mine, padded)


def stack_rows(blocks):
    rows, width = blocks[0].shape

    def kernel(*refs):
        for number, ref in enumerate(refs[:-1]):
            refs[-1][number * rows : (number + 1) * rows, :] = ref[...]

    count = len(blocks)
    return kernel_call(
        kernel,
        jax.ShapeDtypeStruct((count * rows, width), BF),
        [VMEM] * count,
        VMEM,
        (0, 4 * count * rows * width),
    )(*blocks)


def gather_pairs(x, *others):
    pair = stack_rows([after(x, *others)] + [send(x, along_z(k)) for k in (1, 2, 3)])
    return pair, send(pair, other_core)


def gather_tensor(x):
    return stack_rows(gather_pairs(x))


def swap_dp(blocks):
    return lax.all_to_all(blocks, "dp", 0, 0, tiled=True)


def one_hot(condition):
    return condition.astype(BF)


def after(value, *others):
    return lax.optimization_barrier((value, *others))[0]


def body(inputs, cotangent, w_first, w_second):
    w_in, w_out = w_first[0], w_second[0]
    rows, width = inputs.shape
    hidden = w_in.shape[1]
    part = width // 2
    tokens = 8 * rows
    first = lax.axis_index("section") == 0
    at = lax.axis_index("tensor")
    z_at, core_at = at // 2, at % 2
    half = at // 4

    slot_row = jnp.arange(tokens)
    slot_owner = ((z_at - slot_row // rows % 4) % 4) * 2 + (core_at ^ (slot_row // (4 * rows)))
    slot_token = slot_owner * rows + slot_row % rows

    place = jnp.stack([lax.axis_index("section"), half, z_at, core_at]).astype(jnp.int32)
    place_rows = jnp.arange(2 * rows)
    stored_token = (at % 4) * 2 * rows + 2 * (place_rows % rows) + place_rows // rows
    stored_order = one_hot(stored_token[:, None] == slot_token[None, :])

    unit = part // 12
    block = 2 * unit
    index = jnp.arange(block)
    picked = 2 * (index % (block // 2)) + jnp.where(index < block // 2, half, 1 - half)
    pick = one_hot(index[None, :] == picked[:, None])
    sizes = [2 * unit, 3 * unit, 3 * unit, 4 * unit]
    kept, *away = lax.cond(
        first,
        lambda: [blank(size, hidden) for size in (part, *sizes)],
        lambda: list(split_planes(w_in, pick, sizes)),
    )

    lead_pair, lead_other = gather_pairs(jnp.where(first, inputs, cotangent), *away)
    came = [send(after(away[0], lead_other), other_half, LATER)]

    def lead_second():
        return list(cot_spread(place, lead_pair, lead_other, w_out, (128, 128)))

    def lead_first():
        made = pre_part(place, 0, lead_pair, lead_other, [w_in])
        return [made, blank(8, rows, hidden + 128), blank(2, tokens, width), blank(rows, width)]

    part_a, part_b, cot_padded, cot_own = lax.cond(first, lead_first, lead_second)
    swapped = swap_dp(after(part_a, came[0]))
    came.append(send(away[1], other_half, LATER))
    swapped = after(swapped, came[1])
    kept_first, ready, sum_theirs = spread_first(place, swapped, part_b, width)
    grad_theirs = send(sum_theirs, other_half_row, LATER)
    acted_first = swap_dp(ready)
    came.append(send(away[2], other_half, LATER))
    acted_first = after(acted_first, came[2], grad_theirs)
    low, high, grad_mine = branch_first(place, acted_first, w_out)
    came.append(send(away[3], other_half, LATER))
    acted_first = acted_first.reshape(tokens, hidden + 128)
    w_parts = [kept, *came]
    branch = low.astype(F32) + send(high, other_core).astype(F32)
    stream = inputs.astype(F32) + branch[:rows]
    for k in (1, 2, 3):
        block = branch[k * rows : (k + 1) * rows].astype(BF)
        stream = stream + send(block, along_z(-k, FIRST)).astype(F32)
    stream = stream.astype(BF)
    pair = stack_rows([stream] + [send(stream, along_z(k, FIRST)) for k in (1, 2, 3)])

    pair = send(pair, other_section)
    other = send(pair, other_core)
    stream_own = pair[:rows]
    other = after(other, came[3])
    blocks = swap_dp(pre_part(place, 1, pair, other, w_parts))
    ready, acted_mine = grad_pre_later(blocks, grad_mine, grad_theirs, width)
    grad_pre = swap_dp(ready).reshape(tokens, hidden + 128)
    mine, stats, arrived = scatter_tensor(*back_part(place, 1, grad_pre, w_parts))
    later_grad = norm_back(mine, arrived, cot_own, stream_own, stats)

    returned = send(later_grad, other_section)
    own_grad = jnp.where(first, returned, later_grad)
    grad_all = gather_tensor(own_grad)
    acted_theirs = send(after(acted_mine, grad_all), other_half_row, LATER)
    grad_pre_theirs = send(after(grad_pre, grad_all), other_half, LATER)
    ready = grad_spread(place, grad_all, w_out, acted_mine)
    blocks = swap_dp(ready)
    acted_mine_all = blocks.reshape(tokens, hidden)
    ready = grad_pre_first(place, blocks, kept_first, acted_theirs)
    blocks = swap_dp(after(ready, grad_pre_theirs)).reshape(tokens, hidden + 128)
    out_grad, in_grad = products_early(
        place, acted_first, grad_all, pair, other, grad_pre, grad_pre_theirs
    )
    blocks = after(blocks, out_grad)
    mine, _, arrived = scatter_tensor(*back_part(place, 0, blocks, [w_in]))
    out_grad, in_grad = products_late(
        place, out_grad, in_grad, lead_pair, lead_other, acted_first, blocks, acted_mine_all,
        cot_padded,
    )
    result = norm_back(
        mine, arrived, own_grad, inputs, acted_first[:rows, hidden:],
        (place, stored_order, grad_all),
    )
    return (result[None], in_grad[None], out_grad[None])


def solution(mesh):
    return jax.shard_map(
        body,
        mesh=mesh,
        in_specs=(
            P("tensor", "dp"),
            P("tensor", "dp"),
            P("section", "dp", "tensor"),
            P("section", "tensor", "dp"),
        ),
        out_specs=(
            P("section", "tensor", "dp"),
            P("section", "dp", "tensor"),
            P("section", "tensor", "dp"),
        ),
        check_vma=False,
    )
```
